32 devices in a mesh: seq: 4 (over x, core), ray: 8 (over z, y).
Axes of the slice: x: 2, y: 2, z: 4, core: 2. Of those that a mesh axis runs over, the one named last changes fastest.
Arguments:
- rays: bfloat16 [12288, 768], P(('seq', 'ray')), may hold values from -6 to 6
- latents: bfloat16 [12288, 768], P(('seq', 'ray')), may hold values from -6 to 6
- lengths: int32 [4, 3], P('seq'), may hold values from 1 to 1536, 3072 in all within a row
- scenes: int32 [12288], P(('seq', 'ray')), may hold values from 0 to 2
- ln_gain: bfloat16 [768], replicated, may hold values from 0.25 to 1.75
- ln_bias: bfloat16 [768], replicated, may hold values from -3 to 3
- w_query: bfloat16 [768, 768], replicated, may hold values from -0.21875 to 0.21875
- b_query: bfloat16 [768], replicated, may hold values from -3 to 3
- w_key: bfloat16 [768, 768], replicated, may hold values from -0.21875 to 0.21875
- w_value: bfloat16 [768, 768], replicated, may hold values from -0.21875 to 0.21875
- b_value: bfloat16 [768], replicated, may hold values from -0.3125 to 0.3125
- w_out: bfloat16 [768, 768], replicated, may hold values from -2 to 2
- b_out: bfloat16 [768], replicated, may hold values from -3 to 3
- w_up: bfloat16 [768, 1536], replicated, may hold values from -0.21875 to 0.21875
- b_up: bfloat16 [1536], replicated, may hold values from -3 to 3
- w_down: bfloat16 [1536, 768], replicated, may hold values from -0.15625 to 0.15625
- b_down: bfloat16 [768], replicated, may hold values from -3 to 3
- cotangent: bfloat16 [12288, 768], P(('seq', 'ray')), may hold values from -6 to 6
Outputs:
- output: bfloat16 [12288, 768], P(('seq', 'ray'))
- grad_rays: float32 [12288, 768], P(('seq', 'ray'))
- grad_latents: float32 [12288, 768], P(('seq', 'ray'))
- grad_ln_gain: float32 [768], replicated
- grad_ln_bias: float32 [768], replicated
- grad_w_query: float32 [768, 768], replicated
- grad_b_query: float32 [768], replicated
- grad_w_key: float32 [768, 768], replicated
- grad_w_value: float32 [768, 768], replicated
- grad_b_value: float32 [768], replicated
- grad_w_out: float32 [768, 768], replicated
- grad_b_out: float32 [768], replicated
- grad_w_up: float32 [768, 1536], replicated
- grad_b_up: float32 [1536], replicated
- grad_w_down: float32 [1536, 768], replicated
- grad_b_down: float32 [768], replicated
The draws below stay inside these ranges and needn't reach their ends.
Inputs may be any that keep to these rules, and one draw needn't show every extreme that they name: Each row holds the latent lengths of the 3 scenes of one sequence, summing to 3072; the largest of a row is exactly 1536.
All inputs are finite; a program needn't handle non-finite values.
Results may differ from the reference program's by a relative error of at most 0.018.
The reference program's roundings to bfloat16 on the way count: a program that leaves them out, or rounds other values in their place, can miss the bound.
Values may be sent and summed in bfloat16 or wider, within the bound.
A program may use at most 192 MiB of HBM per device.

```python
import math
import jax
import jax.numpy as jnp
import numpy as np
from jax import lax

D = 768
HEADS = 12
HEAD = 64
FF = 1536
RAY_DEV = 384
LEN = 3072
SCENES = 3
SEQS = 4
LATENTS = 12288
RAYS = 12288
N_RAY = 8


def set_ends(result, key, smallest, largest):
    dims = result.shape
    index_at = [jax.random.randint(jax.random.fold_in(key, axis), (), 0, dims[axis]) for axis in range(len(dims))]
    result = result.at[tuple(index_at)].set(smallest)
    longest = dims.index(max(dims))
    index_at[longest] = (index_at[longest] + 1) % dims[longest]
    return result.at[tuple(index_at)].set(largest)


def shard_levels(stream_key, shape, cuts, smallest, high):
    def one(axis_at, blocks):
        steps = jax.random.uniform(jax.random.fold_in(jax.random.fold_in(stream_key, 6), axis_at), (blocks,), jnp.float32, smallest / len(cuts), high / len(cuts))
        return jnp.repeat(jnp.exp(steps), shape[axis_at] // blocks).reshape((-1,) + (1,) * (len(shape) - axis_at - 1))

    gain = one(*cuts[0])
    for cut in cuts[1:]:
        gain = gain * one(*cut)
    return gain


def length_profile(amount, total, most, lean):
    portions = [(1 << 20) // math.isqrt(rank ** lean) + 1 for rank in range(2, amount + 1)]
    spare, holding = total - most - (amount - 1), [1] * (amount - 1)
    while spare > 0:
        free = [i for i in range(amount - 1) if holding[i] < most]
        whole, left = sum([portions[i] for i in free]), spare
        for i in free:
            extra = min(most - holding[i], max(1, left * portions[i] // whole), spare)
            holding[i] = holding[i] + extra
            spare = spare - extra
    return np.array([most] + holding)


def ragged_sizes(rng, amount, total, most, skew):
    if amount == 2:
        one = jax.random.randint(rng, (), max(1, total - most), min(most, total - 1) + 1)
        return jnp.stack([one, total - one])
    sizes = jnp.asarray(length_profile(amount, total, most, skew), jnp.int32)
    couples = (amount - 1) // 2
    source_of, receiver = sizes[1:1 + 2 * couples:2], sizes[2:2 + 2 * couples:2]
    margin = jnp.minimum(source_of - 1, most - receiver)
    moved = jax.random.randint(jax.random.fold_in(rng, 1), (couples,), 0, 1 << 20) % (margin + 1)
    sizes = sizes.at[1:1 + 2 * couples:2].set(source_of - moved).at[2:2 + 2 * couples:2].set(receiver + moved)
    return sizes[jax.random.permutation(jax.random.fold_in(rng, 2), amount)]


def noise(key, shape, scale, most, shards=(), kind=jnp.bfloat16):
    values = scale * jax.random.normal(key, shape, jnp.float32)
    if shards:
        values = values * shard_levels(key, shape, shards, -0.22, 0.18)
    return jnp.clip(values, -most, most).astype(kind)


def setup_inputs(seed: int = 0) -> dict:
    key_list = jax.random.split(jax.random.key(seed), 19)
    return {
        "rays": noise(key_list[0], (RAYS, D), 1.0, 6.0, ((0, 32),)),
        "latents": noise(key_list[1], (LATENTS, D), 1.0, 6.0, ((0, 32),)),
        "lengths": jax.vmap(lambda own: ragged_sizes(own, SCENES, LEN, LEN // 2, 1))(jax.random.split(key_list[2], SEQS)).reshape((SEQS, SCENES)).astype(jnp.int32),
        "scenes": set_ends(jax.random.randint(key_list[3], (RAYS,), 0, SCENES), jax.random.fold_in(key_list[3], 1), 0, SCENES - 1).astype(jnp.int32),
        "ln_gain": jnp.clip(1.0 + 0.15 * jax.random.normal(key_list[4], (D,), jnp.float32), 0.25, 1.75).astype(jnp.bfloat16),
        "ln_bias": noise(key_list[5], (D,), 0.5, 3.0),
        "w_query": noise(key_list[6], (D, D), D ** -0.5, 0.21875),
        "b_query": noise(key_list[7], (D,), 0.5, 3.0),
        "w_key": noise(key_list[8], (D, D), D ** -0.5, 0.21875),
        "w_value": noise(key_list[9], (D, D), D ** -0.5, 0.21875),
        "b_value": noise(key_list[10], (D,), 0.05, 0.3125),
        "w_out": noise(key_list[11], (D, D), 8 ** -0.5, 2.0),
        "b_out": noise(key_list[12], (D,), 0.5, 3.0),
        "w_up": noise(key_list[13], (D, FF), D ** -0.5, 0.21875),
        "b_up": noise(key_list[14], (FF,), 0.5, 3.0),
        "w_down": noise(key_list[15], (FF, D), FF ** -0.5, 0.15625),
        "b_down": noise(key_list[16], (D,), 0.5, 3.0),
        "cotangent": noise(key_list[17], (RAYS, D), 1.0, 6.0, ((0, 32),)),
    }


@jax.custom_vjp
def low(v):
    return lax.optimization_barrier(v.astype(jnp.bfloat16)).astype(jnp.float32)

@jax.custom_vjp
def low_back(v):
    return v

def low_keep(v):
    return (low(v), None)

def low_pass(kept, grad):
    return (grad,)

def back_keep(v):
    return (v, None)

def back_low(kept, grad):
    return (low(grad),)
low.defvjp(low_keep, low_pass)
low_back.defvjp(back_keep, back_low)
masked_score = -1e+30
exact = lax.Precision.HIGHEST

def product(first_arg, second_arg):
    return jnp.dot(first_arg, second_arg, precision=exact)

def attend(queries, keys, values, allowed):
    ray_count = queries.shape[0]
    key_count = keys.shape[0]
    query_heads = queries.reshape(ray_count, HEADS, HEAD)
    key_heads = keys.reshape(key_count, HEADS, HEAD)
    value_heads = values.reshape(key_count, HEADS, HEAD)
    raw_score = jnp.einsum('rhd,lhd->hrl', query_heads, key_heads, precision=exact)
    scores = low_back(raw_score * HEAD ** (-0.5))
    scores = jnp.where(allowed[None], scores, masked_score)
    row_max = lax.optimization_barrier(jnp.max(scores, axis=2, keepdims=True))
    expo_rows = jnp.exp(scores - row_max)
    weights = low(expo_rows / lax.optimization_barrier(jnp.sum(expo_rows, axis=2, keepdims=True)))
    mixed = jnp.einsum('hrl,lhd->rhd', weights, value_heads, precision=exact)
    return mixed.reshape(ray_count, HEADS * HEAD)

def forward(rays, latents, ln_gain, ln_bias, w_query, b_query, w_key, w_value, b_value, w_out, b_out, w_up, b_up, w_down, b_down, scenes, segment):
    row_mean = lax.optimization_barrier(jnp.mean(rays, axis=1, keepdims=True))
    centred = rays - row_mean
    spread = lax.optimization_barrier(jnp.mean(centred * centred, axis=1, keepdims=True))
    normed = centred * lax.rsqrt(spread + 1e-05)
    shifted = low(normed * ln_gain + ln_bias)
    queries = low_back(low(product(shifted, w_query) + b_query))
    keys = low(jnp.einsum('gld,de->gle', latents, w_key, precision=exact))
    values = low(jnp.einsum('gld,de->gle', latents, w_value, precision=exact) + b_value)
    queries = queries.reshape(SEQS, N_RAY, RAY_DEV, D)
    scene_ids = scenes.reshape(SEQS, N_RAY, RAY_DEV)

    def one_group(items):
        group_query, group_key, group_value, group_scene, group_segment = items

        def one_shard(pair):
            shard_query, shard_scene = pair
            allowed = shard_scene[:, None] == group_segment[None, :]
            return jax.checkpoint(attend)(shard_query, low_back(group_key), low_back(group_value), allowed)
        return lax.map(one_shard, (group_query, group_scene))
    attended = lax.map(one_group, (queries, keys, values, scene_ids, segment))
    attended = low_back(low(attended.reshape(RAYS, D)))
    branch = low_back(product(attended, w_out) + b_out)
    hidden = rays + branch
    pre_act = low_back(product(low(hidden), w_up) + b_up)
    active = low(jax.nn.gelu(pre_act, approximate=False))
    return hidden + product(active, w_down) + b_down

def reference(rays, latents, lengths, scenes, ln_gain, ln_bias, w_query, b_query, w_key, w_value, b_value, w_out, b_out, w_up, b_up, w_down, b_down, cotangent):
    scene_ends = jnp.cumsum(lengths, axis=1).astype(jnp.int32)
    positions = jnp.arange(LEN, dtype=jnp.int32)
    segment = lax.optimization_barrier(jnp.sum((positions[None, :, None] >= scene_ends[:, None, :]).astype(jnp.int32), axis=2)).astype(jnp.int32)
    floats = [array_in.astype(jnp.float32) for array_in in (rays, latents.reshape(SEQS, LEN, D), ln_gain, ln_bias, w_query, b_query, w_key, w_value, b_value, w_out, b_out, w_up, b_up, w_down, b_down)]

    def wrapped(*inputs):
        return forward(*inputs, scenes, segment)
    output, pullback = jax.vjp(wrapped, *floats)
    grads = pullback(cotangent.astype(jnp.float32))
    return (output.astype(jnp.bfloat16), grads[0], grads[1].reshape(LATENTS, D), grads[2], grads[3], grads[4], grads[5], grads[6], grads[7], grads[8], grads[9], grads[10], grads[11], grads[12], grads[13], grads[14])
```

```python
import functools

import jax
import jax.numpy as jnp
from jax import lax
from jax.experimental import pallas as pl
from jax.experimental.pallas import tpu as pltpu
from jax.sharding import PartitionSpec as P

HEADS = 12
HEAD = 64
TILE = 64
WIDE = 256
PACK = WIDE // HEAD
CHUNK = 256

masked_score = -1e30
f32 = jnp.float32
bf16 = jnp.bfloat16


def matmul(first_arg, second_arg, first_dim, second_dim):
    return lax.dot_general(
        first_arg,
        second_arg,
        (((first_dim,), (second_dim,)), ((), ())),
        preferred_element_type=jnp.float32,
    )


def gelu_exact(pre_act):
    return jax.nn.gelu(pre_act, approximate=False)


def own_block():
    row = lax.broadcasted_iota(jnp.int32, (WIDE, WIDE), 0) // TILE
    column = lax.broadcasted_iota(jnp.int32, (WIDE, WIDE), 1) // HEAD
    return row == column


def spread_heads(tile):
    return jnp.where(own_block(), jnp.concatenate([tile] * PACK, axis=0), jnp.zeros((), tile.dtype))


def fold_heads(square):
    kept = jnp.where(own_block(), square, 0.0)
    return sum(kept[TILE * h : TILE * (h + 1), :] for h in range(PACK))


def fold_rows(block, combine):
    return combine(block.reshape(block.shape[0] // 8, 8, WIDE), axis=0)


def in_scene(chunk, start, end):
    rows = lax.broadcasted_iota(jnp.int32, (CHUNK, WIDE), 0) + chunk * CHUNK
    return (rows >= start) & (rows < end)


def chunk_at(chunk):
    return pl.ds(pl.multiple_of(chunk * CHUNK, CHUNK), CHUNK)


def attend_kernel(tiles, meta, q_ref, k_ref, vt_ref, att_ref, lse_ref, s_ref):
    att_ref[...] = jnp.zeros_like(att_ref)
    lse_ref[...] = jnp.zeros_like(lse_ref)

    def one_tile(t, carry):
        start, end = meta[1 + t], meta[1 + tiles + t]
        first, last = start // CHUNK, (end + CHUNK - 1) // CHUNK
        ray_rows = pl.ds(pl.multiple_of(t * TILE, TILE), TILE)
        spread = spread_heads(q_ref[ray_rows, :])

        def score(j, top):
            s = matmul(k_ref[chunk_at(j), :], spread, 1, 1)
            s = jnp.where(in_scene(j, start, end), s, masked_score)
            s_ref[chunk_at(j), :] = s
            return jnp.maximum(top, fold_rows(s, jnp.max))

        top = lax.fori_loop(first, last, score, jnp.full((8, WIDE), masked_score, f32))
        top = jnp.max(top, axis=0, keepdims=True)

        def expo(j, total):
            e = jnp.exp(s_ref[chunk_at(j), :] - top)
            s_ref[chunk_at(j), :] = e
            return total + fold_rows(e, jnp.sum)

        total = lax.fori_loop(first, last, expo, jnp.zeros((8, WIDE), f32))
        total = jnp.sum(total, axis=0, keepdims=True)
        rest = 1.0 / total

        def mix(j, mixed):
            w = (s_ref[chunk_at(j), :] * rest).astype(bf16)
            return mixed + matmul(vt_ref[:, chunk_at(j)], w, 1, 0)

        mixed = lax.fori_loop(first, last, mix, jnp.zeros((WIDE, WIDE), f32))
        att_ref[ray_rows, :] = fold_heads(mixed.T)
        lse_ref[0, pl.ds(t, 1), :] = top + jnp.log(total)
        return carry

    lax.fori_loop(0, meta[0], one_tile, 0)


def attend_back_kernel(tiles, meta, q_ref, k_ref, kt_ref, v_ref, g_ref, att_ref, lse_ref, gq_ref, gk_ref, gv_ref, gk_sum, gv_sum, gqt_sum):
    gq_ref[...] = jnp.zeros_like(gq_ref)
    gk_sum[...] = jnp.zeros_like(gk_sum)
    gv_sum[...] = jnp.zeros_like(gv_sum)

    def one_tile(t, carry):
        start, end = meta[1 + t], meta[1 + tiles + t]
        first, last = start // CHUNK, (end + CHUNK - 1) // CHUNK
        ray_rows = pl.ds(pl.multiple_of(t * TILE, TILE), TILE)
        q_spread = spread_heads(q_ref[ray_rows, :])
        g_tile = g_ref[ray_rows, :]
        g_spread = spread_heads(g_tile)
        product = spread_heads(g_tile.astype(f32) * att_ref[ray_rows, :])
        dots = lax.dot_general(
            jnp.ones((8, WIDE), f32),
            product,
            (((1,), (1,)), ((), ())),
            precision=lax.Precision.HIGHEST,
            preferred_element_type=f32,
        )[0:1, :]
        lse = lse_ref[0, pl.ds(t, 1), :]
        gqt_sum[...] = jnp.zeros_like(gqt_sum)

        def step(j, carry):
            at = chunk_at(j)
            s = matmul(k_ref[at, :], q_spread, 1, 1)
            p = jnp.where(in_scene(j, start, end), jnp.exp(s - lse), 0.0)
            gv_sum[at, :] += matmul(p.astype(bf16), g_spread, 1, 0)
            gp = matmul(v_ref[at, :], g_spread, 1, 1)
            gs = (p * (gp - dots)).astype(bf16)
            gk_sum[at, :] += matmul(gs, q_spread, 1, 0)
            gqt_sum[...] += matmul(kt_ref[:, at], gs, 1, 0)
            return carry

        lax.fori_loop(first, last, step, 0)
        gq_ref[ray_rows, :] = (fold_heads(gqt_sum[...].T) * HEAD ** (-0.5)).astype(bf16)
        return carry

    lax.fori_loop(0, meta[0], one_tile, 0)
    gk_ref[...] = gk_sum[...].astype(bf16)
    gv_ref[...] = gv_sum[...].astype(bf16)


def scene_plan(lengths, scenes, rays):
    tiles = rays // TILE + lengths.shape[0] - 1
    kinds = jnp.arange(lengths.shape[0], dtype=jnp.int32)
    one_hot = scenes[:, None] == kinds[None, :]
    before = jnp.tril(jnp.ones((rays, rays), bf16), -1)
    rank = matmul(before, one_hot.astype(bf16), 1, 0).astype(jnp.int32)
    counts = jnp.sum(one_hot.astype(jnp.int32), axis=0)
    scene_tiles = (counts + TILE - 1) // TILE
    tile_ends = jnp.cumsum(scene_tiles)
    first_slot = (tile_ends - scene_tiles) * TILE
    slot = jnp.sum(jnp.where(one_hot, rank + first_slot[None, :], 0), axis=1)
    order = (jnp.arange(tiles * TILE, dtype=jnp.int32)[:, None] == slot[None, :]).astype(bf16)
    ends = jnp.cumsum(lengths)
    tile_scene = jnp.sum(jnp.arange(tiles, dtype=jnp.int32)[:, None] >= tile_ends[None, :], axis=1)
    pick = tile_scene[:, None] == kinds[None, :]
    tile_start = jnp.sum(jnp.where(pick, (ends - lengths)[None, :], 0), axis=1)
    tile_end = jnp.sum(jnp.where(pick, ends[None, :], 0), axis=1)
    meta = jnp.concatenate([tile_ends[-1:], tile_start, tile_end]).astype(jnp.int32)
    return tiles, order, meta


def local(
    rays,
    latents,
    lengths,
    scenes,
    ln_gain,
    ln_bias,
    w_query,
    b_query,
    w_key,
    w_value,
    b_value,
    w_out,
    b_out,
    w_up,
    b_up,
    w_down,
    b_down,
    cotangent,
):
    scale = HEAD ** (-0.5)
    width = rays.shape[1]
    groups = width // WIDE
    gathered = lax.all_gather(latents, "ray", axis=0, tiled=True)
    key_total = gathered.shape[0]
    tiles, order, meta = scene_plan(lengths[0], scenes, rays.shape[0])
    slots = tiles * TILE
    inputs = rays.astype(f32)
    row_mean = jnp.mean(inputs, axis=1, keepdims=True)
    centred = inputs - row_mean
    inverse = lax.rsqrt(jnp.mean(centred * centred, axis=1, keepdims=True) + 1e-05)
    normed = centred * inverse
    gain_full = ln_gain.astype(f32)
    shifted = (normed * gain_full + ln_bias.astype(f32)).astype(bf16)
    queries = (matmul(shifted, w_query, 1, 0) + b_query.astype(f32)).astype(bf16)
    q_sorted = (matmul(order, queries, 1, 0) * scale).astype(bf16)
    keys = matmul(gathered, w_key, 1, 0).astype(bf16)
    keys_t = matmul(w_key, gathered, 0, 1).astype(bf16)
    values = (matmul(gathered, w_value, 1, 0) + b_value.astype(f32)).astype(bf16)
    values_t = (matmul(w_value, gathered, 0, 1) + b_value.astype(f32)[:, None]).astype(bf16)

    smem = pl.BlockSpec(memory_space=pltpu.SMEM)
    slot_spec = pl.BlockSpec((slots, WIDE), lambda g: (0, g))
    key_spec = pl.BlockSpec((key_total, WIDE), lambda g: (0, g))
    turned_spec = pl.BlockSpec((WIDE, key_total), lambda g: (g, 0))
    lse_spec = pl.BlockSpec((1, tiles, WIDE), lambda g: (g, 0, 0))
    params = pltpu.CompilerParams(vmem_limit_bytes=48 << 20)
    att_sorted, lse = pl.pallas_call(
        functools.partial(attend_kernel, tiles),
        grid=(groups,),
        out_shape=(
            jax.ShapeDtypeStruct((slots, width), f32),
            jax.ShapeDtypeStruct((groups, tiles, WIDE), f32),
        ),
        in_specs=[smem, slot_spec, key_spec, turned_spec],
        out_specs=(slot_spec, lse_spec),
        scratch_shapes=[pltpu.VMEM((key_total, WIDE), f32)],
        compiler_params=params,
        name="attend",
    )(meta, q_sorted, keys, values_t)
    attended = matmul(order, att_sorted.astype(bf16), 0, 0).astype(bf16)

    hidden = inputs + matmul(attended, w_out, 1, 0) + b_out.astype(f32)
    hidden_low = hidden.astype(bf16)
    pre_act = matmul(hidden_low, w_up, 1, 0) + b_up.astype(f32)
    active = gelu_exact(pre_act).astype(bf16)
    result = hidden + matmul(active, w_down, 1, 0) + b_down.astype(f32)
    grad_top = cotangent.astype(f32)
    grad_w_down = matmul(active, cotangent, 0, 0)
    grad_b_down = jnp.sum(grad_top, axis=0)
    grad_active = matmul(cotangent, w_down, 1, 1)
    unused_value, gelu_back = jax.vjp(gelu_exact, pre_act)
    grad_pre = gelu_back(grad_active)[0].astype(bf16)
    grad_w_up = matmul(hidden_low, grad_pre, 0, 0)
    grad_b_up = jnp.sum(grad_pre.astype(f32), axis=0)
    grad_hidden = grad_top + matmul(grad_pre, w_up, 1, 1)
    grad_branch = grad_hidden.astype(bf16)
    grad_w_out = matmul(attended, grad_branch, 0, 0)
    grad_b_out = jnp.sum(grad_branch.astype(f32), axis=0)
    grad_attended = matmul(grad_branch, w_out, 1, 1).astype(bf16)
    early = lax.psum(
        tuple(g.astype(bf16) for g in (grad_w_out, grad_w_up, grad_w_down)), ("seq", "ray")
    )
    g_sorted = matmul(order, grad_attended, 1, 0).astype(bf16)

    gq_sorted, grad_keys, grad_values = pl.pallas_call(
        functools.partial(attend_back_kernel, tiles),
        grid=(groups,),
        out_shape=(
            jax.ShapeDtypeStruct((slots, width), bf16),
            jax.ShapeDtypeStruct((key_total, width), bf16),
            jax.ShapeDtypeStruct((key_total, width), bf16),
        ),
        in_specs=[smem, slot_spec, key_spec, turned_spec, key_spec, slot_spec, slot_spec, lse_spec],
        out_specs=(slot_spec, key_spec, key_spec),
        scratch_shapes=[
            pltpu.VMEM((key_total, WIDE), f32),
            pltpu.VMEM((key_total, WIDE), f32),
            pltpu.VMEM((WIDE, WIDE), f32),
        ],
        compiler_params=params,
        name="attend_back",
    )(meta, q_sorted, keys, keys_t, values, g_sorted, att_sorted, lse)
    grad_queries = matmul(order, gq_sorted, 0, 0).astype(bf16)

    grad_w_query = matmul(shifted, grad_queries, 0, 0)
    grad_b_query = jnp.sum(grad_queries.astype(f32), axis=0)
    grad_shifted = matmul(grad_queries, w_query, 1, 1)
    grad_gain = jnp.sum(grad_shifted * normed, axis=0)
    grad_bias = jnp.sum(grad_shifted, axis=0)
    grad_normed = grad_shifted * gain_full
    grad_rays = grad_hidden + inverse * (
        grad_normed
        - jnp.mean(grad_normed, axis=1, keepdims=True)
        - normed * jnp.mean(grad_normed * normed, axis=1, keepdims=True)
    )
    grad_w_key = matmul(gathered, grad_keys, 0, 0)
    grad_w_value = matmul(gathered, grad_values, 0, 0)
    grad_b_value = jnp.sum(grad_values.astype(f32), axis=0)
    grad_latents = lax.psum_scatter(
        (matmul(grad_keys, w_key, 1, 1) + matmul(grad_values, w_value, 1, 1)).astype(bf16),
        "ray",
        scatter_dimension=0,
        tiled=True,
    ).astype(f32)
    late = lax.psum(
        tuple(g.astype(bf16) for g in (grad_w_query, grad_w_key, grad_w_value)), ("seq", "ray")
    )
    rows = lax.psum(
        (grad_gain, grad_bias, grad_b_query, grad_b_value, grad_b_out, grad_b_up, grad_b_down),
        ("seq", "ray"),
    )
    return (
        result.astype(bf16),
        grad_rays,
        grad_latents,
        rows[0],
        rows[1],
        late[0].astype(f32),
        rows[2],
        late[1].astype(f32),
        late[2].astype(f32),
        rows[3],
        early[0].astype(f32),
        rows[4],
        early[1].astype(f32),
        rows[5],
        early[2].astype(f32),
        rows[6],
    )


def solution(mesh):
    whole = P(("seq", "ray"), None)
    in_specs = (whole, whole, P("seq", None), P(("seq", "ray"))) + (P(),) * 13 + (whole,)
    out_specs = (whole,) * 3 + (P(),) * 13
    return jax.shard_map(local, mesh=mesh, in_specs=in_specs, out_specs=out_specs, check_vma=False)
```

```python
import functools

import jax
import jax.numpy as jnp
from jax import lax
from jax.experimental import pallas as pl
from jax.experimental.pallas import tpu as pltpu
from jax.sharding import PartitionSpec as P

HEADS = 12
HEAD = 64
TILE = 64
WIDE = 256
PACK = WIDE // HEAD
CHUNK = 256

masked_score = -1e30
f32 = jnp.float32
bf16 = jnp.bfloat16


def matmul(first_arg, second_arg, first_dim, second_dim):
    return lax.dot_general(
        first_arg,
        second_arg,
        (((first_dim,), (second_dim,)), ((), ())),
        preferred_element_type=jnp.float32,
    )


def gelu_exact(pre_act):
    return jax.nn.gelu(pre_act, approximate=False)


def own_block():
    row = lax.broadcasted_iota(jnp.int32, (WIDE, WIDE), 0) // TILE
    column = lax.broadcasted_iota(jnp.int32, (WIDE, WIDE), 1) // HEAD
    return row == column


def spread_heads(tile):
    return jnp.where(own_block(), jnp.concatenate([tile] * PACK, axis=0), jnp.zeros((), tile.dtype))


def fold_heads(square):
    kept = jnp.where(own_block(), square, 0.0)
    return sum(kept[TILE * h : TILE * (h + 1), :] for h in range(PACK))


def fold_rows(block, combine):
    return combine(block.reshape(block.shape[0] // 8, 8, WIDE), axis=0)


def in_scene(chunk, start, end):
    rows = lax.broadcasted_iota(jnp.int32, (CHUNK, WIDE), 0) + chunk * CHUNK
    return (rows >= start) & (rows < end)


def chunk_at(chunk):
    return pl.ds(pl.multiple_of(chunk * CHUNK, CHUNK), CHUNK)


def attend_kernel(tiles, meta, q_ref, k_ref, vt_ref, att_ref, lse_ref, s_ref):
    att_ref[...] = jnp.zeros_like(att_ref)
    lse_ref[...] = jnp.zeros_like(lse_ref)

    def one_tile(t, carry):
        start, end = meta[1 + t], meta[1 + tiles + t]
        first, last = start // CHUNK, (end + CHUNK - 1) // CHUNK
        ray_rows = pl.ds(pl.multiple_of(t * TILE, TILE), TILE)
        spread = spread_heads(q_ref[ray_rows, :])

        def score(j, top):
            s = matmul(k_ref[chunk_at(j), :], spread, 1, 1)
            s = jnp.where(in_scene(j, start, end), s, masked_score)
            s_ref[chunk_at(j), :] = s
            return jnp.maximum(top, fold_rows(s, jnp.max))

        top = lax.fori_loop(first, last, score, jnp.full((8, WIDE), masked_score, f32))
        top = jnp.max(top, axis=0, keepdims=True)

        def expo(j, total):
            e = jnp.exp(s_ref[chunk_at(j), :] - top)
            s_ref[chunk_at(j), :] = e
            return total + fold_rows(e, jnp.sum)

        total = lax.fori_loop(first, last, expo, jnp.zeros((8, WIDE), f32))
        total = jnp.sum(total, axis=0, keepdims=True)
        rest = 1.0 / total

        def mix(j, mixed):
            w = (s_ref[chunk_at(j), :] * rest).astype(bf16)
            return mixed + matmul(vt_ref[:, chunk_at(j)], w, 1, 0)

        mixed = lax.fori_loop(first, last, mix, jnp.zeros((WIDE, WIDE), f32))
        att_ref[ray_rows, :] = fold_heads(mixed.T)
        lse_ref[0, pl.ds(t, 1), :] = top + jnp.log(total)
        return carry

    lax.fori_loop(0, meta[0], one_tile, 0)


def attend_back_kernel(tiles, meta, q_ref, k_ref, kt_ref, v_ref, g_ref, att_ref, lse_ref, gq_ref, gk_ref, gv_ref, gk_sum, gv_sum, gqt_sum):
    gq_ref[...] = jnp.zeros_like(gq_ref)
    gk_sum[...] = jnp.zeros_like(gk_sum)
    gv_sum[...] = jnp.zeros_like(gv_sum)

    def one_tile(t, carry):
        start, end = meta[1 + t], meta[1 + tiles + t]
        first, last = start // CHUNK, (end + CHUNK - 1) // CHUNK
        ray_rows = pl.ds(pl.multiple_of(t * TILE, TILE), TILE)
        q_spread = spread_heads(q_ref[ray_rows, :])
        g_tile = g_ref[ray_rows, :]
        g_spread = spread_heads(g_tile)
        product = spread_heads(g_tile.astype(f32) * att_ref[ray_rows, :])
        dots = lax.dot_general(
            jnp.ones((8, WIDE), f32),
            product,
            (((1,), (1,)), ((), ())),
            precision=lax.Precision.HIGHEST,
            preferred_element_type=f32,
        )[0:1, :]
        lse = lse_ref[0, pl.ds(t, 1), :]
        gqt_sum[...] = jnp.zeros_like(gqt_sum)

        def step(j, carry):
            at = chunk_at(j)
            s = matmul(k_ref[at, :], q_spread, 1, 1)
            p = jnp.where(in_scene(j, start, end), jnp.exp(s - lse), 0.0)
            gv_sum[at, :] += matmul(p.astype(bf16), g_spread, 1, 0)
            gp = matmul(v_ref[at, :], g_spread, 1, 1)
            gs = (p * (gp - dots)).astype(bf16)
            gk_sum[at, :] += matmul(gs, q_spread, 1, 0)
            gqt_sum[...] += matmul(kt_ref[:, at], gs, 1, 0)
            return carry

        lax.fori_loop(first, last, step, 0)
        gq_ref[ray_rows, :] = (fold_heads(gqt_sum[...].T) * HEAD ** (-0.5)).astype(bf16)
        return carry

    lax.fori_loop(0, meta[0], one_tile, 0)
    gk_ref[...] = gk_sum[...].astype(bf16)
    gv_ref[...] = gv_sum[...].astype(bf16)


def scene_plan(lengths, scenes, rays):
    tiles = rays // TILE + lengths.shape[0] - 1
    kinds = jnp.arange(lengths.shape[0], dtype=jnp.int32)
    one_hot = scenes[:, None] == kinds[None, :]
    before = jnp.tril(jnp.ones((rays, rays), bf16), -1)
    rank = matmul(before, one_hot.astype(bf16), 1, 0).astype(jnp.int32)
    counts = jnp.sum(one_hot.astype(jnp.int32), axis=0)
    scene_tiles = (counts + TILE - 1) // TILE
    tile_ends = jnp.cumsum(scene_tiles)
    first_slot = (tile_ends - scene_tiles) * TILE
    slot = jnp.sum(jnp.where(one_hot, rank + first_slot[None, :], 0), axis=1)
    order = (jnp.arange(tiles * TILE, dtype=jnp.int32)[:, None] == slot[None, :]).astype(bf16)
    ends = jnp.cumsum(lengths)
    tile_scene = jnp.sum(jnp.arange(tiles, dtype=jnp.int32)[:, None] >= tile_ends[None, :], axis=1)
    pick = tile_scene[:, None] == kinds[None, :]
    tile_start = jnp.sum(jnp.where(pick, (ends - lengths)[None, :], 0), axis=1)
    tile_end = jnp.sum(jnp.where(pick, ends[None, :], 0), axis=1)
    meta = jnp.concatenate([tile_ends[-1:], tile_start, tile_end]).astype(jnp.int32)
    return tiles, order, meta


MESH = pl.DeviceIdType.MESH
SLOW = 4


def flip(index, bit):
    return index + bit * (1 - 2 * ((index // bit) % 2))


def bits_of(count):
    bits = []
    while count > 1:
        count //= 2
        bits.append(count)
    return bits


def lane_rows(start, size):
    return pl.ds(pl.multiple_of(start, 16), size)


class Place:
    def __init__(self, n_seq, n_ray):
        self.seq = lax.axis_index("seq")
        self.ray = lax.axis_index("ray")
        self.n_fast = n_ray // SLOW
        self.core = self.seq % 2
        self.slow = self.ray // self.n_fast
        self.fast = self.ray % self.n_fast
        self.x_bits = [("seq", 2 * b) for b in bits_of(n_seq // 2)]
        self.fast_bits = [("ray", b) for b in bits_of(self.n_fast)]
        self.slow_bits = [("ray", self.n_fast * b) for b in bits_of(SLOW)]
        self.spots = (self.slow, SLOW - 1 - self.slow)

    def across(self, axis, bit):
        if axis == "seq":
            return (flip(self.seq, bit), self.ray)
        return (self.seq, flip(self.ray, bit))

    def value(self, axis, bit):
        return ((self.seq if axis == "seq" else self.ray) // bit) % 2

    def along(self, way):
        return (self.seq, self.ray + (self.n_fast if way == 0 else -self.n_fast))

    def mirrored(self, way, chunk):
        return chunk if way == 0 else SLOW - 1 - chunk


def remote(src, dst, send_sem, recv_sem, device):
    return pltpu.make_async_remote_copy(
        src_ref=src,
        dst_ref=dst,
        send_sem=send_sem,
        recv_sem=recv_sem,
        device_id=device,
        device_id_type=MESH,
    )


def greet(place, exchanges):
    barrier = pltpu.get_barrier_semaphore()
    for axis, bit in exchanges:
        pl.semaphore_signal(barrier, inc=1, device_id=place.across(axis, bit), device_id_type=MESH)
    for step in (1, SLOW - 1):
        beside = (place.seq, (place.slow + step) % SLOW * place.n_fast + place.fast)
        pl.semaphore_signal(barrier, inc=1, device_id=beside, device_id_type=MESH)
    pl.semaphore_wait(barrier, len(exchanges) + 2)


class Line:
    def __init__(self, place, stage, recv, send_sem, recv_sem):
        self.place, self.stage, self.recv, self.send_sem, self.recv_sem = place, stage, recv, send_sem, recv_sem

    def copy(self, way, t):
        return remote(
            self.stage(way, t), self.recv(way, t), self.send_sem(way, t), self.recv_sem(way, t), self.place.along(way)
        )

    def landed(self, way, t):
        remote(
            self.stage(way, t), self.recv(way, t), self.send_sem(way, t), self.recv_sem(way, t), self.place.along(1 - way)
        ).wait_recv()
        return self.recv(way, t)[...].astype(f32)

    def step(self, t, own):
        for way in range(2):
            spot = self.place.spots[way]
            chunk = self.place.mirrored(way, SLOW - 1 - (t - spot))

            @pl.when((spot <= t) & (spot < SLOW - 1))
            def _(way=way, spot=spot, chunk=chunk):
                if t == 0:
                    self.stage(way, t)[...] = own(chunk).astype(bf16)
                else:

                    @pl.when(spot == 0)
                    def _():
                        self.stage(way, t)[...] = own(chunk).astype(bf16)

                    @pl.when(spot > 0)
                    def _():
                        self.stage(way, t)[...] = (own(chunk) + self.landed(way, t - 1)).astype(bf16)

                self.copy(way, t).start()

    def last(self, total):
        for way in range(2):

            @pl.when(self.place.spots[way] > 0)
            def _(way=way):
                total[...] += self.landed(way, SLOW - 2)

    def drain(self):
        for way in range(2):
            for t in range(SLOW - 1):
                spot = self.place.spots[way]

                @pl.when((spot <= t) & (spot < SLOW - 1))
                def _(way=way, t=t):
                    self.copy(way, t).wait_send()


class Spread:
    def __init__(self, place, block, send_sem, recv_sem):
        self.place, self.block, self.send_sem, self.recv_sem = place, block, send_sem, recv_sem

    def copy(self, way, t, to):
        chunk = self.place.mirrored(way, self.place.spots[way] - t)
        block = self.block(chunk)
        return remote(block, block, self.send_sem(way, t), self.recv_sem(way, t), self.place.along(to))

    def step(self, t):
        for way in range(2):
            spot = self.place.spots[way]

            @pl.when(spot >= t)
            def _(way=way, spot=spot):
                if t > 0:
                    block = self.block(self.place.mirrored(way, spot - t))
                    remote(
                        block, block, self.send_sem(way, t - 1), self.recv_sem(way, t - 1), self.place.along(1 - way)
                    ).wait_recv()
                if t < SLOW - 1:

                    @pl.when(spot < SLOW - 1)
                    def _():
                        self.copy(way, t, way).start()

    def drain(self):
        for way in range(2):
            for t in range(SLOW - 1):
                spot = self.place.spots[way]

                @pl.when((spot >= t) & (spot < SLOW - 1))
                def _(way=way, t=t):
                    self.copy(way, t, way).wait_send()


def units_of(rows, n_x, n_fast):
    share = n_x * n_fast * SLOW * 16
    return max(1, min(12, rows // share))


def sum_kernel(
    n_seq,
    n_ray,
    units,
    beat,
    g_ref,
    lat_ref,
    small_ref,
    out_ref,
    glat_ref,
    small_out,
    rc,
    held,
    rx,
    z_stage,
    z_recv,
    z_total,
    full,
    lat_recv,
    lat_own,
    lz_stage,
    lz_recv,
    small_now,
    small_recv,
    core_sem,
    halve_sem,
    z_sem,
    zg_sem,
    double_sem,
    core_back_sem,
    out_sem,
    lat_sem,
    lz_sem,
    small_sem,
):
    place = Place(n_seq, n_ray)
    core_pair = ("seq", 1)
    halvings = place.x_bits + place.fast_bits
    exchanges = [core_pair] + halvings + place.slow_bits
    greet(place, exchanges)

    rows = g_ref.shape[1]
    unit_rows = rows // units
    core = place.core
    sizes = [unit_rows >> i for i in range(len(halvings) + 1)]
    share = sizes[-1]
    line = share % (16 * SLOW) == 0
    piece = share // SLOW if line else share

    def base(u, stages):
        start = u * unit_rows
        for i in range(stages):
            start = start + place.value(*halvings[i]) * sizes[i + 1]
        return start

    def unit(u):
        return lane_rows(u * unit_rows, unit_rows)

    def core_copy(u):
        return remote(
            g_ref.at[1 - core, unit(u)], rc.at[unit(u)], core_sem.at[0, u], core_sem.at[1, u], place.across(*core_pair)
        )

    def halve_copy(i, u):
        size = sizes[i + 1]
        sent = base(u, i) + (1 - place.value(*halvings[i])) * size
        return remote(
            held.at[lane_rows(sent, size)],
            rx[i].at[lane_rows(u * size, size)],
            halve_sem.at[0, i, u],
            halve_sem.at[1, i, u],
            place.across(*halvings[i]),
        )

    def start_core(u):
        core_copy(u).start()

    def join_core(u):
        core_copy(u).wait()
        held[unit(u), :] = (g_ref[core, unit(u), :].astype(f32) + rc[unit(u), :].astype(f32)).astype(bf16)
        halve_copy(0, u).start()

    def join_half(i):
        def run(u):
            size = sizes[i + 1]
            halve_copy(i, u).wait()
            kept = lane_rows(base(u, i + 1), size)
            held[kept, :] = (held[kept, :].astype(f32) + rx[i][lane_rows(u * size, size), :].astype(f32)).astype(bf16)
            if i + 1 < len(halvings):
                halve_copy(i + 1, u).start()

        return run

    def z_line(u):
        return Line(
            place,
            lambda way, t: z_stage.at[u, way, t],
            lambda way, t: z_recv.at[u, way, t],
            lambda way, t: z_sem.at[0, u, way, t],
            lambda way, t: z_sem.at[1, u, way, t],
        )

    def z_rows(u, chunk):
        return lane_rows(base(u, len(halvings)) + chunk * piece, piece)

    def z_own(u):
        return lambda chunk: held[z_rows(u, chunk), :].astype(f32)

    def z_spread(u):
        return Spread(
            place,
            lambda chunk: full.at[core, z_rows(u, chunk)],
            lambda way, t: zg_sem.at[0, u, way, t],
            lambda way, t: zg_sem.at[1, u, way, t],
        )

    def z_step(t):
        return lambda u: z_line(u).step(t, z_own(u))

    def z_finish(u):
        z_total[...] = z_own(u)(place.slow)
        z_line(u).last(z_total)
        full[core, z_rows(u, place.slow), :] = z_total[...].astype(bf16)
        z_spread(u).step(0)

    def spread_step(t):
        return lambda u: z_spread(u).step(t)

    def whole_copy(i, u):
        return remote(
            held.at[lane_rows(base(u, len(halvings)), share)],
            z_recv.at[u, 0, i],
            z_sem.at[0, u, 0, i],
            z_sem.at[1, u, 0, i],
            place.across(*place.slow_bits[i]),
        )

    def whole_step(i):
        def run(u):
            mine = lane_rows(base(u, len(halvings)), share)
            if i > 0:
                whole_copy(i - 1, u).wait()
                held[mine, :] = (held[mine, :].astype(f32) + z_recv[u, 0, i - 1].astype(f32)).astype(bf16)
            if i < len(place.slow_bits):
                whole_copy(i, u).start()
            else:
                full[core, mine, :] = held[mine, :]

        return run

    def double_copy(i, u):
        block = full.at[core, lane_rows(base(u, i + 1), sizes[i + 1])]
        return remote(block, block, double_sem.at[0, i, u], double_sem.at[1, i, u], place.across(*halvings[i]))

    def core_back(u):
        block = full.at[core, unit(u)]
        return remote(block, block, core_back_sem.at[0, u], core_back_sem.at[1, u], place.across(*core_pair))

    def out_copy(half, u):
        return pltpu.make_async_copy(full.at[half, unit(u)], out_ref.at[half, unit(u)], out_sem.at[half, u])

    def start_double(u):
        double_copy(len(halvings) - 1, u).start()

    def join_double(i):
        def run(u):
            double_copy(i, u).wait()
            if i > 0:
                double_copy(i - 1, u).start()
            else:
                core_back(u).start()
                out_copy(core, u).start()

        return run

    def finish_unit(u):
        core_back(u).wait()
        out_copy(1 - core, u).start()
        if line:
            z_line(u).drain()
            z_spread(u).drain()

    stages = [[start_core], [join_core]] + [[join_half(i)] for i in range(len(halvings))]
    if line:
        stages[-1].append(z_step(0))
        stages += [[z_step(t)] for t in range(1, SLOW - 1)]
        stages += [[z_finish]] + [[spread_step(t)] for t in range(1, SLOW)]
    else:
        stages[-1].append(whole_step(0))
        stages += [[whole_step(i)] for i in range(1, len(place.slow_bits) + 1)]
    stages[-1].append(start_double)
    stages += [[join_double(i)] for i in reversed(range(len(halvings)))]
    stages += [[finish_unit]]

    half_rows = lat_ref.shape[1] // 2
    n_fast = place.n_fast
    fast_sizes = [n_fast >> i for i in range(len(place.fast_bits) + 1)]

    def chunk_of(k):
        near = jnp.minimum(place.slow, SLOW - 1 - place.slow)
        ahead = SLOW - 1 - near
        chunk = jnp.where(k < ahead, SLOW - 1 - k, jnp.where(k - ahead < near, k - ahead, near))
        return jnp.where(place.slow == near, chunk, SLOW - 1 - chunk)

    def lat_base(i):
        start = 0
        for n in range(i):
            start = start + place.value(*place.fast_bits[n]) * fast_sizes[n + 1]
        return start

    def lat_half(m):
        return lane_rows((m % 2) * half_rows, half_rows)

    def lat_copy(i, m):
        size = fast_sizes[i + 1]
        other = (1 - place.value(*place.fast_bits[i])) * size
        if i == 0:
            source = lat_ref.at[pl.ds(chunk_of(m // 2) * n_fast + other, size), lat_half(m)]
        else:
            source = lat_recv[i - 1].at[m, pl.ds(other, size)]
        return remote(
            source, lat_recv[i].at[m], lat_sem.at[0, i, m], lat_sem.at[1, i, m], place.across(*place.fast_bits[i])
        )

    def start_lat(m):
        lat_copy(0, m).start()

    def lat_line(m):
        half = m % 2
        return Line(
            place,
            lambda way, t: lz_stage.at[half, way, t],
            lambda way, t: lz_recv.at[half, way, t],
            lambda way, t: lz_sem.at[0, half, way, t],
            lambda way, t: lz_sem.at[1, half, way, t],
        )

    def join_lat(i):
        def run(m):
            size = fast_sizes[i + 1]
            lat_copy(i, m).wait()
            mine = place.value(*place.fast_bits[i]) * size
            if i == 0:
                kept = lat_ref[pl.ds(chunk_of(m // 2) * n_fast + mine, size), lat_half(m), :]
            else:
                kept = lat_recv[i - 1][m, pl.ds(mine, size)]
            joined = (kept.astype(f32) + lat_recv[i][m].astype(f32)).astype(bf16)
            if i + 1 < len(place.fast_bits):
                lat_recv[i][m] = joined
                lat_copy(i + 1, m).start()
            else:
                lat_own[chunk_of(m // 2), m % 2] = joined[0]
                walk_lat(m)

        return run

    def walk_lat(m):
        half = m % 2

        def own(chunk):
            return lat_own[chunk, half].astype(f32)

        for t in range(SLOW - 1):

            @pl.when(m // 2 == t)
            def _(t=t):
                lat_line(m).step(t, own)

    def finish_lat(m):
        @pl.when(m // 2 == SLOW - 1)
        def _():
            mine = glat_ref.at[lat_half(m)]
            mine[...] = lat_own[place.slow, m % 2].astype(f32)
            lat_line(m).last(mine)
            lat_line(m).drain()

    lat_stages = [start_lat] + [join_lat(i) for i in range(len(place.fast_bits))] + [finish_lat]
    lat_steps = 2 * SLOW

    def small_copy(i):
        axis, bit = exchanges[i]
        return remote(
            small_now.at[i], small_recv.at[i], small_sem.at[0, i], small_sem.at[1, i], place.across(axis, bit)
        )

    small_now[0] = small_ref[...]
    small_copy(0).start()

    lat_span = beat * (lat_steps - 1 + len(lat_stages) - 1) + 1
    beats = max(units + len(stages) - 1, lat_span, len(exchanges) + 1)

    def one_beat(now, carry):
        for s in reversed(range(len(stages))):
            u = now - s

            @pl.when((u >= 0) & (u < units))
            def _(u=u, s=s):
                for run in stages[s]:
                    run(u)

        for s in reversed(range(len(lat_stages))):
            ahead = now - beat * s
            m = ahead // beat

            @pl.when((ahead >= 0) & (ahead % beat == 0) & (m < lat_steps))
            def _(m=m, s=s):
                lat_stages[s](m)

        for i in range(len(exchanges)):

            @pl.when(now == i + 1)
            def _(i=i):
                small_copy(i).wait()
                small_now[i + 1] = small_now[i] + small_recv[i]
                if i + 1 < len(exchanges):
                    small_copy(i + 1).start()

        return carry

    lax.fori_loop(0, beats, one_beat, 0)
    small_out[...] = small_now[len(exchanges)]

    def end_out(u, carry):
        out_copy(0, u).wait()
        out_copy(1, u).wait()
        return carry

    lax.fori_loop(0, units, end_out, 0)


def sum_over_devices(n_seq, n_ray, grads, lat, small):
    place_fast = n_ray // SLOW
    rows, width = grads.shape[1:]
    n_x = n_seq // 2
    units = units_of(rows, n_x, place_fast)
    halvings = len(bits_of(n_x)) + len(bits_of(place_fast))
    fast_bits = len(bits_of(place_fast))
    exchanges = 1 + halvings + len(bits_of(SLOW))
    unit_rows = rows // units
    share = unit_rows >> halvings
    piece = share // SLOW if share % (16 * SLOW) == 0 else share
    block = lat.shape[1]
    half = block // 2
    vmem = pltpu.VMEM
    sem = pltpu.SemaphoreType.DMA
    return pl.pallas_call(
        functools.partial(sum_kernel, n_seq, n_ray, units, 2),
        out_shape=(
            jax.ShapeDtypeStruct((2, rows, width), bf16),
            jax.ShapeDtypeStruct((block, width), f32),
            jax.ShapeDtypeStruct(small.shape, f32),
        ),
        in_specs=[pl.BlockSpec(memory_space=vmem)] * 3,
        out_specs=(pl.BlockSpec(memory_space=pl.ANY), pl.BlockSpec(memory_space=vmem), pl.BlockSpec(memory_space=vmem)),
        scratch_shapes=[
            vmem((rows, width), bf16),
            vmem((rows, width), bf16),
            [vmem((rows >> (i + 1), width), bf16) for i in range(halvings)],
            vmem((units, 2, SLOW - 1, piece, width), bf16),
            vmem((units, 2, SLOW - 1, piece, width), bf16),
            vmem((piece, width), f32),
            vmem((2, rows, width), bf16),
            [vmem((2 * SLOW, place_fast >> (i + 1), half, width), bf16) for i in range(fast_bits)],
            vmem((SLOW, 2, half, width), bf16),
            vmem((2, 2, SLOW - 1, half, width), bf16),
            vmem((2, 2, SLOW - 1, half, width), bf16),
            vmem((exchanges + 1,) + small.shape, f32),
            vmem((exchanges,) + small.shape, f32),
            sem((2, units)),
            sem((2, halvings, units)),
            sem((2, units, 2, SLOW - 1)),
            sem((2, units, 2, SLOW - 1)),
            sem((2, halvings, units)),
            sem((2, units)),
            sem((2, units)),
            sem((2, fast_bits, 2 * SLOW)),
            sem((2, 2, 2, SLOW - 1)),
            sem((2, exchanges)),
        ],
        compiler_params=pltpu.CompilerParams(collective_id=1, has_side_effects=True, vmem_limit_bytes=60 << 20),
        name="sum_over_devices",
    )(grads, lat, small)


def local(
    rays,
    latents,
    lengths,
    scenes,
    ln_gain,
    ln_bias,
    w_query,
    b_query,
    w_key,
    w_value,
    b_value,
    w_out,
    b_out,
    w_up,
    b_up,
    w_down,
    b_down,
    cotangent,
):
    scale = HEAD ** (-0.5)
    width = rays.shape[1]
    groups = width // WIDE
    gathered = lax.all_gather(latents, "ray", axis=0, tiled=True)
    key_total = gathered.shape[0]
    tiles, order, meta = scene_plan(lengths[0], scenes, rays.shape[0])
    slots = tiles * TILE
    inputs = rays.astype(f32)
    row_mean = jnp.mean(inputs, axis=1, keepdims=True)
    centred = inputs - row_mean
    inverse = lax.rsqrt(jnp.mean(centred * centred, axis=1, keepdims=True) + 1e-05)
    normed = centred * inverse
    gain_full = ln_gain.astype(f32)
    shifted = (normed * gain_full + ln_bias.astype(f32)).astype(bf16)
    queries = (matmul(shifted, w_query, 1, 0) + b_query.astype(f32)).astype(bf16)
    q_sorted = (matmul(order, queries, 1, 0) * scale).astype(bf16)
    keys = matmul(gathered, w_key, 1, 0).astype(bf16)
    keys_t = matmul(w_key, gathered, 0, 1).astype(bf16)
    values = (matmul(gathered, w_value, 1, 0) + b_value.astype(f32)).astype(bf16)
    values_t = (matmul(w_value, gathered, 0, 1) + b_value.astype(f32)[:, None]).astype(bf16)

    smem = pl.BlockSpec(memory_space=pltpu.SMEM)
    slot_spec = pl.BlockSpec((slots, WIDE), lambda g: (0, g))
    key_spec = pl.BlockSpec((key_total, WIDE), lambda g: (0, g))
    turned_spec = pl.BlockSpec((WIDE, key_total), lambda g: (g, 0))
    lse_spec = pl.BlockSpec((1, tiles, WIDE), lambda g: (g, 0, 0))
    params = pltpu.CompilerParams(vmem_limit_bytes=48 << 20)
    att_sorted, lse = pl.pallas_call(
        functools.partial(attend_kernel, tiles),
        grid=(groups,),
        out_shape=(
            jax.ShapeDtypeStruct((slots, width), f32),
            jax.ShapeDtypeStruct((groups, tiles, WIDE), f32),
        ),
        in_specs=[smem, slot_spec, key_spec, turned_spec],
        out_specs=(slot_spec, lse_spec),
        scratch_shapes=[pltpu.VMEM((key_total, WIDE), f32)],
        compiler_params=params,
        name="attend",
    )(meta, q_sorted, keys, values_t)
    attended = matmul(order, att_sorted.astype(bf16), 0, 0).astype(bf16)

    hidden = inputs + matmul(attended, w_out, 1, 0) + b_out.astype(f32)
    hidden_low = hidden.astype(bf16)
    pre_act = matmul(hidden_low, w_up, 1, 0) + b_up.astype(f32)
    active = gelu_exact(pre_act).astype(bf16)
    result = hidden + matmul(active, w_down, 1, 0) + b_down.astype(f32)
    grad_top = cotangent.astype(f32)
    grad_w_down = matmul(active, cotangent, 0, 0)
    grad_b_down = jnp.sum(grad_top, axis=0)
    grad_active = matmul(cotangent, w_down, 1, 1)
    unused_value, gelu_back = jax.vjp(gelu_exact, pre_act)
    grad_pre = gelu_back(grad_active)[0].astype(bf16)
    grad_w_up = matmul(hidden_low, grad_pre, 0, 0)
    grad_b_up = jnp.sum(grad_pre.astype(f32), axis=0)
    grad_hidden = grad_top + matmul(grad_pre, w_up, 1, 1)
    grad_branch = grad_hidden.astype(bf16)
    grad_w_out = matmul(attended, grad_branch, 0, 0)
    grad_b_out = jnp.sum(grad_branch.astype(f32), axis=0)
    grad_attended = matmul(grad_branch, w_out, 1, 1).astype(bf16)
    g_sorted = matmul(order, grad_attended, 1, 0).astype(bf16)

    gq_sorted, grad_keys, grad_values = pl.pallas_call(
        functools.partial(attend_back_kernel, tiles),
        grid=(groups,),
        out_shape=(
            jax.ShapeDtypeStruct((slots, width), bf16),
            jax.ShapeDtypeStruct((key_total, width), bf16),
            jax.ShapeDtypeStruct((key_total, width), bf16),
        ),
        in_specs=[smem, slot_spec, key_spec, turned_spec, key_spec, slot_spec, slot_spec, lse_spec],
        out_specs=(slot_spec, key_spec, key_spec),
        scratch_shapes=[
            pltpu.VMEM((key_total, WIDE), f32),
            pltpu.VMEM((key_total, WIDE), f32),
            pltpu.VMEM((WIDE, WIDE), f32),
        ],
        compiler_params=params,
        name="attend_back",
    )(meta, q_sorted, keys, keys_t, values, g_sorted, att_sorted, lse)
    grad_queries = matmul(order, gq_sorted, 0, 0).astype(bf16)

    grad_w_query = matmul(shifted, grad_queries, 0, 0)
    grad_b_query = jnp.sum(grad_queries.astype(f32), axis=0)
    grad_shifted = matmul(grad_queries, w_query, 1, 1)
    grad_gain = jnp.sum(grad_shifted * normed, axis=0)
    grad_bias = jnp.sum(grad_shifted, axis=0)
    grad_normed = grad_shifted * gain_full
    grad_rays = grad_hidden + inverse * (
        grad_normed
        - jnp.mean(grad_normed, axis=1, keepdims=True)
        - normed * jnp.mean(grad_normed * normed, axis=1, keepdims=True)
    )
    grad_w_key = matmul(gathered, grad_keys, 0, 0)
    grad_w_value = matmul(gathered, grad_values, 0, 0)
    grad_b_value = jnp.sum(grad_values.astype(f32), axis=0)
    partial_latents = (matmul(grad_keys, w_key, 1, 1) + matmul(grad_values, w_value, 1, 1)).astype(bf16)
    n_seq, n_ray = lax.axis_size("seq"), lax.axis_size("ray")
    grads = jnp.stack(
        [
            jnp.concatenate([g.astype(bf16) for g in half], axis=0)
            for half in (
                (grad_w_query, grad_w_key, grad_w_up[:, :width], grad_w_down[:width]),
                (grad_w_value, grad_w_out, grad_w_up[:, width:], grad_w_down[width:]),
            )
        ]
    )
    small = jnp.stack(
        [grad_gain, grad_bias, grad_b_query, grad_b_value, grad_b_out, grad_b_up[:width], grad_b_up[width:], grad_b_down]
    )
    sums, grad_latents, rows = sum_over_devices(
        n_seq, n_ray, grads, partial_latents.reshape(n_ray, latents.shape[0], width), small
    )
    pieces = sums.reshape(2, 4, width, width)
    return (
        result.astype(bf16),
        grad_rays,
        grad_latents,
        rows[0],
        rows[1],
        pieces[0, 0].astype(f32),
        rows[2],
        pieces[0, 1].astype(f32),
        pieces[1, 0].astype(f32),
        rows[3],
        pieces[1, 1].astype(f32),
        rows[4],
        jnp.concatenate([pieces[0, 2], pieces[1, 2]], axis=1).astype(f32),
        rows[5:7].reshape(-1),
        jnp.concatenate([pieces[0, 3], pieces[1, 3]], axis=0).astype(f32),
        rows[7],
    )


def solution(mesh):
    whole = P(("seq", "ray"), None)
    in_specs = (whole, whole, P("seq", None), P(("seq", "ray"))) + (P(),) * 13 + (whole,)
    out_specs = (whole,) * 3 + (P(),) * 13
    return jax.shard_map(local, mesh=mesh, in_specs=in_specs, out_specs=out_specs, check_vma=False)
```

```python
import functools

import jax
import jax.numpy as jnp
from jax import lax
from jax.experimental import pallas as pl
from jax.experimental.pallas import tpu as pltpu
from jax.sharding import PartitionSpec as P

HEADS = 12
HEAD = 64
TILE = 64
WIDE = 256
PACK = WIDE // HEAD
CHUNK = 512

masked_score = -1e30
f32 = jnp.float32
bf16 = jnp.bfloat16


def matmul(first_arg, second_arg, first_dim, second_dim):
    return lax.dot_general(
        first_arg,
        second_arg,
        (((first_dim,), (second_dim,)), ((), ())),
        preferred_element_type=jnp.float32,
    )


def gelu_exact(pre_act):
    return jax.nn.gelu(pre_act, approximate=False)


def own_block():
    row = lax.broadcasted_iota(jnp.int32, (WIDE, WIDE), 0) // TILE
    column = lax.broadcasted_iota(jnp.int32, (WIDE, WIDE), 1) // HEAD
    return row == column


def spread_heads(tile):
    return jnp.where(own_block(), jnp.concatenate([tile] * PACK, axis=0), jnp.zeros((), tile.dtype))


def fold_heads(square):
    kept = jnp.where(own_block(), square, 0.0)
    return sum(kept[TILE * h : TILE * (h + 1), :] for h in range(PACK))


def fold_rows(block, combine):
    return combine(block.reshape(block.shape[0] // 8, 8, WIDE), axis=0)


def in_scene(chunk, start, end):
    rows = lax.broadcasted_iota(jnp.int32, (CHUNK, WIDE), 0) + chunk * CHUNK
    return (rows >= start) & (rows < end)


def chunk_at(chunk):
    return pl.ds(pl.multiple_of(chunk * CHUNK, CHUNK), CHUNK)


def group_at(g):
    return slice(g * WIDE, (g + 1) * WIDE)


def attend_kernel(counts, lengths, q_ref, k_ref, vt_ref, att_ref, lse_ref, s_ref, mixed_ref):
    groups = q_ref.shape[1] // WIDE
    used_tiles, bounds = scene_tiles(counts, lengths)
    att_ref[...] = jnp.zeros_like(att_ref)
    lse_ref[...] = jnp.zeros_like(lse_ref)

    def one_tile(t, carry):
        start, end = bounds(t)
        first, last = start // CHUNK, (end + CHUNK - 1) // CHUNK
        ray_rows = pl.ds(pl.multiple_of(t * TILE, TILE), TILE)
        spread = [spread_heads(q_ref[ray_rows, group_at(g)]) for g in range(groups)]

        def score(j, tops):
            seen = in_scene(j, start, end)
            new = []
            for g in range(groups):
                s = matmul(k_ref[chunk_at(j), group_at(g)], spread[g], 1, 1)
                s = jnp.where(seen, s, masked_score)
                s_ref[g, chunk_at(j), :] = s
                new.append(jnp.maximum(tops[g], fold_rows(s, jnp.max)))
            return tuple(new)

        tops = lax.fori_loop(first, last, score, (jnp.full((8, WIDE), masked_score, f32),) * groups)
        tops = [jnp.max(top, axis=0, keepdims=True) for top in tops]

        def expo(j, totals):
            new = []
            for g in range(groups):
                e = jnp.exp(s_ref[g, chunk_at(j), :] - tops[g])
                s_ref[g, chunk_at(j), :] = e
                new.append(totals[g] + fold_rows(e, jnp.sum))
            return tuple(new)

        totals = lax.fori_loop(first, last, expo, (jnp.zeros((8, WIDE), f32),) * groups)
        totals = [jnp.sum(total, axis=0, keepdims=True) for total in totals]
        rests = [1.0 / total for total in totals]

        def mix(j, carry):
            for g in range(groups):
                w = (s_ref[g, chunk_at(j), :] * rests[g]).astype(bf16)
                mixed_ref[g] += matmul(vt_ref[group_at(g), chunk_at(j)], w, 1, 0)
            return carry

        mixed_ref[...] = jnp.zeros_like(mixed_ref)
        lax.fori_loop(first, last, mix, 0)
        for g in range(groups):
            att_ref[ray_rows, group_at(g)] = fold_heads(mixed_ref[g].T)
            lse_ref[pl.ds(t, 1), group_at(g)] = tops[g] + jnp.log(totals[g])
        return carry

    lax.fori_loop(0, used_tiles, one_tile, 0)


def attend_back_kernel(counts, lengths, q_ref, k_ref, kt_ref, v_ref, g_ref, att_ref, lse_ref, gq_ref, gk_ref, gv_ref, gk_sum, gv_sum, gqt_sum):
    groups = q_ref.shape[1] // WIDE
    used_tiles, bounds = scene_tiles(counts, lengths)
    gq_ref[...] = jnp.zeros_like(gq_ref)
    gk_sum[...] = jnp.zeros_like(gk_sum)
    gv_sum[...] = jnp.zeros_like(gv_sum)

    def one_tile(t, carry):
        start, end = bounds(t)
        first, last = start // CHUNK, (end + CHUNK - 1) // CHUNK
        ray_rows = pl.ds(pl.multiple_of(t * TILE, TILE), TILE)
        q_spread, g_spread, dots, lse = [], [], [], []
        for g in range(groups):
            q_spread.append(spread_heads(q_ref[ray_rows, group_at(g)]))
            g_tile = g_ref[ray_rows, group_at(g)]
            g_spread.append(spread_heads(g_tile))
            product = spread_heads(g_tile.astype(f32) * att_ref[ray_rows, group_at(g)])
            dots.append(
                lax.dot_general(
                    jnp.ones((8, WIDE), f32),
                    product,
                    (((1,), (1,)), ((), ())),
                    precision=lax.Precision.HIGHEST,
                    preferred_element_type=f32,
                )[0:1, :]
            )
            lse.append(lse_ref[pl.ds(t, 1), group_at(g)])
        gqt_sum[...] = jnp.zeros_like(gqt_sum)

        def step(j, carry):
            at = chunk_at(j)
            seen = in_scene(j, start, end)
            for g in range(groups):
                to = group_at(g)
                s = matmul(k_ref[at, to], q_spread[g], 1, 1)
                p = jnp.where(seen, jnp.exp(s - lse[g]), 0.0)
                gv_sum[at, to] += matmul(p.astype(bf16), g_spread[g], 1, 0)
                gp = matmul(v_ref[at, to], g_spread[g], 1, 1)
                gs = (p * (gp - dots[g])).astype(bf16)
                gk_sum[at, to] += matmul(gs, q_spread[g], 1, 0)
                gqt_sum[g] += matmul(kt_ref[to, at], gs, 1, 0)
            return carry

        lax.fori_loop(first, last, step, 0)
        for g in range(groups):
            gq_ref[ray_rows, group_at(g)] = (fold_heads(gqt_sum[g].T) * HEAD ** (-0.5)).astype(bf16)
        return carry

    lax.fori_loop(0, used_tiles, one_tile, 0)
    gk_ref[...] = gk_sum[...].astype(bf16)
    gv_ref[...] = gv_sum[...].astype(bf16)


def attend(counts, lengths, q_sorted, keys, values_t):
    slots, width = q_sorted.shape
    key_total = keys.shape[0]
    vmem = pl.BlockSpec(memory_space=pltpu.VMEM)
    return pl.pallas_call(
        attend_kernel,
        out_shape=(
            jax.ShapeDtypeStruct((slots, width), f32),
            jax.ShapeDtypeStruct((slots // TILE, width), f32),
        ),
        in_specs=[pl.BlockSpec(memory_space=pltpu.SMEM)] * 2 + [vmem] * 3,
        out_specs=(vmem, vmem),
        scratch_shapes=[
            pltpu.VMEM((width // WIDE, key_total, WIDE), f32),
            pltpu.VMEM((width // WIDE, WIDE, WIDE), f32),
        ],
        compiler_params=pltpu.CompilerParams(vmem_limit_bytes=56 << 20),
        name="attend",
    )(counts, lengths, q_sorted, keys, values_t)


def attend_back(counts, lengths, q_sorted, keys, keys_t, values, g_sorted, att_sorted, lse):
    slots, width = q_sorted.shape
    key_total = keys.shape[0]
    vmem = pl.BlockSpec(memory_space=pltpu.VMEM)
    return pl.pallas_call(
        attend_back_kernel,
        out_shape=(
            jax.ShapeDtypeStruct((slots, width), bf16),
            jax.ShapeDtypeStruct((key_total, width), bf16),
            jax.ShapeDtypeStruct((key_total, width), bf16),
        ),
        in_specs=[pl.BlockSpec(memory_space=pltpu.SMEM)] * 2 + [vmem] * 7,
        out_specs=(vmem,) * 3,
        scratch_shapes=[
            pltpu.VMEM((key_total, width), f32),
            pltpu.VMEM((key_total, width), f32),
            pltpu.VMEM((width // WIDE, WIDE, WIDE), f32),
        ],
        compiler_params=pltpu.CompilerParams(vmem_limit_bytes=60 << 20),
        name="attend_back",
    )(counts, lengths, q_sorted, keys, keys_t, values, g_sorted, att_sorted, lse)


def scene_tiles(counts, lengths):
    kinds = lengths.shape[1]
    tile_ends, scene_ends, tiles, latents = [], [], 0, 0
    for c in range(kinds):
        tiles = tiles + (counts[c, 0] + TILE - 1) // TILE
        latents = latents + lengths[0, c]
        tile_ends.append(tiles)
        scene_ends.append(latents)

    def bounds(t):
        start, end = 0, scene_ends[0]
        for c in range(1, kinds):
            later = t >= tile_ends[c - 1]
            start = jnp.where(later, scene_ends[c - 1], start)
            end = jnp.where(later, scene_ends[c], end)
        return start, end

    return tiles, bounds


MESH = pl.DeviceIdType.MESH
SLOW = 4


def flip(index, bit):
    return index + bit * (1 - 2 * ((index // bit) % 2))


def bits_of(count):
    bits = []
    while count > 1:
        count //= 2
        bits.append(count)
    return bits


def lane_rows(start, size):
    return pl.ds(pl.multiple_of(start, 16), size)


class Place:
    def __init__(self, n_seq, n_ray):
        self.seq = lax.axis_index("seq")
        self.ray = lax.axis_index("ray")
        self.n_fast = n_ray // SLOW
        self.core = self.seq % 2
        self.slow = self.ray // self.n_fast
        self.fast = self.ray % self.n_fast
        self.x_bits = [("seq", 2 * b) for b in bits_of(n_seq // 2)]
        self.fast_bits = [("ray", b) for b in bits_of(self.n_fast)]
        self.slow_bits = [("ray", self.n_fast * b) for b in bits_of(SLOW)]
        self.spots = (self.slow, SLOW - 1 - self.slow)

    def across(self, axis, bit):
        if axis == "seq":
            return (flip(self.seq, bit), self.ray)
        return (self.seq, flip(self.ray, bit))

    def value(self, axis, bit):
        return ((self.seq if axis == "seq" else self.ray) // bit) % 2

    def along(self, way):
        return (self.seq, self.ray + (self.n_fast if way == 0 else -self.n_fast))

    def mirrored(self, way, chunk):
        return chunk if way == 0 else SLOW - 1 - chunk


def remote(src, dst, send_sem, recv_sem, device):
    return pltpu.make_async_remote_copy(
        src_ref=src,
        dst_ref=dst,
        send_sem=send_sem,
        recv_sem=recv_sem,
        device_id=device,
        device_id_type=MESH,
    )


def greet(place, exchanges):
    barrier = pltpu.get_barrier_semaphore()
    for axis, bit in exchanges:
        pl.semaphore_signal(barrier, inc=1, device_id=place.across(axis, bit), device_id_type=MESH)
    for step in (1, SLOW - 1):
        beside = (place.seq, (place.slow + step) % SLOW * place.n_fast + place.fast)
        pl.semaphore_signal(barrier, inc=1, device_id=beside, device_id_type=MESH)
    pl.semaphore_wait(barrier, len(exchanges) + 2)


class Line:
    def __init__(self, place, stage, recv, send_sem, recv_sem):
        self.place, self.stage, self.recv, self.send_sem, self.recv_sem = place, stage, recv, send_sem, recv_sem

    def copy(self, way, t):
        return remote(
            self.stage(way, t), self.recv(way, t), self.send_sem(way, t), self.recv_sem(way, t), self.place.along(way)
        )

    def landed(self, way, t):
        remote(
            self.stage(way, t), self.recv(way, t), self.send_sem(way, t), self.recv_sem(way, t), self.place.along(1 - way)
        ).wait_recv()
        return self.recv(way, t)[...].astype(f32)

    def step(self, t, own):
        for way in range(2):
            spot = self.place.spots[way]
            chunk = self.place.mirrored(way, SLOW - 1 - (t - spot))

            @pl.when((spot <= t) & (spot < SLOW - 1))
            def _(way=way, spot=spot, chunk=chunk):
                if t == 0:
                    self.stage(way, t)[...] = own(chunk).astype(bf16)
                else:

                    @pl.when(spot == 0)
                    def _():
                        self.stage(way, t)[...] = own(chunk).astype(bf16)

                    @pl.when(spot > 0)
                    def _():
                        self.stage(way, t)[...] = (own(chunk) + self.landed(way, t - 1)).astype(bf16)

                self.copy(way, t).start()

    def last(self, total):
        for way in range(2):

            @pl.when(self.place.spots[way] > 0)
            def _(way=way):
                total[...] += self.landed(way, SLOW - 2)

    def drain(self):
        for way in range(2):
            for t in range(SLOW - 1):
                spot = self.place.spots[way]

                @pl.when((spot <= t) & (spot < SLOW - 1))
                def _(way=way, t=t):
                    self.copy(way, t).wait_send()


class Spread:
    def __init__(self, place, block, send_sem, recv_sem):
        self.place, self.block, self.send_sem, self.recv_sem = place, block, send_sem, recv_sem

    def copy(self, way, t, to):
        chunk = self.place.mirrored(way, self.place.spots[way] - t)
        block = self.block(chunk)
        return remote(block, block, self.send_sem(way, t), self.recv_sem(way, t), self.place.along(to))

    def step(self, t):
        for way in range(2):
            spot = self.place.spots[way]

            @pl.when(spot >= t)
            def _(way=way, spot=spot):
                if t > 0:
                    block = self.block(self.place.mirrored(way, spot - t))
                    remote(
                        block, block, self.send_sem(way, t - 1), self.recv_sem(way, t - 1), self.place.along(1 - way)
                    ).wait_recv()
                if t < SLOW - 1:

                    @pl.when(spot < SLOW - 1)
                    def _():
                        self.copy(way, t, way).start()

    def drain(self):
        for way in range(2):
            for t in range(SLOW - 1):
                spot = self.place.spots[way]

                @pl.when((spot >= t) & (spot < SLOW - 1))
                def _(way=way, t=t):
                    self.copy(way, t, way).wait_send()


def units_of(rows, n_x, n_fast):
    share = n_x * n_fast * SLOW * 16
    return max(1, min(12, rows // share))


def sum_kernel(
    n_seq,
    n_ray,
    units,
    beat,
    g_ref,
    lat_ref,
    small_ref,
    out_ref,
    glat_ref,
    small_out,
    rc,
    held,
    rx,
    z_stage,
    z_recv,
    z_total,
    full,
    lat_recv,
    lat_own,
    lz_stage,
    lz_recv,
    small_now,
    small_recv,
    core_sem,
    halve_sem,
    z_sem,
    zg_sem,
    double_sem,
    core_back_sem,
    out_sem,
    lat_sem,
    lz_sem,
    small_sem,
):
    place = Place(n_seq, n_ray)
    core_pair = ("seq", 1)
    halvings = place.x_bits + place.fast_bits
    exchanges = [core_pair] + halvings + place.slow_bits
    greet(place, exchanges)

    rows = g_ref.shape[1]
    unit_rows = rows // units
    core = place.core
    sizes = [unit_rows >> i for i in range(len(halvings) + 1)]
    share = sizes[-1]
    line = share % (16 * SLOW) == 0
    piece = share // SLOW if line else share

    def base(u, stages):
        start = u * unit_rows
        for i in range(stages):
            start = start + place.value(*halvings[i]) * sizes[i + 1]
        return start

    def unit(u):
        return lane_rows(u * unit_rows, unit_rows)

    def core_copy(u):
        return remote(
            g_ref.at[1 - core, unit(u)], rc.at[unit(u)], core_sem.at[0, u], core_sem.at[1, u], place.across(*core_pair)
        )

    def halve_copy(i, u):
        size = sizes[i + 1]
        sent = base(u, i) + (1 - place.value(*halvings[i])) * size
        return remote(
            held.at[lane_rows(sent, size)],
            rx[i].at[lane_rows(u * size, size)],
            halve_sem.at[0, i, u],
            halve_sem.at[1, i, u],
            place.across(*halvings[i]),
        )

    def start_core(u):
        core_copy(u).start()

    def join_core(u):
        core_copy(u).wait()
        held[unit(u), :] = (g_ref[core, unit(u), :].astype(f32) + rc[unit(u), :].astype(f32)).astype(bf16)
        halve_copy(0, u).start()

    def join_half(i):
        def run(u):
            size = sizes[i + 1]
            halve_copy(i, u).wait()
            kept = lane_rows(base(u, i + 1), size)
            held[kept, :] = (held[kept, :].astype(f32) + rx[i][lane_rows(u * size, size), :].astype(f32)).astype(bf16)
            if i + 1 < len(halvings):
                halve_copy(i + 1, u).start()

        return run

    def z_line(u):
        return Line(
            place,
            lambda way, t: z_stage.at[u, way, t],
            lambda way, t: z_recv.at[u, way, t],
            lambda way, t: z_sem.at[0, u, way, t],
            lambda way, t: z_sem.at[1, u, way, t],
        )

    def z_rows(u, chunk):
        return lane_rows(base(u, len(halvings)) + chunk * piece, piece)

    def z_own(u):
        return lambda chunk: held[z_rows(u, chunk), :].astype(f32)

    def z_spread(u):
        return Spread(
            place,
            lambda chunk: full.at[core, z_rows(u, chunk)],
            lambda way, t: zg_sem.at[0, u, way, t],
            lambda way, t: zg_sem.at[1, u, way, t],
        )

    def z_step(t):
        return lambda u: z_line(u).step(t, z_own(u))

    def z_finish(u):
        z_total[...] = z_own(u)(place.slow)
        z_line(u).last(z_total)
        full[core, z_rows(u, place.slow), :] = z_total[...].astype(bf16)
        z_spread(u).step(0)

    def spread_step(t):
        return lambda u: z_spread(u).step(t)

    def whole_copy(i, u):
        return remote(
            held.at[lane_rows(base(u, len(halvings)), share)],
            z_recv.at[u, 0, i],
            z_sem.at[0, u, 0, i],
            z_sem.at[1, u, 0, i],
            place.across(*place.slow_bits[i]),
        )

    def whole_step(i):
        def run(u):
            mine = lane_rows(base(u, len(halvings)), share)
            if i > 0:
                whole_copy(i - 1, u).wait()
                held[mine, :] = (held[mine, :].astype(f32) + z_recv[u, 0, i - 1].astype(f32)).astype(bf16)
            if i < len(place.slow_bits):
                whole_copy(i, u).start()
            else:
                full[core, mine, :] = held[mine, :]

        return run

    def double_copy(i, u):
        block = full.at[core, lane_rows(base(u, i + 1), sizes[i + 1])]
        return remote(block, block, double_sem.at[0, i, u], double_sem.at[1, i, u], place.across(*halvings[i]))

    def core_back(u):
        block = full.at[core, unit(u)]
        return remote(block, block, core_back_sem.at[0, u], core_back_sem.at[1, u], place.across(*core_pair))

    def out_copy(half, u):
        return pltpu.make_async_copy(full.at[half, unit(u)], out_ref.at[half, unit(u)], out_sem.at[half, u])

    def start_double(u):
        double_copy(len(halvings) - 1, u).start()

    def join_double(i):
        def run(u):
            double_copy(i, u).wait()
            if i > 0:
                double_copy(i - 1, u).start()
            else:
                core_back(u).start()
                out_copy(core, u).start()

        return run

    def finish_unit(u):
        core_back(u).wait()
        out_copy(1 - core, u).start()
        if line:
            z_line(u).drain()
            z_spread(u).drain()

    stages = [[start_core], [join_core]] + [[join_half(i)] for i in range(len(halvings))]
    if line:
        stages[-1].append(z_step(0))
        stages += [[z_step(t)] for t in range(1, SLOW - 1)]
        stages += [[z_finish]] + [[spread_step(t)] for t in range(1, SLOW)]
    else:
        stages[-1].append(whole_step(0))
        stages += [[whole_step(i)] for i in range(1, len(place.slow_bits) + 1)]
    stages[-1].append(start_double)
    stages.insert(2, [])
    stages += [[join_double(i)] for i in reversed(range(len(halvings)))]
    stages.insert(-1, [])
    stages += [[finish_unit]]

    half_rows = lat_ref.shape[1] // 2
    n_fast = place.n_fast
    fast_sizes = [n_fast >> i for i in range(len(place.fast_bits) + 1)]

    def chunk_of(k):
        near = jnp.minimum(place.slow, SLOW - 1 - place.slow)
        ahead = SLOW - 1 - near
        chunk = jnp.where(k < ahead, SLOW - 1 - k, jnp.where(k - ahead < near, k - ahead, near))
        return jnp.where(place.slow == near, chunk, SLOW - 1 - chunk)

    def lat_base(i):
        start = 0
        for n in range(i):
            start = start + place.value(*place.fast_bits[n]) * fast_sizes[n + 1]
        return start

    def lat_half(m):
        return lane_rows((m % 2) * half_rows, half_rows)

    def lat_copy(i, m):
        size = fast_sizes[i + 1]
        other = (1 - place.value(*place.fast_bits[i])) * size
        if i == 0:
            source = lat_ref.at[pl.ds(chunk_of(m // 2) * n_fast + other, size), lat_half(m)]
        else:
            source = lat_recv[i - 1].at[m, pl.ds(other, size)]
        return remote(
            source, lat_recv[i].at[m], lat_sem.at[0, i, m], lat_sem.at[1, i, m], place.across(*place.fast_bits[i])
        )

    def start_lat(m):
        lat_copy(0, m).start()

    def lat_line(m):
        half = m % 2
        return Line(
            place,
            lambda way, t: lz_stage.at[half, way, t],
            lambda way, t: lz_recv.at[half, way, t],
            lambda way, t: lz_sem.at[0, half, way, t],
            lambda way, t: lz_sem.at[1, half, way, t],
        )

    def join_lat(i):
        def run(m):
            size = fast_sizes[i + 1]
            lat_copy(i, m).wait()
            mine = place.value(*place.fast_bits[i]) * size
            if i == 0:
                kept = lat_ref[pl.ds(chunk_of(m // 2) * n_fast + mine, size), lat_half(m), :]
            else:
                kept = lat_recv[i - 1][m, pl.ds(mine, size)]
            joined = (kept.astype(f32) + lat_recv[i][m].astype(f32)).astype(bf16)
            if i + 1 < len(place.fast_bits):
                lat_recv[i][m] = joined
                lat_copy(i + 1, m).start()
            else:
                lat_own[chunk_of(m // 2), m % 2] = joined[0]
                walk_lat(m)

        return run

    def walk_lat(m):
        half = m % 2

        def own(chunk):
            return lat_own[chunk, half].astype(f32)

        for t in range(SLOW - 1):

            @pl.when(m // 2 == t)
            def _(t=t):
                lat_line(m).step(t, own)

    def finish_lat(m):
        @pl.when(m // 2 == SLOW - 1)
        def _():
            mine = glat_ref.at[lat_half(m)]
            mine[...] = lat_own[place.slow, m % 2].astype(f32)
            lat_line(m).last(mine)
            lat_line(m).drain()

    lat_stages = [start_lat] + [join_lat(i) for i in range(len(place.fast_bits))] + [finish_lat]
    lat_steps = 2 * SLOW

    def small_copy(i):
        axis, bit = exchanges[i]
        return remote(
            small_now.at[i], small_recv.at[i], small_sem.at[0, i], small_sem.at[1, i], place.across(axis, bit)
        )

    small_now[0] = small_ref[...]
    small_copy(0).start()

    lat_span = beat * (lat_steps - 1 + len(lat_stages) - 1) + 1
    beats = max(units + len(stages) - 1, lat_span, len(exchanges) + 1)

    def one_beat(now, carry):
        for s in range(len(stages)):
            u = now - s

            @pl.when((u >= 0) & (u < units))
            def _(u=u, s=s):
                for run in stages[s]:
                    run(u)

        for s in range(len(lat_stages)):
            ahead = now - beat * s
            m = ahead // beat

            @pl.when((ahead >= 0) & (ahead % beat == 0) & (m < lat_steps))
            def _(m=m, s=s):
                lat_stages[s](m)

        for i in range(len(exchanges)):

            @pl.when(now == i + 1)
            def _(i=i):
                small_copy(i).wait()
                small_now[i + 1] = small_now[i] + small_recv[i]
                if i + 1 < len(exchanges):
                    small_copy(i + 1).start()

        return carry

    lax.fori_loop(0, beats, one_beat, 0)
    small_out[...] = small_now[len(exchanges)]

    def end_out(u, carry):
        out_copy(0, u).wait()
        out_copy(1, u).wait()
        return carry

    lax.fori_loop(0, units, end_out, 0)


def sum_over_devices(n_seq, n_ray, grads, lat, small):
    place_fast = n_ray // SLOW
    rows, width = grads.shape[1:]
    n_x = n_seq // 2
    units = units_of(rows, n_x, place_fast)
    halvings = len(bits_of(n_x)) + len(bits_of(place_fast))
    fast_bits = len(bits_of(place_fast))
    exchanges = 1 + halvings + len(bits_of(SLOW))
    unit_rows = rows // units
    share = unit_rows >> halvings
    piece = share // SLOW if share % (16 * SLOW) == 0 else share
    block = lat.shape[1]
    half = block // 2
    vmem = pltpu.VMEM
    sem = pltpu.SemaphoreType.DMA
    return pl.pallas_call(
        functools.partial(sum_kernel, n_seq, n_ray, units, 3),
        out_shape=(
            jax.ShapeDtypeStruct((2, rows, width), bf16),
            jax.ShapeDtypeStruct((block, width), f32),
            jax.ShapeDtypeStruct(small.shape, f32),
        ),
        in_specs=[pl.BlockSpec(memory_space=vmem)] * 3,
        out_specs=(pl.BlockSpec(memory_space=pl.ANY), pl.BlockSpec(memory_space=vmem), pl.BlockSpec(memory_space=vmem)),
        scratch_shapes=[
            vmem((rows, width), bf16),
            vmem((rows, width), bf16),
            [vmem((rows >> (i + 1), width), bf16) for i in range(halvings)],
            vmem((units, 2, SLOW - 1, piece, width), bf16),
            vmem((units, 2, SLOW - 1, piece, width), bf16),
            vmem((piece, width), f32),
            vmem((2, rows, width), bf16),
            [vmem((2 * SLOW, place_fast >> (i + 1), half, width), bf16) for i in range(fast_bits)],
            vmem((SLOW, 2, half, width), bf16),
            vmem((2, 2, SLOW - 1, half, width), bf16),
            vmem((2, 2, SLOW - 1, half, width), bf16),
            vmem((exchanges + 1,) + small.shape, f32),
            vmem((exchanges,) + small.shape, f32),
            sem((2, units)),
            sem((2, halvings, units)),
            sem((2, units, 2, SLOW - 1)),
            sem((2, units, 2, SLOW - 1)),
            sem((2, halvings, units)),
            sem((2, units)),
            sem((2, units)),
            sem((2, fast_bits, 2 * SLOW)),
            sem((2, 2, 2, SLOW - 1)),
            sem((2, exchanges)),
        ],
        compiler_params=pltpu.CompilerParams(collective_id=1, has_side_effects=True, vmem_limit_bytes=60 << 20),
        name="sum_over_devices",
    )(grads, lat, small)


def gather_kernel(
    n_seq,
    n_ray,
    kinds,
    rays_ref,
    lat_ref,
    scenes_ref,
    rows_ref,
    wq_ref,
    wk_ref,
    wv_ref,
    all_ref,
    k_ref,
    kt_ref,
    v_ref,
    vt_ref,
    qs_ref,
    order_ref,
    shifted_ref,
    counts_ref,
    full,
    k_own,
    kt_own,
    v_own,
    vt_own,
    z_sem,
    y_sem,
    out_sem,
):
    place = Place(n_seq, n_ray)
    fast_bits = place.fast_bits[::-1]
    greet(place, place.fast_bits)
    block, width = lat_ref.shape
    half_rows = block // 2
    group = place.n_fast * block
    full[place.slow, place.fast] = lat_ref[...]

    def half_at(half):
        return pl.ds(half * half_rows, half_rows)

    def spread(half):
        return Spread(
            place,
            lambda chunk: full.at[chunk, place.fast, half_at(half)],
            lambda way, t: z_sem.at[0, half, way, t],
            lambda way, t: z_sem.at[1, half, way, t],
        )

    def fast_copy(i, chunk, half):
        axis, bit = fast_bits[i]
        mine = full.at[chunk, pl.ds(place.fast // bit * bit, bit), half_at(half)]
        return remote(mine, mine, y_sem.at[0, i, chunk, half], y_sem.at[1, i, chunk, half], place.across(axis, bit))

    def chunk_of(way, t):
        return place.mirrored(way, place.spots[way] - t)

    for half in range(2):
        fast_copy(0, place.slow, half).start()
        spread(half).step(0)

    inputs = rays_ref[...].astype(f32)
    centred = inputs - jnp.mean(inputs, axis=1, keepdims=True)
    inverse = lax.rsqrt(jnp.mean(centred * centred, axis=1, keepdims=True) + 1e-05)
    shifted = (centred * inverse * rows_ref[0:1, :] + rows_ref[1:2, :]).astype(bf16)
    shifted_ref[...] = shifted
    queries = (matmul(shifted, wq_ref[...], 1, 0) + rows_ref[2:3, :]).astype(bf16)
    n_rays = rays_ref.shape[0]
    slots = order_ref.shape[0]
    scenes = scenes_ref[...]
    same = scenes == lax.broadcasted_iota(jnp.int32, (8, n_rays), 0)
    one_hot = same.astype(f32)
    before = (
        lax.broadcasted_iota(jnp.int32, (n_rays, n_rays), 0) < lax.broadcasted_iota(jnp.int32, (n_rays, n_rays), 1)
    ).astype(bf16)
    rank = matmul(one_hot.astype(bf16), before, 1, 0)
    counts = jnp.sum(one_hot, axis=1, keepdims=True)
    counts_ref[...] = jnp.broadcast_to(counts, counts_ref.shape).astype(jnp.int32)
    scene_tiles = jnp.floor((counts + (TILE - 1)) * (1.0 / TILE))
    slot = jnp.zeros((1, n_rays), f32)
    first = jnp.zeros((1, 1), f32)
    for c in range(kinds):
        slot = slot + jnp.where(same[c : c + 1, :], rank[c : c + 1, :] + first, 0.0)
        first = first + scene_tiles[c : c + 1, :] * TILE
    order = (lax.broadcasted_iota(jnp.int32, (slots, n_rays), 0) == slot.astype(jnp.int32)).astype(f32).astype(bf16)
    order_ref[...] = order
    qs_ref[...] = (matmul(order, queries, 1, 0) * HEAD ** (-0.5)).astype(bf16)

    def results(chunk):
        rows = pl.ds(pl.multiple_of(chunk * group, 16), group)
        columns = pl.ds(pl.multiple_of(chunk * group, 128), group)
        return [
            (k_own.at[chunk], k_ref.at[rows]),
            (kt_own.at[chunk], kt_ref.at[:, columns]),
            (v_own.at[chunk], v_ref.at[rows]),
            (vt_own.at[chunk], vt_ref.at[:, columns]),
        ] + [
            (full.at[chunk, f], all_ref.at[pl.ds(pl.multiple_of(chunk * group + f * block, 16), block)])
            for f in range(place.n_fast)
        ]

    def project(chunk):
        for half in range(2):
            for i in range(len(fast_bits)):
                fast_copy(i, chunk, half).wait()
                if i + 1 < len(fast_bits):
                    fast_copy(i + 1, chunk, half).start()
        latents = full[chunk].reshape(group, width)
        keys = matmul(latents, wk_ref[...], 1, 0).astype(bf16)
        k_own[chunk] = keys
        kt_own[chunk] = keys.T
        values = (matmul(latents, wv_ref[...], 1, 0) + rows_ref[3:4, :]).astype(bf16)
        v_own[chunk] = values
        vt_own[chunk] = values.T
        for n, (source, target) in enumerate(results(chunk)):
            pltpu.make_async_copy(source, target, out_sem.at[n, chunk]).start()

    def visit(index, carry):
        t, way = index // 2, index % 2
        for later in range(1, SLOW):

            @pl.when(index == 2 * (later - 1))
            def _(later=later):
                for half in range(2):
                    spread(half).step(later)
                    for to in range(2):

                        @pl.when(place.spots[to] >= later)
                        def _(half=half, to=to):
                            fast_copy(0, chunk_of(to, later), half).start()

        spot = jnp.where(way == 0, place.slow, SLOW - 1 - place.slow)
        chunk = jnp.where(way == 0, spot - t, SLOW - 1 - spot + t)

        @pl.when((spot >= t) & (index != 1))
        def _():
            project(chunk)

        return carry

    lax.fori_loop(0, 2 * SLOW, visit, 0)

    def end(chunk, carry):
        for n, (source, target) in enumerate(results(chunk)):
            pltpu.make_async_copy(source, target, out_sem.at[n, chunk]).wait()
        return carry

    lax.fori_loop(0, SLOW, end, 0)
    for half in range(2):
        spread(half).drain()


def gather_and_project(n_seq, n_ray, kinds, rays, latents, scenes, rows, w_query, w_key, w_value):
    block, width = latents.shape
    n_rays = rays.shape[0]
    n_fast = n_ray // SLOW
    group = n_fast * block
    total = n_ray * block
    tiles = n_rays // TILE + kinds - 1
    fast_bits = len(bits_of(n_fast))
    vmem = pltpu.VMEM
    sem = pltpu.SemaphoreType.DMA
    in_vmem = pl.BlockSpec(memory_space=vmem)
    anywhere = pl.BlockSpec(memory_space=pl.ANY)
    tall = jax.ShapeDtypeStruct((total, width), bf16)
    wide = jax.ShapeDtypeStruct((width, total), bf16)
    return pl.pallas_call(
        functools.partial(gather_kernel, n_seq, n_ray, kinds),
        out_shape=(
            tall,
            tall,
            wide,
            tall,
            wide,
            jax.ShapeDtypeStruct((tiles * TILE, width), bf16),
            jax.ShapeDtypeStruct((tiles * TILE, n_rays), bf16),
            jax.ShapeDtypeStruct((n_rays, width), bf16),
            jax.ShapeDtypeStruct((8, 128), jnp.int32),
        ),
        in_specs=[in_vmem] * 7,
        out_specs=(anywhere,) * 5 + (in_vmem,) * 4,
        scratch_shapes=[
            vmem((SLOW, n_fast, block, width), bf16),
            vmem((SLOW, group, width), bf16),
            vmem((SLOW, width, group), bf16),
            vmem((SLOW, group, width), bf16),
            vmem((SLOW, width, group), bf16),
            sem((2, 2, 2, SLOW - 1)),
            sem((2, fast_bits, SLOW, 2)),
            sem((4 + n_fast, SLOW)),
        ],
        compiler_params=pltpu.CompilerParams(collective_id=0, has_side_effects=True, vmem_limit_bytes=48 << 20),
        name="gather_and_project",
    )(rays, latents, scenes, rows, w_query, w_key, w_value)


def local(
    rays,
    latents,
    lengths,
    scenes,
    ln_gain,
    ln_bias,
    w_query,
    b_query,
    w_key,
    w_value,
    b_value,
    w_out,
    b_out,
    w_up,
    b_up,
    w_down,
    b_down,
    cotangent,
):
    width = rays.shape[1]
    n_seq, n_ray = lax.axis_size("seq"), lax.axis_size("ray")
    vectors = (ln_gain, ln_bias, b_query, b_value)
    gathered, keys, keys_t, values, values_t, q_sorted, order, shifted, counts = gather_and_project(
        n_seq,
        n_ray,
        lengths.shape[1],
        rays,
        latents,
        scenes.reshape(1, -1),
        jnp.concatenate([v.reshape(1, width) for v in vectors] * 2).astype(f32),
        w_query,
        w_key,
        w_value,
    )
    inputs = rays.astype(f32)
    row_mean = jnp.mean(inputs, axis=1, keepdims=True)
    centred = inputs - row_mean
    inverse = lax.rsqrt(jnp.mean(centred * centred, axis=1, keepdims=True) + 1e-05)
    normed = centred * inverse
    gain_full = ln_gain.astype(f32)
    att_sorted, lse = attend(counts, lengths, q_sorted, keys, values_t)
    attended = matmul(order, att_sorted.astype(bf16), 0, 0).astype(bf16)

    hidden = inputs + matmul(attended, w_out, 1, 0) + b_out.astype(f32)
    hidden_low = hidden.astype(bf16)
    pre_act = matmul(hidden_low, w_up, 1, 0) + b_up.astype(f32)
    active = gelu_exact(pre_act).astype(bf16)
    result = hidden + matmul(active, w_down, 1, 0) + b_down.astype(f32)
    grad_top = cotangent.astype(f32)
    grad_w_down = matmul(active, cotangent, 0, 0)
    grad_b_down = jnp.sum(grad_top, axis=0)
    grad_active = matmul(cotangent, w_down, 1, 1)
    unused_value, gelu_back = jax.vjp(gelu_exact, pre_act)
    grad_pre = gelu_back(grad_active)[0].astype(bf16)
    grad_w_up = matmul(hidden_low, grad_pre, 0, 0)
    grad_b_up = jnp.sum(grad_pre.astype(f32), axis=0)
    grad_hidden = grad_top + matmul(grad_pre, w_up, 1, 1)
    grad_branch = grad_hidden.astype(bf16)
    grad_w_out = matmul(attended, grad_branch, 0, 0)
    grad_b_out = jnp.sum(grad_branch.astype(f32), axis=0)
    grad_attended = matmul(grad_branch, w_out, 1, 1).astype(bf16)
    g_sorted = matmul(order, grad_attended, 1, 0).astype(bf16)

    gq_sorted, grad_keys, grad_values = attend_back(
        counts, lengths, q_sorted, keys, keys_t, values, g_sorted, att_sorted, lse
    )
    grad_queries = matmul(order, gq_sorted, 0, 0).astype(bf16)

    grad_w_query = matmul(shifted, grad_queries, 0, 0)
    grad_b_query = jnp.sum(grad_queries.astype(f32), axis=0)
    grad_shifted = matmul(grad_queries, w_query, 1, 1)
    grad_gain = jnp.sum(grad_shifted * normed, axis=0)
    grad_bias = jnp.sum(grad_shifted, axis=0)
    grad_normed = grad_shifted * gain_full
    grad_rays = grad_hidden + inverse * (
        grad_normed
        - jnp.mean(grad_normed, axis=1, keepdims=True)
        - normed * jnp.mean(grad_normed * normed, axis=1, keepdims=True)
    )
    grad_w_key = matmul(gathered, grad_keys, 0, 0)
    grad_w_value = matmul(gathered, grad_values, 0, 0)
    grad_b_value = jnp.sum(grad_values.astype(f32), axis=0)
    partial_latents = (matmul(grad_keys, w_key, 1, 1) + matmul(grad_values, w_value, 1, 1)).astype(bf16)
    grads = jnp.stack(
        [
            jnp.concatenate([g.astype(bf16) for g in half], axis=0)
            for half in (
                (grad_w_query, grad_w_key, grad_w_up[:, :width], grad_w_down[:width]),
                (grad_w_value, grad_w_out, grad_w_up[:, width:], grad_w_down[width:]),
            )
        ]
    )
    small = jnp.stack(
        [grad_gain, grad_bias, grad_b_query, grad_b_value, grad_b_out, grad_b_up[:width], grad_b_up[width:], grad_b_down]
    )
    sums, grad_latents, rows = sum_over_devices(
        n_seq, n_ray, grads, partial_latents.reshape(n_ray, latents.shape[0], width), small
    )
    pieces = sums.reshape(2, 4, width, width)
    return (
        result.astype(bf16),
        grad_rays,
        grad_latents,
        rows[0],
        rows[1],
        pieces[0, 0].astype(f32),
        rows[2],
        pieces[0, 1].astype(f32),
        pieces[1, 0].astype(f32),
        rows[3],
        pieces[1, 1].astype(f32),
        rows[4],
        jnp.concatenate([pieces[0, 2], pieces[1, 2]], axis=1).astype(f32),
        rows[5:7].reshape(-1),
        jnp.concatenate([pieces[0, 3], pieces[1, 3]], axis=0).astype(f32),
        rows[7],
    )


def solution(mesh):
    whole = P(("seq", "ray"), None)
    in_specs = (whole, whole, P("seq", None), P(("seq", "ray"))) + (P(),) * 13 + (whole,)
    out_specs = (whole,) * 3 + (P(),) * 13
    return jax.shard_map(local, mesh=mesh, in_specs=in_specs, out_specs=out_specs, check_vma=False)
```

```python
import functools
import math

import jax
import jax.numpy as jnp
from jax import lax
from jax.experimental import pallas as pl
from jax.experimental.pallas import tpu as pltpu
from jax.sharding import PartitionSpec as P

HEADS = 12
HEAD = 64
TILE = 64
WIDE = 256
PACK = WIDE // HEAD
CHUNK = 512

masked_score = -1e30
f32 = jnp.float32
bf16 = jnp.bfloat16


def matmul(first_arg, second_arg, first_dim, second_dim):
    return lax.dot_general(
        first_arg,
        second_arg,
        (((first_dim,), (second_dim,)), ((), ())),
        preferred_element_type=jnp.float32,
    )


def own_block():
    row = lax.broadcasted_iota(jnp.int32, (WIDE, WIDE), 0) // TILE
    column = lax.broadcasted_iota(jnp.int32, (WIDE, WIDE), 1) // HEAD
    return row == column


def spread_heads(tile):
    return jnp.where(own_block(), jnp.concatenate([tile] * PACK, axis=0), jnp.zeros((), tile.dtype))


def fold_heads(square):
    kept = jnp.where(own_block(), square, 0.0)
    return sum(kept[TILE * h : TILE * (h + 1), :] for h in range(PACK))


def fold_rows(block, combine):
    return combine(block.reshape(block.shape[0] // 8, 8, WIDE), axis=0)


def in_scene(chunk, start, end):
    rows = lax.broadcasted_iota(jnp.int32, (CHUNK, WIDE), 0) + chunk * CHUNK
    return (rows >= start) & (rows < end)


def chunk_at(chunk):
    return pl.ds(pl.multiple_of(chunk * CHUNK, CHUNK), CHUNK)


def group_at(g):
    return slice(g * WIDE, (g + 1) * WIDE)


def scene_tiles(counts, lengths):
    kinds = lengths.shape[1]
    tile_ends, scene_ends, tiles, latents = [], [], 0, 0
    for c in range(kinds):
        tiles = tiles + (counts[c, 0] + TILE - 1) // TILE
        latents = latents + lengths[0, c]
        tile_ends.append(tiles)
        scene_ends.append(latents)

    def bounds(t):
        start, end = 0, scene_ends[0]
        for c in range(1, kinds):
            later = t >= tile_ends[c - 1]
            start = jnp.where(later, scene_ends[c - 1], start)
            end = jnp.where(later, scene_ends[c], end)
        return start, end

    return tiles, bounds


def gelu_both(pre):
    half = 0.5 * (1.0 + lax.erf(pre * math.sqrt(0.5)))
    return pre * half, half + pre * jnp.exp(-0.5 * pre * pre) * (1.0 / math.sqrt(2.0 * math.pi))


def attend(used_tiles, bounds, q_ref, k_ref, vt_ref, att_ref, lse_ref, s_ref, mixed_ref):
    groups = q_ref.shape[1] // WIDE
    att_ref[...] = jnp.zeros_like(att_ref)

    def one_tile(t, carry):
        start, end = bounds(t)
        first, last = start // CHUNK, (end + CHUNK - 1) // CHUNK
        ray_rows = pl.ds(pl.multiple_of(t * TILE, TILE), TILE)
        spread = [spread_heads(q_ref[ray_rows, group_at(g)]) for g in range(groups)]

        def score(j, tops):
            seen = in_scene(j, start, end)
            new = []
            for g in range(groups):
                s = matmul(k_ref[chunk_at(j), group_at(g)], spread[g], 1, 1)
                s = jnp.where(seen, s, masked_score)
                s_ref[chunk_at(j), group_at(g)] = s
                new.append(jnp.maximum(tops[g], fold_rows(s, jnp.max)))
            return tuple(new)

        tops = lax.fori_loop(first, last, score, (jnp.full((8, WIDE), masked_score, f32),) * groups)
        tops = [jnp.max(top, axis=0, keepdims=True) for top in tops]

        def expo(j, totals):
            new = []
            for g in range(groups):
                e = jnp.exp(s_ref[chunk_at(j), group_at(g)] - tops[g])
                s_ref[chunk_at(j), group_at(g)] = e
                new.append(totals[g] + fold_rows(e, jnp.sum))
            return tuple(new)

        totals = lax.fori_loop(first, last, expo, (jnp.zeros((8, WIDE), f32),) * groups)
        totals = [jnp.sum(total, axis=0, keepdims=True) for total in totals]
        rests = [1.0 / total for total in totals]

        def mix(j, carry):
            for g in range(groups):
                w = (s_ref[chunk_at(j), group_at(g)] * rests[g]).astype(bf16)
                mixed_ref[g] += matmul(vt_ref[group_at(g), chunk_at(j)], w, 1, 0)
            return carry

        mixed_ref[...] = jnp.zeros_like(mixed_ref)
        lax.fori_loop(first, last, mix, 0)
        for g in range(groups):
            att_ref[ray_rows, group_at(g)] = fold_heads(mixed_ref[g].T)
            lse_ref[pl.ds(t, 1), group_at(g)] = tops[g] + jnp.log(totals[g])
        return carry

    lax.fori_loop(0, used_tiles, one_tile, 0)


def attend_back(
    used_tiles, bounds, q_ref, k_ref, kt_ref, v_ref, g_ref, att_ref, lse_ref, gq_ref, gk_sum, gv_sum, gqt_sum
):
    groups = q_ref.shape[1] // WIDE
    gq_ref[...] = jnp.zeros_like(gq_ref)
    gk_sum[...] = jnp.zeros_like(gk_sum)
    gv_sum[...] = jnp.zeros_like(gv_sum)

    def one_tile(t, carry):
        start, end = bounds(t)
        first, last = start // CHUNK, (end + CHUNK - 1) // CHUNK
        ray_rows = pl.ds(pl.multiple_of(t * TILE, TILE), TILE)
        q_spread, g_spread, dots, lse = [], [], [], []
        for g in range(groups):
            q_spread.append(spread_heads(q_ref[ray_rows, group_at(g)]))
            g_tile = g_ref[ray_rows, group_at(g)]
            g_spread.append(spread_heads(g_tile))
            product = spread_heads(g_tile.astype(f32) * att_ref[ray_rows, group_at(g)])
            dots.append(
                lax.dot_general(
                    jnp.ones((8, WIDE), f32),
                    product,
                    (((1,), (1,)), ((), ())),
                    precision=lax.Precision.HIGHEST,
                    preferred_element_type=f32,
                )[0:1, :]
            )
            lse.append(lse_ref[pl.ds(t, 1), group_at(g)])
        gqt_sum[...] = jnp.zeros_like(gqt_sum)

        def step(j, carry):
            at = chunk_at(j)
            seen = in_scene(j, start, end)
            for g in range(groups):
                to = group_at(g)
                s = matmul(k_ref[at, to], q_spread[g], 1, 1)
                p = jnp.where(seen, jnp.exp(s - lse[g]), 0.0)
                gv_sum[at, to] += matmul(p.astype(bf16), g_spread[g], 1, 0)
                gp = matmul(v_ref[at, to], g_spread[g], 1, 1)
                gs = (p * (gp - dots[g])).astype(bf16)
                gk_sum[at, to] += matmul(gs, q_spread[g], 1, 0)
                gqt_sum[g] += matmul(kt_ref[to, at], gs, 1, 0)
            return carry

        lax.fori_loop(first, last, step, 0)
        for g in range(groups):
            gq_ref[ray_rows, group_at(g)] = (fold_heads(gqt_sum[g].T) * HEAD ** (-0.5)).astype(bf16)
        return carry

    lax.fori_loop(0, used_tiles, one_tile, 0)


def middle_kernel(
    counts,
    lengths,
    q_ref,
    order_ref,
    rays_ref,
    cot_ref,
    rows_ref,
    k_hbm,
    kt_hbm,
    v_hbm,
    vt_hbm,
    wo_hbm,
    wu_hbm,
    wd_hbm,
    result_ref,
    gh_ref,
    gq_out,
    small_ref,
    early_hbm,
    go_hbm,
    gk_hbm,
    gv_hbm,
    k_ref,
    v_ref,
    turned_ref,
    wo_ref,
    wu_ref,
    wd_ref,
    gk_sum,
    gv_sum,
    square_ref,
    lse_ref,
    att_ref,
    gs_ref,
    gq_ref,
    active_ref,
    gpre_ref,
    gu_slot,
    gd_slot,
    go_slot,
    in_sem,
    out_sem,
    early_sem,
):
    used_tiles, bounds = scene_tiles(counts, lengths)
    loads = [
        pltpu.make_async_copy(source, target, in_sem.at[n])
        for n, (source, target) in enumerate(
            (
                (k_hbm, k_ref),
                (vt_hbm, turned_ref),
                (wo_hbm, wo_ref),
                (wu_hbm, wu_ref),
                (wd_hbm, wd_ref),
                (v_hbm, v_ref),
                (kt_hbm, turned_ref),
            )
        )
    ]
    for load in loads[:6]:
        load.start()
    loads[0].wait()
    loads[1].wait()
    attend(used_tiles, bounds, q_ref, k_ref, turned_ref, att_ref, lse_ref, gk_sum, square_ref)
    loads[6].start()

    order = order_ref[...]
    attended = matmul(order, att_ref[...].astype(bf16), 0, 0).astype(bf16)
    loads[2].wait()
    hidden = rays_ref[...].astype(f32) + matmul(attended, wo_ref[...], 1, 0) + rows_ref[0:1, :]
    hidden_low = hidden.astype(bf16)
    hidden_turned = hidden_low.T
    cot = cot_ref[...]
    width, inner = wu_ref.shape
    blocks = inner // WIDE
    per_half = blocks // 2
    loads[3].wait()
    loads[4].wait()

    def early_copies(n):
        half, part = n // per_half, n % per_half
        slot = n % 2
        return (
            pltpu.make_async_copy(
                gu_slot.at[slot], early_hbm.at[half, pl.ds(0, width), pl.ds(part * WIDE, WIDE)], early_sem.at[0, slot]
            ),
            pltpu.make_async_copy(
                gd_slot.at[slot], early_hbm.at[half, pl.ds(width + part * WIDE, WIDE)], early_sem.at[1, slot]
            ),
        )

    for n in range(blocks):
        at = slice(n * WIDE, (n + 1) * WIDE)
        bias_row, bias_at = 1 + n * WIDE // width, slice(n * WIDE % width, n * WIDE % width + WIDE)
        pre = matmul(hidden_low, wu_ref[:, at], 1, 0) + rows_ref[bias_row : bias_row + 1, bias_at]
        active, slope = gelu_both(pre)
        active = active.astype(bf16)
        active_ref[:, at] = active
        grad_pre = (matmul(cot, wd_ref[at, :], 1, 1) * slope).astype(bf16)
        gpre_ref[:, at] = grad_pre
        small_ref[bias_row : bias_row + 1, bias_at] = jnp.sum(grad_pre.astype(f32), axis=0, keepdims=True)
        if n >= 2:
            for copy in early_copies(n - 2):
                copy.wait()
        gu_slot[n % 2] = matmul(hidden_turned, grad_pre, 1, 0).astype(bf16)
        gd_slot[n % 2] = matmul(active, cot, 0, 0).astype(bf16)
        for copy in early_copies(n):
            copy.start()
    result_ref[...] = (hidden + matmul(active_ref[...], wd_ref[...], 1, 0) + rows_ref[3:4, :]).astype(bf16)
    grad_top = cot.astype(f32)
    small_ref[3:4, :] = jnp.sum(grad_top, axis=0, keepdims=True)
    grad_hidden = grad_top + matmul(gpre_ref[...], wu_ref[...], 1, 1)
    gh_ref[...] = grad_hidden
    grad_branch = grad_hidden.astype(bf16)
    small_ref[0:1, :] = jnp.sum(grad_branch.astype(f32), axis=0, keepdims=True)
    small_ref[4:8, :] = jnp.zeros((4, width), f32)
    go_slot[...] = matmul(attended, grad_branch, 0, 0).astype(bf16)
    go_copy = pltpu.make_async_copy(go_slot, go_hbm, out_sem.at[0])
    go_copy.start()
    grad_attended = matmul(grad_branch, wo_ref[...], 1, 1).astype(bf16)
    gs_ref[...] = matmul(order, grad_attended, 1, 0).astype(bf16)

    loads[5].wait()
    loads[6].wait()
    attend_back(
        used_tiles,
        bounds,
        q_ref,
        k_ref,
        turned_ref,
        v_ref,
        gs_ref,
        att_ref,
        lse_ref,
        gq_ref,
        gk_sum,
        gv_sum,
        square_ref,
    )
    k_ref[...] = gk_sum[...].astype(bf16)
    gk_copy = pltpu.make_async_copy(k_ref, gk_hbm, out_sem.at[1])
    gk_copy.start()
    v_ref[...] = gv_sum[...].astype(bf16)
    gv_copy = pltpu.make_async_copy(v_ref, gv_hbm, out_sem.at[2])
    gv_copy.start()
    gq_out[...] = matmul(order, gq_ref[...], 0, 0).astype(bf16)
    for copy in early_copies(blocks - 2) + early_copies(blocks - 1) + (go_copy, gk_copy, gv_copy):
        copy.wait()


def attend_and_mlp(counts, lengths, q_sorted, order, rays, cotangent, rows, keys, keys_t, values, values_t, w_out, w_up, w_down):
    slots, width = q_sorted.shape
    n_rays = rays.shape[0]
    inner = w_up.shape[1]
    total = keys.shape[0]
    vmem = pltpu.VMEM
    smem = pl.BlockSpec(memory_space=pltpu.SMEM)
    in_vmem = pl.BlockSpec(memory_space=vmem)
    anywhere = pl.BlockSpec(memory_space=pl.ANY)
    struct = jax.ShapeDtypeStruct
    return pl.pallas_call(
        middle_kernel,
        out_shape=(
            struct((n_rays, width), bf16),
            struct((n_rays, width), f32),
            struct((n_rays, width), bf16),
            struct((8, width), f32),
            struct((2, 2 * width, width), bf16),
            struct((width, width), bf16),
            struct((total, width), bf16),
            struct((total, width), bf16),
        ),
        in_specs=[smem] * 2 + [in_vmem] * 5 + [anywhere] * 7,
        out_specs=(in_vmem,) * 4 + (anywhere,) * 4,
        scratch_shapes=[
            vmem((total, width), bf16),
            vmem((total, width), bf16),
            vmem((width, total), bf16),
            vmem((width, width), bf16),
            vmem((width, inner), bf16),
            vmem((inner, width), bf16),
            vmem((total, width), f32),
            vmem((total, width), f32),
            vmem((width // WIDE, WIDE, WIDE), f32),
            vmem((slots // TILE, width), f32),
            vmem((slots, width), f32),
            vmem((slots, width), bf16),
            vmem((slots, width), bf16),
            vmem((n_rays, inner), bf16),
            vmem((n_rays, inner), bf16),
            vmem((2, width, WIDE), bf16),
            vmem((2, WIDE, width), bf16),
            vmem((width, width), bf16),
            pltpu.SemaphoreType.DMA((7,)),
            pltpu.SemaphoreType.DMA((3,)),
            pltpu.SemaphoreType.DMA((2, 2)),
        ],
        compiler_params=pltpu.CompilerParams(vmem_limit_bytes=62 << 20),
        name="attend_and_mlp",
    )(counts, lengths, q_sorted, order, rays, cotangent, rows, keys, keys_t, values, values_t, w_out, w_up, w_down)


MESH = pl.DeviceIdType.MESH
BLOCK = 256
SLOW = 4


def flip(index, bit):
    return index + bit * (1 - 2 * ((index // bit) % 2))


def bits_of(count):
    bits = []
    while count > 1:
        count //= 2
        bits.append(count)
    return bits


def lane_rows(start, size):
    return pl.ds(pl.multiple_of(start, 16), size)


class Place:
    def __init__(self, n_seq, n_ray):
        self.seq = lax.axis_index("seq")
        self.ray = lax.axis_index("ray")
        self.n_fast = n_ray // SLOW
        self.core = self.seq % 2
        self.slow = self.ray // self.n_fast
        self.fast = self.ray % self.n_fast
        self.x_bits = [("seq", 2 * b) for b in bits_of(n_seq // 2)]
        self.fast_bits = [("ray", b) for b in bits_of(self.n_fast)]
        self.slow_bits = [("ray", self.n_fast * b) for b in bits_of(SLOW)]
        self.spots = (self.slow, SLOW - 1 - self.slow)

    def across(self, axis, bit):
        if axis == "seq":
            return (flip(self.seq, bit), self.ray)
        return (self.seq, flip(self.ray, bit))

    def value(self, axis, bit):
        return ((self.seq if axis == "seq" else self.ray) // bit) % 2

    def along(self, way):
        return (self.seq, self.ray + (self.n_fast if way == 0 else -self.n_fast))

    def mirrored(self, way, chunk):
        return chunk if way == 0 else SLOW - 1 - chunk


def remote(src, dst, send_sem, recv_sem, device):
    return pltpu.make_async_remote_copy(
        src_ref=src,
        dst_ref=dst,
        send_sem=send_sem,
        recv_sem=recv_sem,
        device_id=device,
        device_id_type=MESH,
    )


def greet(place, exchanges):
    barrier = pltpu.get_barrier_semaphore()
    for axis, bit in exchanges:
        pl.semaphore_signal(barrier, inc=1, device_id=place.across(axis, bit), device_id_type=MESH)
    for step in (1, SLOW - 1):
        beside = (place.seq, (place.slow + step) % SLOW * place.n_fast + place.fast)
        pl.semaphore_signal(barrier, inc=1, device_id=beside, device_id_type=MESH)
    pl.semaphore_wait(barrier, len(exchanges) + 2)


class Line:
    def __init__(self, place, block, recv, send_sem, recv_sem):
        self.place, self.block, self.recv, self.send_sem, self.recv_sem = place, block, recv, send_sem, recv_sem

    def copy(self, way, t, to):
        chunk = self.place.mirrored(way, SLOW - 1 - (t - self.place.spots[way]))
        return remote(
            self.block(chunk), self.recv(way, t), self.send_sem(way, t), self.recv_sem(way, t), self.place.along(to)
        )

    def landed(self, way, t):
        remote(
            self.recv(way, t), self.recv(way, t), self.send_sem(way, t), self.recv_sem(way, t), self.place.along(1 - way)
        ).wait_recv()
        return self.recv(way, t)[...].astype(f32)

    def step(self, t):
        for way in range(2):
            spot = self.place.spots[way]

            @pl.when((spot <= t) & (spot < SLOW - 1))
            def _(way=way, spot=spot):
                if t > 0:

                    @pl.when(spot > 0)
                    def _():
                        block = self.block(self.place.mirrored(way, SLOW - 1 - (t - spot)))
                        block[...] = (block[...].astype(f32) + self.landed(way, t - 1)).astype(bf16)

                self.copy(way, t, way).start()

    def last(self, total):
        total[...] = self.block(self.place.slow)[...].astype(f32)
        for way in range(2):

            @pl.when(self.place.spots[way] > 0)
            def _(way=way):
                total[...] += self.landed(way, SLOW - 2)

    def drain(self):
        for way in range(2):
            for t in range(SLOW - 1):
                spot = self.place.spots[way]

                @pl.when((spot <= t) & (spot < SLOW - 1))
                def _(way=way, t=t):
                    self.copy(way, t, way).wait_send()


class Spread:
    def __init__(self, place, block, send_sem, recv_sem):
        self.place, self.block, self.send_sem, self.recv_sem = place, block, send_sem, recv_sem

    def copy(self, way, t, to):
        chunk = self.place.mirrored(way, self.place.spots[way] - t)
        block = self.block(chunk)
        return remote(block, block, self.send_sem(way, t), self.recv_sem(way, t), self.place.along(to))

    def step(self, t):
        for way in range(2):
            spot = self.place.spots[way]

            @pl.when(spot >= t)
            def _(way=way, spot=spot):
                if t > 0:
                    block = self.block(self.place.mirrored(way, spot - t))
                    remote(
                        block, block, self.send_sem(way, t - 1), self.recv_sem(way, t - 1), self.place.along(1 - way)
                    ).wait_recv()
                if t < SLOW - 1:

                    @pl.when(spot < SLOW - 1)
                    def _():
                        self.copy(way, t, way).start()

    def drain(self):
        for way in range(2):
            for t in range(SLOW - 1):
                spot = self.place.spots[way]

                @pl.when((spot >= t) & (spot < SLOW - 1))
                def _(way=way, t=t):
                    self.copy(way, t, way).wait_send()


def units_of(rows, n_x, n_fast):
    share = n_x * n_fast * SLOW * 16
    return rows // BLOCK if BLOCK % share == 0 else 1


def sum_kernel(
    n_seq,
    n_ray,
    units,
    lat_start,
    lat_beat,
    wq_ref,
    wk_ref,
    wv_ref,
    shifted_ref,
    gq_ref,
    rays_ref,
    gh_ref,
    rows_ref,
    small_ref,
    early_hbm,
    go_hbm,
    gk_hbm,
    gv_hbm,
    all_hbm,
    o_q,
    o_k,
    o_v,
    o_o,
    o_u,
    o_d,
    glat_ref,
    grays_ref,
    small_out,
    grads_kv,
    all_ref,
    go_gq,
    own,
    other,
    rc,
    rx,
    z_recv,
    z_total,
    full,
    lat,
    lat_recv,
    lz_recv,
    small_now,
    small_recv,
    load_sem,
    core_sem,
    halve_sem,
    z_sem,
    zg_sem,
    double_sem,
    back_sem,
    out_sem,
    lat_sem,
    lz_sem,
    small_sem,
):
    place = Place(n_seq, n_ray)
    core_pair = ("seq", 1)
    halvings = place.x_bits + place.fast_bits
    exchanges = [core_pair] + halvings + place.slow_bits
    core = place.core
    rows, width = own.shape
    late_from = rows // 2
    unit_rows = rows // units
    sizes = [unit_rows >> i for i in range(len(halvings) + 1)]
    share = sizes[-1]
    line = share % (16 * SLOW) == 0
    piece = share // SLOW if line else share

    loads = [
        pltpu.make_async_copy(source, target, load_sem.at[n])
        for n, (source, target) in enumerate(
            (
                (early_hbm.at[core], own.at[pl.ds(0, late_from)]),
                (go_hbm, go_gq.at[0]),
                (gk_hbm, grads_kv.at[0]),
                (gv_hbm, grads_kv.at[1]),
                (all_hbm, all_ref),
            )
        )
    ]
    for load in loads:
        load.start()
    greet(place, exchanges)

    def base(u, stages):
        start = u * unit_rows
        for i in range(stages):
            start = start + place.value(*halvings[i]) * sizes[i + 1]
        return start

    def unit(u):
        return lane_rows(u * unit_rows, unit_rows)

    def core_parts(u):
        if units == 1:
            rows_of = (pl.ds(0, late_from), pl.ds(0, late_from))
            when = (u == 0, u == 0)
            into = (pl.ds(0, late_from), pl.ds(late_from, late_from))
        else:
            rows_of = (unit(u), lane_rows(u * unit_rows - late_from, unit_rows))
            when = (u < units // 2, u >= units // 2)
            into = (unit(u), unit(u))
        sources = (early_hbm.at[1 - core, rows_of[0]], other.at[rows_of[1]])
        return [
            (
                when[n],
                remote(
                    sources[n], rc.at[into[n]], core_sem.at[0, n, u], core_sem.at[1, n, u], place.across(*core_pair)
                ),
            )
            for n in range(2)
        ]

    def halve_copy(i, u):
        size = sizes[i + 1]
        sent = base(u, i) + (1 - place.value(*halvings[i])) * size
        return remote(
            own.at[lane_rows(sent, size)],
            rx[i].at[lane_rows(u * size, size)],
            halve_sem.at[0, i, u],
            halve_sem.at[1, i, u],
            place.across(*halvings[i]),
        )

    def start_core(u):
        for when, copy in core_parts(u):

            @pl.when(when)
            def _(copy=copy):
                copy.start()

    def join_core(u):
        for when, copy in core_parts(u):

            @pl.when(when)
            def _(copy=copy):
                copy.wait()

        own[unit(u), :] = (own[unit(u), :].astype(f32) + rc[unit(u), :].astype(f32)).astype(bf16)
        halve_copy(0, u).start()

    def join_half(i):
        def run(u):
            size = sizes[i + 1]
            halve_copy(i, u).wait()
            kept = lane_rows(base(u, i + 1), size)
            own[kept, :] = (own[kept, :].astype(f32) + rx[i][lane_rows(u * size, size), :].astype(f32)).astype(bf16)
            if i + 1 < len(halvings):
                halve_copy(i + 1, u).start()

        return run

    def z_rows(u, chunk):
        return lane_rows(base(u, len(halvings)) + chunk * piece, piece)

    def z_line(u):
        return Line(
            place,
            lambda chunk: own.at[z_rows(u, chunk)],
            lambda way, t: z_recv.at[u, way, t],
            lambda way, t: z_sem.at[0, u, way, t],
            lambda way, t: z_sem.at[1, u, way, t],
        )

    def z_spread(u):
        return Spread(
            place,
            lambda chunk: full.at[z_rows(u, chunk)],
            lambda way, t: zg_sem.at[0, u, way, t],
            lambda way, t: zg_sem.at[1, u, way, t],
        )

    def z_step(t):
        return lambda u: z_line(u).step(t)

    def z_finish(u):
        z_line(u).last(z_total)
        full[z_rows(u, place.slow), :] = z_total[...].astype(bf16)
        z_spread(u).step(0)

    def spread_step(t):
        return lambda u: z_spread(u).step(t)

    def whole_copy(i, u):
        return remote(
            own.at[lane_rows(base(u, len(halvings)), share)],
            z_recv.at[u, 0, i],
            z_sem.at[0, u, 0, i],
            z_sem.at[1, u, 0, i],
            place.across(*place.slow_bits[i]),
        )

    def whole_step(i):
        def run(u):
            mine = lane_rows(base(u, len(halvings)), share)
            if i > 0:
                whole_copy(i - 1, u).wait()
                own[mine, :] = (own[mine, :].astype(f32) + z_recv[u, 0, i - 1].astype(f32)).astype(bf16)
            if i < len(place.slow_bits):
                whole_copy(i, u).start()
            else:
                full[mine, :] = own[mine, :]

        return run

    def double_copy(i, u):
        block = full.at[lane_rows(base(u, i + 1), sizes[i + 1])]
        return remote(block, block, double_sem.at[0, i, u], double_sem.at[1, i, u], place.across(*halvings[i]))

    def targets(n, c):
        per = width // BLOCK
        part, at = n // per, n % per
        rows_at = pl.ds(pl.multiple_of(at * BLOCK, BLOCK), BLOCK)
        half_at = pl.ds(pl.multiple_of(c * width, 128), width)
        lower = pl.ds(pl.multiple_of(c * width + at * BLOCK, BLOCK), BLOCK)
        even = (at + c) % 2 == 0
        return [
            (part == 0, o_u.at[rows_at, half_at]),
            (part == 1, o_d.at[lower]),
            ((part == 2) & even, o_o.at[rows_at]),
            ((part == 2) & ((at + c) % 2 == 1), o_q.at[rows_at]),
            ((part == 3) & (c == 0), o_k.at[rows_at]),
            ((part == 3) & (c == 1), o_v.at[rows_at]),
        ]

    def block_rows(n):
        return lane_rows(n * BLOCK, BLOCK)

    def blocks_of(u):
        return [u] if units > 1 else list(range(rows // BLOCK))

    def send_block(n):
        for when, target in targets(n, core):

            @pl.when(when)
            def _(target=target):
                source = full.at[block_rows(n)]
                remote(source, target, back_sem.at[0, n], back_sem.at[1, n], place.across(*core_pair)).start()
                pltpu.make_async_copy(source, target, out_sem.at[n]).start()

    def end_block(n):
        for when, target in targets(n, core):

            @pl.when(when)
            def _(target=target):
                source = full.at[block_rows(n)]
                remote(source, target, back_sem.at[0, n], back_sem.at[1, n], place.across(*core_pair)).wait_send()
                pltpu.make_async_copy(source, target, out_sem.at[n]).wait()

        for when, target in targets(n, 1 - core):

            @pl.when(when)
            def _(target=target):
                source = full.at[block_rows(n)]
                remote(source, target, back_sem.at[0, n], back_sem.at[1, n], place.across(*core_pair)).wait_recv()

    def start_double(u):
        double_copy(len(halvings) - 1, u).start()

    def join_double(i):
        def run(u):
            double_copy(i, u).wait()
            if i > 0:
                double_copy(i - 1, u).start()
            else:
                for n in blocks_of(u):
                    send_block(n)

        return run

    def finish_unit(u):
        for n in blocks_of(u):
            end_block(n)
        if line:
            z_line(u).drain()
            z_spread(u).drain()

    stages = [[start_core], [join_core], []] + [[join_half(i)] for i in range(len(halvings))]
    if line:
        stages[-1].append(z_step(0))
        stages += [[z_step(t)] for t in range(1, SLOW - 1)]
        stages += [[z_finish]] + [[spread_step(t)] for t in range(1, SLOW)]
    else:
        stages[-1].append(whole_step(0))
        stages += [[whole_step(i)] for i in range(1, len(place.slow_bits) + 1)]
    stages[-1].append(start_double)
    stages += [[join_double(i)] for i in reversed(range(len(halvings)))]
    stages += [[], [finish_unit]]

    n_fast, block = lat.shape[1:3]
    group = n_fast * block
    half_rows = block // 2
    fast_sizes = [n_fast >> i for i in range(len(place.fast_bits) + 1)]

    def chunk_of(k):
        near = jnp.minimum(place.slow, SLOW - 1 - place.slow)
        ahead = SLOW - 1 - near
        chunk = jnp.where(k < ahead, SLOW - 1 - k, jnp.where(k - ahead < near, k - ahead, near))
        return jnp.where(place.slow == near, chunk, SLOW - 1 - chunk)

    def lat_base(stages):
        start = 0
        for i in range(stages):
            start = start + place.value(*place.fast_bits[i]) * fast_sizes[i + 1]
        return start

    def lat_half(m):
        return lane_rows((m % 2) * half_rows, half_rows)

    def lat_copy(i, m):
        size = fast_sizes[i + 1]
        sent = lat_base(i) + (1 - place.value(*place.fast_bits[i])) * size
        return remote(
            lat.at[chunk_of(m // 2), pl.ds(sent, size), lat_half(m)],
            lat_recv[i].at[m],
            lat_sem.at[0, i, m],
            lat_sem.at[1, i, m],
            place.across(*place.fast_bits[i]),
        )

    def start_lat(m):
        lat_copy(0, m).start()

    def lat_line(m):
        half = m % 2
        return Line(
            place,
            lambda chunk: lat.at[chunk, place.fast, lat_half(m)],
            lambda way, t: lz_recv.at[half, way, t],
            lambda way, t: lz_sem.at[0, half, way, t],
            lambda way, t: lz_sem.at[1, half, way, t],
        )

    def join_lat(i):
        def run(m):
            lat_copy(i, m).wait()
            kept = lat.at[chunk_of(m // 2), pl.ds(lat_base(i + 1), fast_sizes[i + 1]), lat_half(m)]
            kept[...] = (kept[...].astype(f32) + lat_recv[i][m].astype(f32)).astype(bf16)
            if i + 1 < len(place.fast_bits):
                lat_copy(i + 1, m).start()
            else:
                for t in range(SLOW - 1):

                    @pl.when(m // 2 == t)
                    def _(t=t):
                        lat_line(m).step(t)

        return run

    def finish_lat(m):
        @pl.when(m // 2 == SLOW - 1)
        def _():
            lat_line(m).last(glat_ref.at[lat_half(m)])
            lat_line(m).drain()

    lat_stages = [start_lat] + [join_lat(i) for i in range(len(place.fast_bits))] + [finish_lat]
    lat_steps = 2 * SLOW

    def small_copy(i):
        axis, bit = exchanges[i]
        return remote(
            small_now.at[i], small_recv.at[i], small_sem.at[0, i], small_sem.at[1, i], place.across(axis, bit)
        )

    def start_small():
        small_copy(0).start()

    def join_small(i):
        def run():
            small_copy(i).wait()
            small_now[i + 1] = small_now[i] + small_recv[i]
            if i + 1 < len(exchanges):
                small_copy(i + 1).start()

        return run

    def query_terms():
        loads[1].wait()
        go_gq[1] = matmul(shifted_ref[...], gq_ref[...], 0, 0).astype(bf16)
        for b in range(width // BLOCK):
            at = slice(b * BLOCK, (b + 1) * BLOCK)
            own[slice(late_from + at.start, late_from + at.stop), :] = go_gq[(b + core) % 2, at, :]
            other[at, :] = go_gq[(b + 1 - core) % 2, at, :]

    def ray_terms():
        inputs = rays_ref[...].astype(f32)
        centred = inputs - jnp.mean(inputs, axis=1, keepdims=True)
        inverse = lax.rsqrt(jnp.mean(centred * centred, axis=1, keepdims=True) + 1e-05)
        normed = centred * inverse
        grad_shifted = matmul(gq_ref[...], wq_ref[...], 1, 1)
        grad_normed = grad_shifted * rows_ref[0:1, :]
        grays_ref[...] = gh_ref[...] + inverse * (
            grad_normed
            - jnp.mean(grad_normed, axis=1, keepdims=True)
            - normed * jnp.mean(grad_normed * normed, axis=1, keepdims=True)
        )
        small_now[0] = small_ref[...]
        small_now[0, 4:5] = jnp.sum(grad_shifted * normed, axis=0, keepdims=True)
        small_now[0, 5:6] = jnp.sum(grad_shifted, axis=0, keepdims=True)
        small_now[0, 6:7] = jnp.sum(gq_ref[...].astype(f32), axis=0, keepdims=True)

    def lat_terms(k):
        def run():
            if k == 0:
                loads[2].wait()
                loads[3].wait()
            at = lane_rows(chunk_of(k) * group, group)
            total = matmul(grads_kv[0, at, :], wk_ref[...], 1, 1) + matmul(grads_kv[1, at, :], wv_ref[...], 1, 1)
            lat[chunk_of(k)] = total.astype(bf16).reshape(n_fast, block, width)

        return run

    def own_key_terms():
        loads[4].wait()
        own[late_from + width :, :] = matmul(all_ref[...], grads_kv[core], 1, 0).astype(bf16)

    def other_key_terms():
        other[width:, :] = matmul(all_ref[...], grads_kv[1 - core], 1, 0).astype(bf16)
        small_now[0, 7:8] = jnp.sum(grads_kv[1].astype(f32), axis=0, keepdims=True)

    work = {6 + 2 * i: [join_small(i)] for i in range(len(exchanges))}
    terms = [query_terms, ray_terms, lat_terms(0), own_key_terms, other_key_terms]
    late_lat = [lat_terms(k) for k in range(1, SLOW)]
    if units == 1:
        work[-1] = terms + late_lat + [start_small]
    else:
        for beat, run in enumerate(terms):
            work.setdefault(beat, []).append(run)
        work[len(terms) - 1].append(start_small)
        for k, run in enumerate(late_lat):
            work.setdefault(min(6 + 2 * k, lat_start + 2 * (k + 1) * lat_beat), []).append(run)
    lat_span = lat_start + lat_beat * (lat_steps - 1 + len(lat_stages) - 1) + 1
    beats = max(units + len(stages) - 1, lat_span, max(work) + 1)
    loads[0].wait()
    for run in work.pop(-1, []):
        run()

    def one_beat(now, carry):
        for s in range(len(stages)):
            u = now - s

            @pl.when((u >= 0) & (u < units))
            def _(u=u, s=s):
                for run in stages[s]:
                    run(u)

        for beat, runs in work.items():

            @pl.when(now == beat)
            def _(runs=runs):
                for run in runs:
                    run()

        for s in range(len(lat_stages)):
            ahead = now - lat_start - lat_beat * s
            m = ahead // lat_beat

            @pl.when((ahead >= 0) & (ahead % lat_beat == 0) & (m < lat_steps))
            def _(m=m, s=s):
                lat_stages[s](m)

        return carry

    lax.fori_loop(0, beats, one_beat, 0)
    small_out[...] = small_now[len(exchanges)]


def back_and_sum(n_seq, n_ray, block, w_query, w_key, w_value, shifted, gq, rays, gh, rows, small, early, go, gk, gv, all_t):
    n_fast = n_ray // SLOW
    n_x = n_seq // 2
    width = w_query.shape[0]
    sum_rows = 2 * early.shape[1]
    total = gk.shape[0]
    units = units_of(sum_rows, n_x, n_fast)
    halvings = len(bits_of(n_x)) + len(bits_of(n_fast))
    fast_bits = len(bits_of(n_fast))
    exchanges = 1 + halvings + len(bits_of(SLOW))
    share = sum_rows // units >> halvings
    piece = share // SLOW if share % (16 * SLOW) == 0 else share
    half = block // 2
    vmem = pltpu.VMEM
    sem = pltpu.SemaphoreType.DMA
    struct = jax.ShapeDtypeStruct
    in_vmem = pl.BlockSpec(memory_space=vmem)
    anywhere = pl.BlockSpec(memory_space=pl.ANY)
    return pl.pallas_call(
        functools.partial(sum_kernel, n_seq, n_ray, units, 2, 3),
        out_shape=(
            struct((width, width), bf16),
            struct((width, width), bf16),
            struct((width, width), bf16),
            struct((width, width), bf16),
            struct((width, 2 * width), bf16),
            struct((2 * width, width), bf16),
            struct((block, width), f32),
            struct(rays.shape, f32),
            struct(small.shape, f32),
        ),
        in_specs=[in_vmem] * 9 + [anywhere] * 5,
        out_specs=(anywhere,) * 6 + (in_vmem,) * 3,
        scratch_shapes=[
            vmem((2, total, width), bf16),
            vmem((width, total), bf16),
            vmem((2, width, width), bf16),
            vmem((sum_rows, width), bf16),
            vmem((sum_rows // 2, width), bf16),
            vmem((sum_rows, width), bf16),
            [vmem((sum_rows >> (i + 1), width), bf16) for i in range(halvings)],
            vmem((units, 2, SLOW - 1, piece, width), bf16),
            vmem((piece, width), f32),
            vmem((sum_rows, width), bf16),
            vmem((SLOW, n_fast, block, width), bf16),
            [vmem((2 * SLOW, n_fast >> (i + 1), half, width), bf16) for i in range(fast_bits)],
            vmem((2, 2, SLOW - 1, half, width), bf16),
            vmem((exchanges + 1,) + small.shape, f32),
            vmem((exchanges,) + small.shape, f32),
            sem((5,)),
            sem((2, 2, units)),
            sem((2, halvings, units)),
            sem((2, units, 2, SLOW - 1)),
            sem((2, units, 2, SLOW - 1)),
            sem((2, halvings, units)),
            sem((2, sum_rows // BLOCK)),
            sem((sum_rows // BLOCK,)),
            sem((2, fast_bits, 2 * SLOW)),
            sem((2, 2, 2, SLOW - 1)),
            sem((2, exchanges)),
        ],
        compiler_params=pltpu.CompilerParams(collective_id=1, has_side_effects=True, vmem_limit_bytes=62 << 20),
        name="back_and_sum",
    )(w_query, w_key, w_value, shifted, gq, rays, gh, rows, small, early, go, gk, gv, all_t)


def gather_kernel(
    n_seq,
    n_ray,
    kinds,
    rays_ref,
    lat_ref,
    scenes_ref,
    rows_ref,
    wq_ref,
    wk_ref,
    wv_ref,
    all_ref,
    k_ref,
    kt_ref,
    v_ref,
    vt_ref,
    qs_ref,
    order_ref,
    shifted_ref,
    counts_ref,
    full,
    all_own,
    k_own,
    kt_own,
    v_own,
    vt_own,
    z_sem,
    y_sem,
    out_sem,
):
    place = Place(n_seq, n_ray)
    fast_bits = place.fast_bits[::-1]
    greet(place, place.fast_bits)
    block, width = lat_ref.shape
    half_rows = block // 2
    group = place.n_fast * block
    full[place.slow, place.fast] = lat_ref[...]

    def half_at(half):
        return pl.ds(half * half_rows, half_rows)

    def spread(half):
        return Spread(
            place,
            lambda chunk: full.at[chunk, place.fast, half_at(half)],
            lambda way, t: z_sem.at[0, half, way, t],
            lambda way, t: z_sem.at[1, half, way, t],
        )

    def fast_copy(i, chunk, half):
        axis, bit = fast_bits[i]
        mine = full.at[chunk, pl.ds(place.fast // bit * bit, bit), half_at(half)]
        return remote(mine, mine, y_sem.at[0, i, chunk, half], y_sem.at[1, i, chunk, half], place.across(axis, bit))

    def chunk_of(way, t):
        return place.mirrored(way, place.spots[way] - t)

    for half in range(2):
        fast_copy(0, place.slow, half).start()
        spread(half).step(0)

    inputs = rays_ref[...].astype(f32)
    centred = inputs - jnp.mean(inputs, axis=1, keepdims=True)
    inverse = lax.rsqrt(jnp.mean(centred * centred, axis=1, keepdims=True) + 1e-05)
    shifted = (centred * inverse * rows_ref[0:1, :] + rows_ref[1:2, :]).astype(bf16)
    shifted_ref[...] = shifted
    queries = (matmul(shifted, wq_ref[...], 1, 0) + rows_ref[2:3, :]).astype(bf16)
    n_rays = rays_ref.shape[0]
    slots = order_ref.shape[0]
    scenes = scenes_ref[...]
    same = scenes == lax.broadcasted_iota(jnp.int32, (8, n_rays), 0)
    one_hot = same.astype(f32)
    before = (
        lax.broadcasted_iota(jnp.int32, (n_rays, n_rays), 0) < lax.broadcasted_iota(jnp.int32, (n_rays, n_rays), 1)
    ).astype(bf16)
    rank = matmul(one_hot.astype(bf16), before, 1, 0)
    counts = jnp.sum(one_hot, axis=1, keepdims=True)
    counts_ref[...] = jnp.broadcast_to(counts, counts_ref.shape).astype(jnp.int32)
    scene_tiles = jnp.floor((counts + (TILE - 1)) * (1.0 / TILE))
    slot = jnp.zeros((1, n_rays), f32)
    first = jnp.zeros((1, 1), f32)
    for c in range(kinds):
        slot = slot + jnp.where(same[c : c + 1, :], rank[c : c + 1, :] + first, 0.0)
        first = first + scene_tiles[c : c + 1, :] * TILE
    order = (lax.broadcasted_iota(jnp.int32, (slots, n_rays), 0) == slot.astype(jnp.int32)).astype(f32).astype(bf16)
    order_ref[...] = order
    qs_ref[...] = (matmul(order, queries, 1, 0) * HEAD ** (-0.5)).astype(bf16)

    def results(chunk):
        rows = pl.ds(pl.multiple_of(chunk * group, 16), group)
        columns = pl.ds(pl.multiple_of(chunk * group, 128), group)
        return [
            (k_own.at[chunk], k_ref.at[rows]),
            (kt_own.at[chunk], kt_ref.at[:, columns]),
            (v_own.at[chunk], v_ref.at[rows]),
            (vt_own.at[chunk], vt_ref.at[:, columns]),
            (all_own.at[chunk], all_ref.at[:, columns]),
        ]

    def project(chunk):
        for half in range(2):
            for i in range(len(fast_bits)):
                fast_copy(i, chunk, half).wait()
                if i + 1 < len(fast_bits):
                    fast_copy(i + 1, chunk, half).start()
        latents = full[chunk].reshape(group, width)
        keys = matmul(latents, wk_ref[...], 1, 0).astype(bf16)
        k_own[chunk] = keys
        all_own[chunk] = latents.T
        kt_own[chunk] = keys.T
        values = (matmul(latents, wv_ref[...], 1, 0) + rows_ref[3:4, :]).astype(bf16)
        v_own[chunk] = values
        vt_own[chunk] = values.T
        for n, (source, target) in enumerate(results(chunk)):
            pltpu.make_async_copy(source, target, out_sem.at[n, chunk]).start()

    def visit(index, carry):
        t, way = index // 2, index % 2
        for later in range(1, SLOW):

            @pl.when(index == 2 * (later - 1))
            def _(later=later):
                for half in range(2):
                    spread(half).step(later)
                    for to in range(2):

                        @pl.when(place.spots[to] >= later)
                        def _(half=half, to=to):
                            fast_copy(0, chunk_of(to, later), half).start()

        spot = jnp.where(way == 0, place.slow, SLOW - 1 - place.slow)
        chunk = jnp.where(way == 0, spot - t, SLOW - 1 - spot + t)

        @pl.when((spot >= t) & (index != 1))
        def _():
            project(chunk)

        return carry

    lax.fori_loop(0, 2 * SLOW, visit, 0)

    def end(chunk, carry):
        for n, (source, target) in enumerate(results(chunk)):
            pltpu.make_async_copy(source, target, out_sem.at[n, chunk]).wait()
        return carry

    lax.fori_loop(0, SLOW, end, 0)
    for half in range(2):
        spread(half).drain()


def gather_and_project(n_seq, n_ray, kinds, rays, latents, scenes, rows, w_query, w_key, w_value):
    block, width = latents.shape
    n_rays = rays.shape[0]
    n_fast = n_ray // SLOW
    group = n_fast * block
    total = n_ray * block
    tiles = n_rays // TILE + kinds - 1
    fast_bits = len(bits_of(n_fast))
    vmem = pltpu.VMEM
    sem = pltpu.SemaphoreType.DMA
    in_vmem = pl.BlockSpec(memory_space=vmem)
    anywhere = pl.BlockSpec(memory_space=pl.ANY)
    tall = jax.ShapeDtypeStruct((total, width), bf16)
    wide = jax.ShapeDtypeStruct((width, total), bf16)
    return pl.pallas_call(
        functools.partial(gather_kernel, n_seq, n_ray, kinds),
        out_shape=(
            wide,
            tall,
            wide,
            tall,
            wide,
            jax.ShapeDtypeStruct((tiles * TILE, width), bf16),
            jax.ShapeDtypeStruct((tiles * TILE, n_rays), bf16),
            jax.ShapeDtypeStruct((n_rays, width), bf16),
            jax.ShapeDtypeStruct((8, 128), jnp.int32),
        ),
        in_specs=[in_vmem] * 7,
        out_specs=(anywhere,) * 5 + (in_vmem,) * 4,
        scratch_shapes=[
            vmem((SLOW, n_fast, block, width), bf16),
            vmem((SLOW, width, group), bf16),
            vmem((SLOW, group, width), bf16),
            vmem((SLOW, width, group), bf16),
            vmem((SLOW, group, width), bf16),
            vmem((SLOW, width, group), bf16),
            sem((2, 2, 2, SLOW - 1)),
            sem((2, fast_bits, SLOW, 2)),
            sem((5, SLOW)),
        ],
        compiler_params=pltpu.CompilerParams(collective_id=0, has_side_effects=True, vmem_limit_bytes=48 << 20),
        name="gather_and_project",
    )(rays, latents, scenes, rows, w_query, w_key, w_value)


def local(
    rays,
    latents,
    lengths,
    scenes,
    ln_gain,
    ln_bias,
    w_query,
    b_query,
    w_key,
    w_value,
    b_value,
    w_out,
    b_out,
    w_up,
    b_up,
    w_down,
    b_down,
    cotangent,
):
    width = rays.shape[1]
    n_seq, n_ray = lax.axis_size("seq"), lax.axis_size("ray")
    rows = jnp.concatenate([v.reshape(1, width) for v in (ln_gain, ln_bias, b_query, b_value)] * 2).astype(f32)
    all_t, keys, keys_t, values, values_t, q_sorted, order, shifted, counts = gather_and_project(
        n_seq,
        n_ray,
        lengths.shape[1],
        rays,
        latents,
        scenes.reshape(1, -1),
        rows,
        w_query,
        w_key,
        w_value,
    )
    result, grad_hidden, grad_queries, small, early, grad_w_out, grad_keys, grad_values = attend_and_mlp(
        counts,
        lengths,
        q_sorted,
        order,
        rays,
        cotangent,
        jnp.concatenate([b_out.reshape(1, width), b_up.reshape(2, width), b_down.reshape(1, width)] * 2).astype(f32),
        keys,
        keys_t,
        values,
        values_t,
        w_out,
        w_up,
        w_down,
    )

    sum_q, sum_k, sum_v, sum_o, sum_u, sum_d, grad_latents, grad_rays, vectors = back_and_sum(
        n_seq,
        n_ray,
        latents.shape[0],
        w_query,
        w_key,
        w_value,
        shifted,
        grad_queries,
        rays,
        grad_hidden,
        rows,
        small,
        early,
        grad_w_out,
        grad_keys,
        grad_values,
        all_t,
    )
    return (
        result,
        grad_rays,
        grad_latents,
        vectors[4],
        vectors[5],
        sum_q.astype(f32),
        vectors[6],
        sum_k.astype(f32),
        sum_v.astype(f32),
        vectors[7],
        sum_o.astype(f32),
        vectors[0],
        sum_u.astype(f32),
        vectors[1:3].reshape(-1),
        sum_d.astype(f32),
        vectors[3],
    )


def solution(mesh):
    whole = P(("seq", "ray"), None)
    in_specs = (whole, whole, P("seq", None), P(("seq", "ray"))) + (P(),) * 13 + (whole,)
    out_specs = (whole,) * 3 + (P(),) * 13
    return jax.shard_map(local, mesh=mesh, in_specs=in_specs, out_specs=out_specs, check_vma=False)
```

```python
import functools
import math

import jax
import jax.numpy as jnp
from jax import lax
from jax.experimental import pallas as pl
from jax.experimental.pallas import tpu as pltpu
from jax.sharding import PartitionSpec as P

HEADS = 12
HEAD = 64
TILE = 64
WIDE = 256
PACK = WIDE // HEAD
EARLY_WAIT = 2
LATE_CORE, LATE_X, LATE_STEP = 1, 2, 1
LAT_WAIT = 3
PAIR = 2
STEP = 384

masked_score = -1e30
f32 = jnp.float32
bf16 = jnp.bfloat16


def matmul(first_arg, second_arg, first_dim, second_dim):
    return lax.dot_general(
        first_arg,
        second_arg,
        (((first_dim,), (second_dim,)), ((), ())),
        preferred_element_type=jnp.float32,
    )


def own_block():
    row = lax.broadcasted_iota(jnp.int32, (WIDE, WIDE), 0) // TILE
    column = lax.broadcasted_iota(jnp.int32, (WIDE, WIDE), 1) // HEAD
    return row == column


def spread_heads(tile):
    return jnp.where(own_block(), jnp.concatenate([tile] * PACK, axis=0), jnp.zeros((), tile.dtype))


def fold_heads(turned):
    kept = jnp.where(own_block(), turned, 0.0)
    folded = (kept[:, : WIDE // 2] + kept[:, WIDE // 2 :]).T
    return folded[:TILE, :] + folded[TILE:, :]


def fold_rows(block, combine):
    return combine(block.reshape(block.shape[0] // 8, 8, block.shape[1]), axis=0)


def group_at(g):
    return slice(g * WIDE, (g + 1) * WIDE)


def segments(lengths, first, count):
    at = lax.broadcasted_iota(jnp.int32, (count, WIDE), 0) + first
    end, scene = 0, jnp.zeros((count, WIDE), f32)
    for c in range(lengths.shape[1] - 1):
        end = end + lengths[0, c]
        scene = scene + (at >= end).astype(f32)
    return scene


def gelu_both(pre):
    half = 0.5 * (1.0 + lax.erf(pre * math.sqrt(0.5)))
    return pre * half, half + pre * jnp.exp(-0.5 * pre * pre) * (1.0 / math.sqrt(2.0 * math.pi))


def mlp_kernel(
    att_ref,
    rays_ref,
    cot_ref,
    rows_ref,
    wo_ref,
    wu_ref,
    wd_ref,
    result_ref,
    gh_ref,
    ga_ref,
    dots_ref,
    small_ref,
    early_hbm,
    rest_ref,
    active_ref,
    gpre_ref,
    gu_slot,
    gd_slot,
    go_slot,
    early_sem,
    go_sem,
):
    attended = att_ref[...].astype(bf16)
    hidden = rays_ref[...].astype(f32) + matmul(attended, wo_ref[...], 1, 0) + rows_ref[4:5, :]
    hidden_low = hidden.astype(bf16)
    hidden_turned = hidden_low.T
    cot = cot_ref[...]
    width, inner = wu_ref.shape
    blocks = inner // WIDE
    per_half = blocks // 2

    def early_copies(n):
        half, part = n // per_half, n % per_half
        slot = n % 2
        return (
            pltpu.make_async_copy(
                gu_slot.at[slot], early_hbm.at[half, pl.ds(0, width), pl.ds(part * WIDE, WIDE)], early_sem.at[0, slot]
            ),
            pltpu.make_async_copy(
                gd_slot.at[slot], early_hbm.at[half, pl.ds(width + part * WIDE, WIDE)], early_sem.at[1, slot]
            ),
        )

    for n in range(blocks):
        at = slice(n * WIDE, (n + 1) * WIDE)
        bias_row, bias_at = 5 + n * WIDE // width, slice(n * WIDE % width, n * WIDE % width + WIDE)
        pre = matmul(hidden_low, wu_ref[:, at], 1, 0) + rows_ref[bias_row : bias_row + 1, bias_at]
        active, slope = gelu_both(pre)
        active = active.astype(bf16)
        active_ref[:, at] = active
        grad_pre = (matmul(cot, wd_ref[at, :], 1, 1) * slope).astype(bf16)
        gpre_ref[:, at] = grad_pre
        small_ref[bias_row - 4 : bias_row - 3, bias_at] = jnp.sum(grad_pre.astype(f32), axis=0, keepdims=True)
        if n >= 2:
            for copy in early_copies(n - 2):
                copy.wait()
        gu_slot[n % 2] = matmul(hidden_turned, grad_pre, 1, 0).astype(bf16)
        gd_slot[n % 2] = matmul(active, cot, 0, 0).astype(bf16)
        for copy in early_copies(n):
            copy.start()
    result_ref[...] = (hidden + matmul(active_ref[...], wd_ref[...], 1, 0) + rows_ref[7:8, :]).astype(bf16)
    grad_top = cot.astype(f32)
    small_ref[3:4, :] = jnp.sum(grad_top, axis=0, keepdims=True)
    grad_hidden = grad_top + matmul(gpre_ref[...], wu_ref[...], 1, 1)
    gh_ref[...] = grad_hidden
    grad_branch = grad_hidden.astype(bf16)
    small_ref[0:1, :] = jnp.sum(grad_branch.astype(f32), axis=0, keepdims=True)
    small_ref[4:8, :] = jnp.zeros((4, width), f32)
    grad_out = matmul(attended, grad_branch, 0, 0).astype(bf16)
    go_slot[...] = grad_out[: 2 * BLOCK]
    go_copies = [
        pltpu.make_async_copy(
            go_slot.at[pl.ds(c * BLOCK, BLOCK)], early_hbm.at[c, pl.ds(2 * width, BLOCK)], go_sem.at[c]
        )
        for c in range(2)
    ]
    for copy in go_copies:
        copy.start()
    rest_ref[...] = grad_out[2 * BLOCK :]
    grad_attended = matmul(grad_branch, wo_ref[...], 1, 1).astype(bf16)
    ga_ref[...] = grad_attended
    product = grad_attended.astype(f32) * att_ref[...]
    for t in range(dots_ref.shape[0]):
        for g in range(width // WIDE):
            dots_ref[t : t + 1, group_at(g)] = lax.dot_general(
                jnp.ones((8, WIDE), f32),
                spread_heads(product[t * TILE : (t + 1) * TILE, group_at(g)]),
                (((1,), (1,)), ((), ())),
                precision=lax.Precision.HIGHEST,
                preferred_element_type=f32,
            )[0:1, :]
    for copy in early_copies(blocks - 2) + early_copies(blocks - 1) + tuple(go_copies):
        copy.wait()


def mlp(attended, rays, cotangent, rows, w_out, w_up, w_down):
    n_rays, width = rays.shape
    inner = w_up.shape[1]
    vmem = pltpu.VMEM
    in_vmem = pl.BlockSpec(memory_space=vmem)
    struct = jax.ShapeDtypeStruct
    return pl.pallas_call(
        mlp_kernel,
        out_shape=(
            struct((n_rays, width), bf16),
            struct((n_rays, width), f32),
            struct((n_rays, width), bf16),
            struct((n_rays // TILE, width), f32),
            struct((8, width), f32),
            struct((2, 2 * width + BLOCK, width), bf16),
            struct((width - 2 * BLOCK, width), bf16),
        ),
        in_specs=[in_vmem] * 7,
        out_specs=(in_vmem,) * 5 + (pl.BlockSpec(memory_space=pl.ANY), in_vmem),
        scratch_shapes=[
            vmem((n_rays, inner), bf16),
            vmem((n_rays, inner), bf16),
            vmem((2, width, WIDE), bf16),
            vmem((2, WIDE, width), bf16),
            vmem((2 * BLOCK, width), bf16),
            pltpu.SemaphoreType.DMA((2, 2)),
            pltpu.SemaphoreType.DMA((2,)),
        ],
        compiler_params=pltpu.CompilerParams(vmem_limit_bytes=40 << 20),
        name="mlp",
    )(attended, rays, cotangent, rows, w_out, w_up, w_down)


MESH = pl.DeviceIdType.MESH
BLOCK = 256
SLOW = 4


def flip(index, bit):
    return index + bit * (1 - 2 * ((index // bit) % 2))


def bits_of(count):
    bits = []
    while count > 1:
        count //= 2
        bits.append(count)
    return bits


def lane_rows(start, size):
    return pl.ds(pl.multiple_of(start, 16), size)


class Place:
    def __init__(self, n_seq, n_ray):
        self.seq = lax.axis_index("seq")
        self.ray = lax.axis_index("ray")
        self.n_fast = n_ray // SLOW
        self.core = self.seq % 2
        self.slow = self.ray // self.n_fast
        self.fast = self.ray % self.n_fast
        self.x_bits = [("seq", 2 * b) for b in bits_of(n_seq // 2)]
        self.fast_bits = [("ray", b) for b in bits_of(self.n_fast)]
        self.slow_bits = [("ray", self.n_fast * b) for b in bits_of(SLOW)]
        self.spots = (self.slow, SLOW - 1 - self.slow)

    def across(self, axis, bit):
        if axis == "seq":
            return (flip(self.seq, bit), self.ray)
        return (self.seq, flip(self.ray, bit))

    def value(self, axis, bit):
        return ((self.seq if axis == "seq" else self.ray) // bit) % 2

    def along(self, way):
        return (self.seq, self.ray + (self.n_fast if way == 0 else -self.n_fast))

    def after(self, step):
        return (self.seq, (self.slow + step) % SLOW * self.n_fast + self.fast)

    def mirrored(self, way, chunk):
        return chunk if way == 0 else SLOW - 1 - chunk


def remote(src, dst, send_sem, recv_sem, device):
    return pltpu.make_async_remote_copy(
        src_ref=src,
        dst_ref=dst,
        send_sem=send_sem,
        recv_sem=recv_sem,
        device_id=device,
        device_id_type=MESH,
    )


def greet(place, exchanges):
    barrier = pltpu.get_barrier_semaphore()
    for axis, bit in exchanges:
        pl.semaphore_signal(barrier, inc=1, device_id=place.across(axis, bit), device_id_type=MESH)
    for step in range(1, SLOW):
        pl.semaphore_signal(barrier, inc=1, device_id=place.after(step), device_id_type=MESH)
    pl.semaphore_wait(barrier, len(exchanges) + SLOW - 1)


class Line:
    def __init__(self, place, block, recv, send_sem, recv_sem):
        self.place, self.block, self.recv, self.send_sem, self.recv_sem = place, block, recv, send_sem, recv_sem

    def copy(self, way, t, to):
        chunk = self.place.mirrored(way, SLOW - 1 - (t - self.place.spots[way]))
        return remote(
            self.block(chunk), self.recv(way, t), self.send_sem(way, t), self.recv_sem(way, t), self.place.along(to)
        )

    def landed(self, way, t):
        remote(
            self.recv(way, t), self.recv(way, t), self.send_sem(way, t), self.recv_sem(way, t), self.place.along(1 - way)
        ).wait_recv()
        return self.recv(way, t)[...].astype(f32)

    def step(self, t):
        for way in range(2):
            spot = self.place.spots[way]

            @pl.when((spot <= t) & (spot < SLOW - 1))
            def _(way=way, spot=spot):
                if t > 0:

                    @pl.when(spot > 0)
                    def _():
                        block = self.block(self.place.mirrored(way, SLOW - 1 - (t - spot)))
                        block[...] = (block[...].astype(f32) + self.landed(way, t - 1)).astype(bf16)

                self.copy(way, t, way).start()

    def last(self, total):
        total[...] = self.block(self.place.slow)[...].astype(f32)
        for way in range(2):

            @pl.when(self.place.spots[way] > 0)
            def _(way=way):
                total[...] += self.landed(way, SLOW - 2)

    def drain(self):
        for way in range(2):
            for t in range(SLOW - 1):
                spot = self.place.spots[way]

                @pl.when((spot <= t) & (spot < SLOW - 1))
                def _(way=way, t=t):
                    self.copy(way, t, way).wait_send()


class Spread:
    def __init__(self, place, block, send_sem, recv_sem):
        self.place, self.block, self.send_sem, self.recv_sem = place, block, send_sem, recv_sem

    def copy(self, way, t, to):
        chunk = self.place.mirrored(way, self.place.spots[way] - t)
        block = self.block(chunk)
        return remote(block, block, self.send_sem(way, t), self.recv_sem(way, t), self.place.along(to))

    def step(self, t):
        for way in range(2):
            spot = self.place.spots[way]

            @pl.when(spot >= t)
            def _(way=way, spot=spot):
                if t > 0:
                    block = self.block(self.place.mirrored(way, spot - t))
                    remote(
                        block, block, self.send_sem(way, t - 1), self.recv_sem(way, t - 1), self.place.along(1 - way)
                    ).wait_recv()
                if t < SLOW - 1:

                    @pl.when(spot < SLOW - 1)
                    def _():
                        self.copy(way, t, way).start()

    def drain(self):
        for way in range(2):
            for t in range(SLOW - 1):
                spot = self.place.spots[way]

                @pl.when((spot >= t) & (spot < SLOW - 1))
                def _(way=way, t=t):
                    self.copy(way, t, way).wait_send()


def units_of(rows, n_x, n_fast):
    share = n_x * n_fast * SLOW * 16
    return rows // BLOCK if BLOCK % share == 0 else 1


def sum_kernel(
    n_seq,
    n_ray,
    units,
    lengths,
    wq_ref,
    wk_ref,
    wv_ref,
    shifted_ref,
    rays_ref,
    rows_ref,
    small_ref,
    q_ref,
    g_ref,
    lse_ref,
    dots_ref,
    scene_ref,
    rest_ref,
    gh_hbm,
    early_hbm,
    k_hbm,
    kt_hbm,
    v_hbm,
    all_hbm,
    o_q,
    o_k,
    o_v,
    o_o,
    o_u,
    o_d,
    glat_ref,
    grays_ref,
    small_out,
    k_slot,
    kt_slot,
    v_slot,
    all_slot,
    seg_ref,
    sum_kv,
    grads_kv,
    weights_kv,
    turned_q,
    gq_ref,
    own,
    other,
    full,
    rx,
    z_recv,
    lat,
    lat_recv,
    lz_recv,
    small_now,
    small_recv,
    early_sem,
    slot_sem,
    core_sem,
    halve_sem,
    z_sem,
    zg_sem,
    double_sem,
    back_sem,
    out_sem,
    lat_sem,
    lz_sem,
    small_sem,
):
    place = Place(n_seq, n_ray)
    core_pair = ("seq", 1)
    halvings = place.x_bits + place.fast_bits
    exchanges = [core_pair] + halvings + place.slow_bits
    core = place.core
    rows, width = own.shape
    late_from = early_hbm.shape[1]
    unit_rows = rows // units
    early_units = late_from // unit_rows
    sizes = [unit_rows >> i for i in range(len(halvings) + 1)]
    share = sizes[-1]
    line = share % (16 * SLOW) == 0
    piece = share // SLOW if line else share

    early_load = pltpu.make_async_copy(early_hbm.at[core], own.at[pl.ds(0, late_from)], early_sem.at[0])
    early_load.start()
    gh_load = pltpu.make_async_copy(gh_hbm, grays_ref, early_sem.at[1])
    gh_load.start()
    greet(place, [core_pair] + halvings)

    def base(u, stages):
        start = u * unit_rows
        for i in range(stages):
            start = start + place.value(*halvings[i]) * sizes[i + 1]
        return start

    def unit(u):
        return lane_rows(u * unit_rows, unit_rows)

    def core_parts(u):
        if units == 1:
            rows_of = (pl.ds(0, late_from), pl.ds(0, rows - late_from))
            when = (u == 0, u == 0)
            into = (pl.ds(0, late_from), pl.ds(late_from, rows - late_from))
        else:
            rows_of = (unit(u), lane_rows(u * unit_rows - late_from, unit_rows))
            when = (u < early_units, u >= early_units)
            into = (unit(u), unit(u))
        sources = (early_hbm.at[1 - core, rows_of[0]], other.at[rows_of[1]])
        return [
            (
                when[n],
                remote(
                    sources[n], full.at[into[n]], core_sem.at[0, n, u], core_sem.at[1, n, u], place.across(*core_pair)
                ),
            )
            for n in range(2)
        ]

    def halve_copy(i, u):
        size = sizes[i + 1]
        sent = base(u, i) + (1 - place.value(*halvings[i])) * size
        return remote(
            own.at[lane_rows(sent, size)],
            rx[i].at[lane_rows(u * size, size)],
            halve_sem.at[0, i, u],
            halve_sem.at[1, i, u],
            place.across(*halvings[i]),
        )

    def start_core(u):
        for when, copy in core_parts(u):

            @pl.when(when)
            def _(copy=copy):
                copy.start()

    def join_core(u):
        for when, copy in core_parts(u):

            @pl.when(when)
            def _(copy=copy):
                copy.wait()

        own[unit(u), :] = (own[unit(u), :].astype(f32) + full[unit(u), :].astype(f32)).astype(bf16)
        halve_copy(0, u).start()

    def join_half(i):
        def run(u):
            size = sizes[i + 1]
            halve_copy(i, u).wait()
            kept = lane_rows(base(u, i + 1), size)
            own[kept, :] = (own[kept, :].astype(f32) + rx[i][lane_rows(u * size, size), :].astype(f32)).astype(bf16)
            if i + 1 < len(halvings):
                halve_copy(i + 1, u).start()

        return run

    def z_rows(u, chunk):
        return lane_rows(base(u, len(halvings)) + chunk * piece, piece)

    def z_copy(u, step):
        return remote(
            own.at[z_rows(u, (place.slow + step) % SLOW)],
            z_recv.at[u, step - 1],
            z_sem.at[0, u, step - 1],
            z_sem.at[1, u, step - 1],
            place.after(step),
        )

    def z_back_copy(u, step, chunk):
        block = full.at[z_rows(u, chunk)]
        return remote(block, block, zg_sem.at[0, u, step - 1], zg_sem.at[1, u, step - 1], place.after(step))

    def start_z(u):
        for step in range(1, SLOW):
            z_copy(u, step).start()

    def join_z(u):
        total = own[z_rows(u, place.slow), :].astype(f32)
        for step in range(1, SLOW):
            z_copy(u, step).wait()
            total = total + z_recv[u, step - 1].astype(f32)
        full[z_rows(u, place.slow), :] = total.astype(bf16)
        for step in range(1, SLOW):
            z_back_copy(u, step, place.slow).start()

    def join_z_back(u):
        for step in range(1, SLOW):
            z_back_copy(u, step, place.slow).wait_send()
            z_back_copy(u, step, (place.slow + SLOW - step) % SLOW).wait_recv()

    def whole_copy(i, u):
        return remote(
            own.at[lane_rows(base(u, len(halvings)), share)],
            z_recv.at[u, i],
            z_sem.at[0, u, i],
            z_sem.at[1, u, i],
            place.across(*place.slow_bits[i]),
        )

    def whole_step(i):
        def run(u):
            mine = lane_rows(base(u, len(halvings)), share)
            if i > 0:
                whole_copy(i - 1, u).wait()
                own[mine, :] = (own[mine, :].astype(f32) + z_recv[u, i - 1].astype(f32)).astype(bf16)
            if i < len(place.slow_bits):
                whole_copy(i, u).start()
            else:
                full[mine, :] = own[mine, :]

        return run

    def double_copy(i, u):
        block = full.at[lane_rows(base(u, i + 1), sizes[i + 1])]
        return remote(block, block, double_sem.at[0, i, u], double_sem.at[1, i, u], place.across(*halvings[i]))

    def targets(n, c):
        per = width // BLOCK
        part, at = n // per, n % per
        rows_at = pl.ds(pl.multiple_of(at * BLOCK, BLOCK), BLOCK)
        after = pl.ds(pl.multiple_of((n + per - 1) % per * BLOCK, BLOCK), BLOCK)
        half_at = pl.ds(pl.multiple_of(c * width, 128), width)
        lower = pl.ds(pl.multiple_of(c * width + at * BLOCK, BLOCK), BLOCK)
        last = pl.ds(2 * BLOCK, BLOCK)
        return [
            (part == 0, o_u.at[rows_at, half_at]),
            (part == 1, o_d.at[lower]),
            (n == 2 * per, o_o.at[pl.ds(pl.multiple_of(c * BLOCK, BLOCK), BLOCK)]),
            ((n > 2 * per) & (n <= 3 * per) & (c == 0), o_k.at[after]),
            ((n > 2 * per) & (n <= 3 * per) & (c == 1), o_v.at[after]),
            ((n == 3 * per + 1) & (c == 0), o_o.at[last]),
            ((n == 3 * per + 1) & (c == 1), o_q.at[pl.ds(0, BLOCK)]),
            (n == 3 * per + 2, o_q.at[pl.ds(pl.multiple_of((1 + c) * BLOCK, BLOCK), BLOCK)]),
        ]

    def block_rows(n):
        return lane_rows(n * BLOCK, BLOCK)

    def blocks_of(u):
        return [u] if units > 1 else list(range(rows // BLOCK))

    def send_block(n):
        for when, target in targets(n, core):

            @pl.when(when)
            def _(target=target):
                source = full.at[block_rows(n)]
                remote(source, target, back_sem.at[0, n], back_sem.at[1, n], place.across(*core_pair)).start()
                pltpu.make_async_copy(source, target, out_sem.at[n]).start()

    def end_block(n):
        for when, target in targets(n, core):

            @pl.when(when)
            def _(target=target):
                source = full.at[block_rows(n)]
                remote(source, target, back_sem.at[0, n], back_sem.at[1, n], place.across(*core_pair)).wait_send()
                pltpu.make_async_copy(source, target, out_sem.at[n]).wait()

        for when, target in targets(n, 1 - core):

            @pl.when(when)
            def _(target=target):
                source = full.at[block_rows(n)]
                remote(source, target, back_sem.at[0, n], back_sem.at[1, n], place.across(*core_pair)).wait_recv()

    def start_double(u):
        double_copy(len(halvings) - 1, u).start()

    def join_double(i):
        def run(u):
            double_copy(i, u).wait()
            if i > 0:
                double_copy(i - 1, u).start()
            else:
                for n in blocks_of(u):
                    send_block(n)

        return run

    def finish_unit(u):
        for n in blocks_of(u):
            end_block(n)

    stages = [[start_core], [join_core]] + [[join_half(i)] for i in range(len(halvings))]
    if line:
        stages[-1].append(start_z)
        stages += [[join_z], [join_z_back]]
    else:
        stages[-1].append(whole_step(0))
        stages += [[whole_step(i)] for i in range(1, len(place.slow_bits) + 1)]
    stages[-1].append(start_double)
    stages += [[join_double(i)] for i in reversed(range(len(halvings)))]
    stages += [[finish_unit]]

    n_fast, block = lat.shape[1:3]
    group = n_fast * block
    half_rows = block // 2
    fast_sizes = [n_fast >> i for i in range(len(place.fast_bits) + 1)]

    def chunk_of(k):
        near = jnp.minimum(place.slow, SLOW - 1 - place.slow)
        ahead = SLOW - 1 - near
        chunk = jnp.where(k < ahead, SLOW - 1 - k, jnp.where(k - ahead < near, k - ahead, near))
        return jnp.where(place.slow == near, chunk, SLOW - 1 - chunk)

    def lat_base(stages):
        start = 0
        for i in range(stages):
            start = start + place.value(*place.fast_bits[i]) * fast_sizes[i + 1]
        return start

    def lat_half(m):
        return lane_rows((m % 2) * half_rows, half_rows)

    def lat_copy(i, m):
        size = fast_sizes[i + 1]
        sent = lat_base(i) + (1 - place.value(*place.fast_bits[i])) * size
        return remote(
            lat.at[chunk_of(m // 2), pl.ds(sent, size), lat_half(m)],
            lat_recv[i].at[m],
            lat_sem.at[0, i, m],
            lat_sem.at[1, i, m],
            place.across(*place.fast_bits[i]),
        )

    def start_lat(m):
        lat_copy(0, m).start()

    def lat_line(m):
        half = m % 2
        return Line(
            place,
            lambda chunk: lat.at[chunk, place.fast, lat_half(m)],
            lambda way, t: lz_recv.at[half, way, t],
            lambda way, t: lz_sem.at[0, half, way, t],
            lambda way, t: lz_sem.at[1, half, way, t],
        )

    def join_lat(i):
        def run(m):
            lat_copy(i, m).wait()
            kept = lat.at[chunk_of(m // 2), pl.ds(lat_base(i + 1), fast_sizes[i + 1]), lat_half(m)]
            kept[...] = (kept[...].astype(f32) + lat_recv[i][m].astype(f32)).astype(bf16)
            if i + 1 < len(place.fast_bits):
                lat_copy(i + 1, m).start()
            else:
                for t in range(SLOW - 1):

                    @pl.when(m // 2 == t)
                    def _(t=t):
                        lat_line(m).step(t)

        return run

    def finish_lat(m):
        @pl.when(m // 2 == SLOW - 1)
        def _():
            lat_line(m).last(glat_ref.at[lat_half(m)])
            lat_line(m).drain()

    lat_stages = [start_lat] + [join_lat(i) for i in range(len(place.fast_bits))] + [finish_lat]

    def small_copy(i):
        axis, bit = exchanges[i]
        return remote(
            small_now.at[i], small_recv.at[i], small_sem.at[0, i], small_sem.at[1, i], place.across(axis, bit)
        )

    def start_small():
        small_copy(0).start()

    def join_small(i):
        def run():
            small_copy(i).wait()
            small_now[i + 1] = small_now[i] + small_recv[i]
            if i + 1 < len(exchanges):
                small_copy(i + 1).start()

        return run

    tiles, groups = scene_ref.shape[0], width // WIDE
    pairs, parts = tiles // PAIR, group // STEP
    per_chunk = pairs * parts

    def slot_loads(k):
        chunk = chunk_of(k)
        at, columns = lane_rows(chunk * group, group), pl.ds(pl.multiple_of(chunk * group, 128), group)
        return (
            pltpu.make_async_copy(k_hbm.at[at], k_slot, slot_sem.at[0]),
            pltpu.make_async_copy(kt_hbm.at[:, columns], kt_slot, slot_sem.at[1]),
            pltpu.make_async_copy(v_hbm.at[at], v_slot, slot_sem.at[2]),
        )

    def all_load(k):
        columns = pl.ds(pl.multiple_of(chunk_of(k) * group, 128), group)
        return pltpu.make_async_copy(all_hbm.at[:, columns], all_slot, slot_sem.at[3])

    def open_chunk(k):
        for load in slot_loads(k):
            load.wait()

        all_load(k).start()
        seg_ref[...] = segments(lengths, chunk_of(k) * group, group)
        sum_kv[...] = jnp.zeros_like(sum_kv)

    def tile_rows(t):
        return pl.ds(pl.multiple_of(t * TILE, TILE), TILE)

    def back_step(pair, part):
        at = pl.ds(pl.multiple_of(part * STEP, 128), STEP)
        own_tiles = [pair * PAIR + i for i in range(PAIR)]
        seen = jnp.concatenate([seg_ref[at, :]] * PAIR, axis=1) == jnp.concatenate(
            [scene_ref[pl.ds(t, 1), :] for t in own_tiles], axis=1
        )
        for g in range(groups):
            to = group_at(g)
            q_spread = jnp.concatenate([spread_heads(q_ref[tile_rows(t), to]) for t in own_tiles], axis=0)
            g_spread = jnp.concatenate([spread_heads(g_ref[tile_rows(t), to]) for t in own_tiles], axis=0)
            lse = jnp.concatenate([lse_ref[pl.ds(t, 1), to] for t in own_tiles], axis=1)
            dots = jnp.concatenate([dots_ref[pl.ds(t, 1), to] for t in own_tiles], axis=1)
            s = matmul(k_slot[at, to], q_spread, 1, 1)
            p = jnp.where(seen, jnp.exp(s - lse), 0.0)
            sum_kv[1, at, to] += matmul(p.astype(bf16), g_spread, 1, 0)
            gp = matmul(v_slot[at, to], g_spread, 1, 1)
            gs = (p * (gp - dots)).astype(bf16)
            sum_kv[0, at, to] += matmul(gs, q_spread, 1, 0)
            turned_q[g, pair] += matmul(kt_slot[to, at], gs, 1, 0)

    def close_chunk(k):
        @pl.when(k + 1 < SLOW)
        def _():
            for load in slot_loads(k + 1):
                load.start()

        grads_kv[...] = sum_kv[...].astype(bf16)
        total = matmul(grads_kv[0], wk_ref[...], 1, 1) + matmul(grads_kv[1], wv_ref[...], 1, 1)
        lat[chunk_of(k)] = total.astype(bf16).reshape(n_fast, block, width)
        all_load(k).wait()
        for n in range(2):
            weights_kv[n] += matmul(all_slot[...], grads_kv[n], 1, 0)
        small_now[0, 7:8] += jnp.sum(grads_kv[1].astype(f32), axis=0, keepdims=True)

    def attend(step):
        k, part_of = step // per_chunk, step % per_chunk

        @pl.when(part_of == 0)
        def _():
            open_chunk(k)

        back_step(part_of // parts, part_of % parts)

        @pl.when(part_of == per_chunk - 1)
        def _():
            close_chunk(k)

    def key_terms():
        own[late_from : late_from + width, :] = weights_kv[core].astype(bf16)
        other[:width, :] = weights_kv[1 - core].astype(bf16)

    def query_terms():
        for t in range(tiles):
            for g in range(groups):
                turned = turned_q[g, t // PAIR, :, t % PAIR * WIDE : (t % PAIR + 1) * WIDE]
                gq_ref[t * TILE : (t + 1) * TILE, group_at(g)] = (fold_heads(turned) * HEAD ** (-0.5)).astype(bf16)

    def query_weight_terms():
        terms = matmul(shifted_ref[...], gq_ref[...], 0, 0).astype(bf16)
        first, second, third = [terms[b * BLOCK : (b + 1) * BLOCK] for b in range(width // BLOCK)]
        after = late_from + width

        @pl.when(core == 0)
        def _():
            own[after : after + BLOCK, :] = rest_ref[...]
            own[after + BLOCK :, :] = second
            other[width : width + BLOCK, :] = first
            other[width + BLOCK :, :] = third

        @pl.when(core == 1)
        def _():
            own[after : after + BLOCK, :] = first
            own[after + BLOCK :, :] = third
            other[width : width + BLOCK, :] = rest_ref[...]
            other[width + BLOCK :, :] = second

    def ray_terms():
        inputs = rays_ref[...].astype(f32)
        centred = inputs - jnp.mean(inputs, axis=1, keepdims=True)
        inverse = lax.rsqrt(jnp.mean(centred * centred, axis=1, keepdims=True) + 1e-05)
        normed = centred * inverse
        grad_shifted = matmul(gq_ref[...], wq_ref[...], 1, 1)
        grad_normed = grad_shifted * rows_ref[0:1, :]
        gh_load.wait()
        grays_ref[...] += inverse * (
            grad_normed
            - jnp.mean(grad_normed, axis=1, keepdims=True)
            - normed * jnp.mean(grad_normed * normed, axis=1, keepdims=True)
        )
        small_now[0, 4:5] = jnp.sum(grad_shifted * normed, axis=0, keepdims=True)
        small_now[0, 5:6] = jnp.sum(grad_shifted, axis=0, keepdims=True)
        small_now[0, 6:7] = jnp.sum(gq_ref[...].astype(f32), axis=0, keepdims=True)

    for load in slot_loads(0):
        load.start()
    turned_q[...] = jnp.zeros_like(turned_q)
    weights_kv[...] = jnp.zeros_like(weights_kv)
    small_now[0] = small_ref[...]
    early_load.wait()

    steps = SLOW * per_chunk
    late_start = steps if units > 1 else steps + 3
    finish = [key_terms, query_terms, query_weight_terms, ray_terms, start_small]
    work = {steps + n: [run] for n, run in enumerate(finish)}
    for i in range(len(exchanges)):
        work.setdefault(steps + len(finish) + i, []).append(join_small(i))
    lat_wait = LAT_WAIT
    late_waits = [0, LATE_CORE] + [LATE_X] + [LATE_STEP] * (len(stages) - 5) + [LATE_X, 1]
    late_at = [sum(late_waits[: n + 1]) for n in range(len(stages))]
    lat_span = steps + 2 + lat_wait * (len(lat_stages) - 1)
    beats = max(late_start + units - early_units + late_at[-1], lat_span, max(work) + 1)

    def one_beat(now, carry):
        for beat, runs in work.items():

            @pl.when(now == beat)
            def _(runs=runs):
                for run in runs:
                    run()

        for s in range(len(stages)):
            early = now - EARLY_WAIT * s
            late = now - late_start - late_at[s]
            u = jnp.where(late >= 0, late + early_units, early)

            @pl.when(((late >= 0) & (u < units)) | ((early >= 0) & (early < early_units)))
            def _(u=u, s=s):
                for run in stages[s]:
                    run(u)

        for s in range(len(lat_stages)):
            ahead = now - per_chunk - lat_wait * s
            m = ahead // per_chunk * 2 + ahead % per_chunk

            @pl.when((ahead >= 0) & (ahead % per_chunk < 2) & (m < 2 * SLOW))
            def _(m=m, s=s):
                lat_stages[s](m)

        @pl.when(now < steps)
        def _():
            attend(now)

        return carry

    lax.fori_loop(0, beats, one_beat, 0)
    small_out[...] = small_now[len(exchanges)]


def back_and_sum(
    n_seq,
    n_ray,
    block,
    lengths,
    w_query,
    w_key,
    w_value,
    shifted,
    rays,
    gh,
    rows,
    small,
    queries,
    ga,
    lse,
    dots,
    scene_rows,
    rest,
    early,
    keys,
    keys_t,
    values,
    all_t,
):
    n_fast = n_ray // SLOW
    n_x = n_seq // 2
    n_rays, width = rays.shape
    group = n_fast * block
    groups, pairs = width // WIDE, n_rays // TILE // PAIR
    sum_rows = 4 * width
    late_rows = sum_rows - early.shape[1]
    units = units_of(sum_rows, n_x, n_fast)
    halvings = len(bits_of(n_x)) + len(bits_of(n_fast))
    fast_bits = len(bits_of(n_fast))
    exchanges = 1 + halvings + len(bits_of(SLOW))
    share = sum_rows // units >> halvings
    piece = share // SLOW if share % (16 * SLOW) == 0 else share
    half = block // 2
    vmem = pltpu.VMEM
    sem = pltpu.SemaphoreType.DMA
    struct = jax.ShapeDtypeStruct
    in_vmem = pl.BlockSpec(memory_space=vmem)
    anywhere = pl.BlockSpec(memory_space=pl.ANY)
    return pl.pallas_call(
        functools.partial(sum_kernel, n_seq, n_ray, units),
        out_shape=(
            struct((width, width), bf16),
            struct((width, width), bf16),
            struct((width, width), bf16),
            struct((width, width), bf16),
            struct((width, 2 * width), bf16),
            struct((2 * width, width), bf16),
            struct((block, width), f32),
            struct((n_rays, width), f32),
            struct((8, width), f32),
        ),
        in_specs=[pl.BlockSpec(memory_space=pltpu.SMEM)] + [in_vmem] * 13 + [anywhere] * 6,
        out_specs=(anywhere,) * 6 + (in_vmem,) * 3,
        scratch_shapes=[
            vmem((group, width), bf16),
            vmem((width, group), bf16),
            vmem((group, width), bf16),
            vmem((width, group), bf16),
            vmem((group, WIDE), f32),
            vmem((2, group, width), f32),
            vmem((2, group, width), bf16),
            vmem((2, width, width), f32),
            vmem((groups, pairs, WIDE, PAIR * WIDE), f32),
            vmem((n_rays, width), bf16),
            vmem((sum_rows, width), bf16),
            vmem((late_rows, width), bf16),
            vmem((sum_rows, width), bf16),
            [vmem((sum_rows >> (i + 1), width), bf16) for i in range(halvings)],
            vmem((units, SLOW - 1, piece, width), bf16),
            vmem((SLOW, n_fast, block, width), bf16),
            [vmem((2 * SLOW, n_fast >> (i + 1), half, width), bf16) for i in range(fast_bits)],
            vmem((2, 2, SLOW - 1, half, width), bf16),
            vmem((exchanges + 1, 8, width), f32),
            vmem((exchanges, 8, width), f32),
            sem((2,)),
            sem((4,)),
            sem((2, 2, units)),
            sem((2, halvings, units)),
            sem((2, units, SLOW - 1)),
            sem((2, units, SLOW - 1)),
            sem((2, halvings, units)),
            sem((2, sum_rows // BLOCK)),
            sem((sum_rows // BLOCK,)),
            sem((2, fast_bits, 2 * SLOW)),
            sem((2, 2, 2, SLOW - 1)),
            sem((2, exchanges)),
        ],
        compiler_params=pltpu.CompilerParams(collective_id=1, has_side_effects=True, vmem_limit_bytes=63 << 20),
        name="back_and_sum",
    )(
        lengths,
        w_query,
        w_key,
        w_value,
        shifted,
        rays,
        rows,
        small,
        queries,
        ga,
        lse,
        dots,
        scene_rows,
        rest,
        gh,
        early,
        keys,
        keys_t,
        values,
        all_t,
    )


def gather_kernel(
    n_seq,
    n_ray,
    lengths,
    rays_ref,
    lat_ref,
    scene_ref,
    rows_ref,
    wq_ref,
    wk_ref,
    wv_ref,
    all_ref,
    k_ref,
    kt_ref,
    v_ref,
    q_ref,
    shifted_ref,
    att_ref,
    lse_ref,
    full,
    all_own,
    k_own,
    kt_own,
    v_own,
    vt_own,
    seg_ref,
    tops,
    totals,
    mixed,
    z_sem,
    y_sem,
    out_sem,
):
    place = Place(n_seq, n_ray)
    fast_bits = place.fast_bits[::-1]
    greet(place, place.fast_bits)
    block, width = lat_ref.shape
    half_rows = block // 2
    group = place.n_fast * block
    full[place.slow, place.fast] = lat_ref[...]

    def half_at(half):
        return pl.ds(half * half_rows, half_rows)

    def spread(half):
        return Spread(
            place,
            lambda chunk: full.at[chunk, place.fast, half_at(half)],
            lambda way, t: z_sem.at[0, half, way, t],
            lambda way, t: z_sem.at[1, half, way, t],
        )

    def fast_copy(i, chunk, half):
        axis, bit = fast_bits[i]
        mine = full.at[chunk, pl.ds(place.fast // bit * bit, bit), half_at(half)]
        return remote(mine, mine, y_sem.at[0, i, chunk, half], y_sem.at[1, i, chunk, half], place.across(axis, bit))

    def chunk_of(way, t):
        return place.mirrored(way, place.spots[way] - t)

    for half in range(2):
        fast_copy(0, place.slow, half).start()
        spread(half).step(0)

    inputs = rays_ref[...].astype(f32)
    centred = inputs - jnp.mean(inputs, axis=1, keepdims=True)
    inverse = lax.rsqrt(jnp.mean(centred * centred, axis=1, keepdims=True) + 1e-05)
    shifted = (centred * inverse * rows_ref[0:1, :] + rows_ref[1:2, :]).astype(bf16)
    shifted_ref[...] = shifted
    queries = (matmul(shifted, wq_ref[...], 1, 0) + rows_ref[2:3, :]).astype(bf16)
    q_ref[...] = (queries.astype(f32) * HEAD ** (-0.5)).astype(bf16)
    tiles, groups = scene_ref.shape[0], width // WIDE
    tops[...] = jnp.full_like(tops, masked_score)
    totals[...] = jnp.zeros_like(totals)
    mixed[...] = jnp.zeros_like(mixed)

    def attend(chunk):
        seg_ref[...] = segments(lengths, chunk * group, group)

        def one_tile(t, carry):
            ray_rows = pl.ds(pl.multiple_of(t * TILE, TILE), TILE)
            seen = seg_ref[...] == scene_ref[pl.ds(t, 1), :]
            for g in range(groups):
                s = matmul(k_own[chunk, :, group_at(g)], spread_heads(q_ref[ray_rows, group_at(g)]), 1, 1)
                s = jnp.where(seen, s, masked_score)
                old = tops[g, t]
                new = jnp.maximum(old, jnp.max(fold_rows(s, jnp.max), axis=0, keepdims=True))
                e = jnp.exp(s - new[0:1])
                fix = jnp.exp(old - new)
                tops[g, t] = new
                totals[g, t] = totals[g, t] * fix + fold_rows(e, jnp.sum)
                mixed[g, t] = mixed[g, t] * fix[0:1] + matmul(vt_own[chunk, group_at(g), :], e.astype(bf16), 1, 0)
            return carry

        lax.fori_loop(0, tiles, one_tile, 0)

    def results(chunk):
        rows = pl.ds(pl.multiple_of(chunk * group, 16), group)
        columns = pl.ds(pl.multiple_of(chunk * group, 128), group)
        return [
            (k_own.at[chunk], k_ref.at[rows]),
            (kt_own.at[chunk], kt_ref.at[:, columns]),
            (v_own.at[chunk], v_ref.at[rows]),
            (all_own.at[chunk], all_ref.at[:, columns]),
        ]

    def project(chunk):
        for half in range(2):
            for i in range(len(fast_bits)):
                fast_copy(i, chunk, half).wait()
                if i + 1 < len(fast_bits):
                    fast_copy(i + 1, chunk, half).start()
        latents = full[chunk].reshape(group, width)
        keys = matmul(latents, wk_ref[...], 1, 0).astype(bf16)
        k_own[chunk] = keys
        all_own[chunk] = latents.T
        kt_own[chunk] = keys.T
        values = (matmul(latents, wv_ref[...], 1, 0) + rows_ref[3:4, :]).astype(bf16)
        v_own[chunk] = values
        vt_own[chunk] = values.T
        for n, (source, target) in enumerate(results(chunk)):
            pltpu.make_async_copy(source, target, out_sem.at[n, chunk]).start()
        attend(chunk)

    def visit(index, carry):
        t, way = index // 2, index % 2
        for later in range(1, SLOW):

            @pl.when(index == 2 * (later - 1))
            def _(later=later):
                for half in range(2):
                    spread(half).step(later)
                    for to in range(2):

                        @pl.when(place.spots[to] >= later)
                        def _(half=half, to=to):
                            fast_copy(0, chunk_of(to, later), half).start()

        spot = jnp.where(way == 0, place.slow, SLOW - 1 - place.slow)
        chunk = jnp.where(way == 0, spot - t, SLOW - 1 - spot + t)

        @pl.when((spot >= t) & (index != 1))
        def _():
            project(chunk)

        return carry

    lax.fori_loop(0, 2 * SLOW, visit, 0)

    for t in range(tiles):
        for g in range(groups):
            total = jnp.sum(totals[g, t], axis=0, keepdims=True)
            att_ref[t * TILE : (t + 1) * TILE, group_at(g)] = fold_heads(mixed[g, t] * (1.0 / total))
            lse_ref[t : t + 1, group_at(g)] = tops[g, t][0:1] + jnp.log(total)

    def end(chunk, carry):
        for n, (source, target) in enumerate(results(chunk)):
            pltpu.make_async_copy(source, target, out_sem.at[n, chunk]).wait()
        return carry

    lax.fori_loop(0, SLOW, end, 0)
    for half in range(2):
        spread(half).drain()


def gather_and_attend(n_seq, n_ray, rays, latents, lengths, scene_rows, rows, w_query, w_key, w_value):
    block, width = latents.shape
    n_rays = rays.shape[0]
    n_fast = n_ray // SLOW
    group = n_fast * block
    total = n_ray * block
    tiles, groups = n_rays // TILE, width // WIDE
    fast_bits = len(bits_of(n_fast))
    vmem = pltpu.VMEM
    sem = pltpu.SemaphoreType.DMA
    in_vmem = pl.BlockSpec(memory_space=vmem)
    anywhere = pl.BlockSpec(memory_space=pl.ANY)
    struct = jax.ShapeDtypeStruct
    tall, wide = struct((total, width), bf16), struct((width, total), bf16)
    return pl.pallas_call(
        functools.partial(gather_kernel, n_seq, n_ray),
        out_shape=(
            wide,
            tall,
            wide,
            tall,
            struct((n_rays, width), bf16),
            struct((n_rays, width), bf16),
            struct((n_rays, width), f32),
            struct((tiles, width), f32),
        ),
        in_specs=[pl.BlockSpec(memory_space=pltpu.SMEM)] + [in_vmem] * 7,
        out_specs=(anywhere,) * 4 + (in_vmem,) * 4,
        scratch_shapes=[
            vmem((SLOW, n_fast, block, width), bf16),
            vmem((SLOW, width, group), bf16),
            vmem((SLOW, group, width), bf16),
            vmem((SLOW, width, group), bf16),
            vmem((SLOW, group, width), bf16),
            vmem((SLOW, width, group), bf16),
            vmem((group, WIDE), f32),
            vmem((groups, tiles, 8, WIDE), f32),
            vmem((groups, tiles, 8, WIDE), f32),
            vmem((groups, tiles, WIDE, WIDE), f32),
            sem((2, 2, 2, SLOW - 1)),
            sem((2, fast_bits, SLOW, 2)),
            sem((4, SLOW)),
        ],
        compiler_params=pltpu.CompilerParams(collective_id=0, has_side_effects=True, vmem_limit_bytes=58 << 20),
        name="gather_and_attend",
    )(lengths, rays, latents, scene_rows, rows, w_query, w_key, w_value)


def local(
    rays,
    latents,
    lengths,
    scenes,
    ln_gain,
    ln_bias,
    w_query,
    b_query,
    w_key,
    w_value,
    b_value,
    w_out,
    b_out,
    w_up,
    b_up,
    w_down,
    b_down,
    cotangent,
):
    width = rays.shape[1]
    n_seq, n_ray = lax.axis_size("seq"), lax.axis_size("ray")
    tiles = rays.shape[0] // TILE
    names = (ln_gain, ln_bias, b_query, b_value, b_out, b_up, b_down)
    rows = jnp.concatenate([v.reshape(-1, width) for v in names]).astype(f32)
    scene_rows = jnp.broadcast_to(scenes.reshape(tiles, 1, TILE), (tiles, PACK, TILE)).reshape(tiles, WIDE).astype(f32)
    all_t, keys, keys_t, values, queries, shifted, attended, lse = gather_and_attend(
        n_seq, n_ray, rays, latents, lengths, scene_rows, rows, w_query, w_key, w_value
    )
    result, grad_hidden, grad_attended, dots, small, early, rest = mlp(attended, rays, cotangent, rows, w_out, w_up, w_down)
    sum_q, sum_k, sum_v, sum_o, sum_u, sum_d, grad_latents, grad_rays, vectors = back_and_sum(
        n_seq,
        n_ray,
        latents.shape[0],
        lengths,
        w_query,
        w_key,
        w_value,
        shifted,
        rays,
        grad_hidden,
        rows,
        small,
        queries,
        grad_attended,
        lse,
        dots,
        scene_rows,
        rest,
        early,
        keys,
        keys_t,
        values,
        all_t,
    )
    return (
        result,
        grad_rays,
        grad_latents,
        vectors[4],
        vectors[5],
        sum_q.astype(f32),
        vectors[6],
        sum_k.astype(f32),
        sum_v.astype(f32),
        vectors[7],
        sum_o.astype(f32),
        vectors[0],
        sum_u.astype(f32),
        vectors[1:3].reshape(-1),
        sum_d.astype(f32),
        vectors[3],
    )


def solution(mesh):
    whole = P(("seq", "ray"), None)
    in_specs = (whole, whole, P("seq", None), P(("seq", "ray"))) + (P(),) * 13 + (whole,)
    out_specs = (whole,) * 3 + (P(),) * 13
    return jax.shard_map(local, mesh=mesh, in_specs=in_specs, out_specs=out_specs, check_vma=False)
```

```python
import functools
import math

import jax
import jax.numpy as jnp
from jax import lax
from jax.experimental import pallas as pl
from jax.experimental.pallas import tpu as pltpu
from jax.sharding import PartitionSpec as P

HEADS = 12
HEAD = 64
TILE = 64
WIDE = 256
PACK = WIDE // HEAD
EARLY_WAIT = 2
LATE_CORE, LATE_X, LATE_STEP = 1, 2, 1
LAT_WAIT = 3
FORWARD = 2
PAIR = 3
STEP = 256

masked_score = -1e30
f32 = jnp.float32
bf16 = jnp.bfloat16


def matmul(first_arg, second_arg, first_dim, second_dim):
    return lax.dot_general(
        first_arg,
        second_arg,
        (((first_dim,), (second_dim,)), ((), ())),
        preferred_element_type=jnp.float32,
    )


def own_block():
    row = lax.broadcasted_iota(jnp.int32, (WIDE, WIDE), 0) // TILE
    column = lax.broadcasted_iota(jnp.int32, (WIDE, WIDE), 1) // HEAD
    return row == column


def spread_heads(tile):
    return jnp.where(own_block(), jnp.concatenate([tile] * PACK, axis=0), jnp.zeros((), tile.dtype))


def fold_heads(turned):
    kept = jnp.where(own_block(), turned, 0.0)
    folded = (kept[:, : WIDE // 2] + kept[:, WIDE // 2 :]).T
    return folded[:TILE, :] + folded[TILE:, :]


def fold_rows(block, combine):
    return combine(block.reshape(block.shape[0] // 8, 8, block.shape[1]), axis=0)


def group_at(g):
    return slice(g * WIDE, (g + 1) * WIDE)


def segments(lengths, first, count):
    at = lax.broadcasted_iota(jnp.int32, (count, WIDE), 0) + first
    end, scene = 0, jnp.zeros((count, WIDE), f32)
    for c in range(lengths.shape[1] - 1):
        end = end + lengths[0, c]
        scene = scene + (at >= end).astype(f32)
    return scene


def gelu_both(pre):
    half = 0.5 * (1.0 + lax.erf(pre * math.sqrt(0.5)))
    return pre * half, half + pre * jnp.exp(-0.5 * pre * pre) * (1.0 / math.sqrt(2.0 * math.pi))


MESH = pl.DeviceIdType.MESH
BLOCK = 256
SLOW = 4


def flip(index, bit):
    return index + bit * (1 - 2 * ((index // bit) % 2))


def bits_of(count):
    bits = []
    while count > 1:
        count //= 2
        bits.append(count)
    return bits


def lane_rows(start, size):
    return pl.ds(pl.multiple_of(start, 16), size)


class Place:
    def __init__(self, n_seq, n_ray):
        self.seq = lax.axis_index("seq")
        self.ray = lax.axis_index("ray")
        self.n_fast = n_ray // SLOW
        self.core = self.seq % 2
        self.slow = self.ray // self.n_fast
        self.fast = self.ray % self.n_fast
        self.x_bits = [("seq", 2 * b) for b in bits_of(n_seq // 2)]
        self.fast_bits = [("ray", b) for b in bits_of(self.n_fast)]
        self.slow_bits = [("ray", self.n_fast * b) for b in bits_of(SLOW)]
        self.spots = (self.slow, SLOW - 1 - self.slow)

    def across(self, axis, bit):
        if axis == "seq":
            return (flip(self.seq, bit), self.ray)
        return (self.seq, flip(self.ray, bit))

    def value(self, axis, bit):
        return ((self.seq if axis == "seq" else self.ray) // bit) % 2

    def along(self, way):
        return (self.seq, self.ray + (self.n_fast if way == 0 else -self.n_fast))

    def after(self, step):
        return (self.seq, (self.slow + step) % SLOW * self.n_fast + self.fast)

    def mirrored(self, way, chunk):
        return chunk if way == 0 else SLOW - 1 - chunk


def remote(src, dst, send_sem, recv_sem, device):
    return pltpu.make_async_remote_copy(
        src_ref=src,
        dst_ref=dst,
        send_sem=send_sem,
        recv_sem=recv_sem,
        device_id=device,
        device_id_type=MESH,
    )


def greet(place, exchanges):
    barrier = pltpu.get_barrier_semaphore()
    for axis, bit in exchanges:
        pl.semaphore_signal(barrier, inc=1, device_id=place.across(axis, bit), device_id_type=MESH)
    for step in range(1, SLOW):
        pl.semaphore_signal(barrier, inc=1, device_id=place.after(step), device_id_type=MESH)
    pl.semaphore_wait(barrier, len(exchanges) + SLOW - 1)


class Line:
    def __init__(self, place, block, recv, send_sem, recv_sem):
        self.place, self.block, self.recv, self.send_sem, self.recv_sem = place, block, recv, send_sem, recv_sem

    def copy(self, way, t, to):
        chunk = self.place.mirrored(way, SLOW - 1 - (t - self.place.spots[way]))
        return remote(
            self.block(chunk), self.recv(way, t), self.send_sem(way, t), self.recv_sem(way, t), self.place.along(to)
        )

    def landed(self, way, t):
        remote(
            self.recv(way, t), self.recv(way, t), self.send_sem(way, t), self.recv_sem(way, t), self.place.along(1 - way)
        ).wait_recv()
        return self.recv(way, t)[...].astype(f32)

    def step(self, t):
        for way in range(2):
            spot = self.place.spots[way]

            @pl.when((spot <= t) & (spot < SLOW - 1))
            def _(way=way, spot=spot):
                if t > 0:

                    @pl.when(spot > 0)
                    def _():
                        block = self.block(self.place.mirrored(way, SLOW - 1 - (t - spot)))
                        block[...] = (block[...].astype(f32) + self.landed(way, t - 1)).astype(bf16)

                self.copy(way, t, way).start()

    def last(self, total):
        total[...] = self.block(self.place.slow)[...].astype(f32)
        for way in range(2):

            @pl.when(self.place.spots[way] > 0)
            def _(way=way):
                total[...] += self.landed(way, SLOW - 2)

    def drain(self):
        for way in range(2):
            for t in range(SLOW - 1):
                spot = self.place.spots[way]

                @pl.when((spot <= t) & (spot < SLOW - 1))
                def _(way=way, t=t):
                    self.copy(way, t, way).wait_send()


class Spread:
    def __init__(self, place, block, send_sem, recv_sem):
        self.place, self.block, self.send_sem, self.recv_sem = place, block, send_sem, recv_sem

    def copy(self, way, t, to):
        chunk = self.place.mirrored(way, self.place.spots[way] - t)
        block = self.block(chunk)
        return remote(block, block, self.send_sem(way, t), self.recv_sem(way, t), self.place.along(to))

    def step(self, t):
        for way in range(2):
            spot = self.place.spots[way]

            @pl.when(spot >= t)
            def _(way=way, spot=spot):
                if t > 0:
                    block = self.block(self.place.mirrored(way, spot - t))
                    remote(
                        block, block, self.send_sem(way, t - 1), self.recv_sem(way, t - 1), self.place.along(1 - way)
                    ).wait_recv()
                if t < SLOW - 1:

                    @pl.when(spot < SLOW - 1)
                    def _():
                        self.copy(way, t, way).start()

    def drain(self):
        for way in range(2):
            for t in range(SLOW - 1):
                spot = self.place.spots[way]

                @pl.when((spot >= t) & (spot < SLOW - 1))
                def _(way=way, t=t):
                    self.copy(way, t, way).wait_send()


def units_of(rows, n_x, n_fast):
    share = n_x * n_fast * SLOW * 16
    return rows // BLOCK if BLOCK % share == 0 else 1


def sum_kernel(
    n_seq,
    n_ray,
    units,
    lengths,
    wq_ref,
    wk_ref,
    wv_ref,
    shifted_ref,
    rays_ref,
    rows_ref,
    small_ref,
    q_ref,
    g_ref,
    lse_ref,
    dots_ref,
    scene_ref,
    rest_ref,
    gh_hbm,
    early_hbm,
    k_hbm,
    kt_hbm,
    v_hbm,
    all_hbm,
    o_q,
    o_k,
    o_v,
    o_o,
    o_u,
    o_d,
    glat_ref,
    grays_ref,
    small_out,
    k_slot,
    kt_slot,
    v_slot,
    all_slot,
    seg_ref,
    sum_kv,
    grads_kv,
    weights_kv,
    turned_q,
    gq_ref,
    own,
    other,
    full,
    rx,
    z_recv,
    lat,
    lat_recv,
    lz_recv,
    small_now,
    small_recv,
    early_sem,
    slot_sem,
    core_sem,
    halve_sem,
    z_sem,
    zg_sem,
    double_sem,
    back_sem,
    out_sem,
    lat_sem,
    lz_sem,
    small_sem,
):
    place = Place(n_seq, n_ray)
    core_pair = ("seq", 1)
    halvings = place.x_bits + place.fast_bits
    exchanges = [core_pair] + halvings + place.slow_bits
    core = place.core
    rows, width = own.shape
    late_from = early_hbm.shape[1]
    unit_rows = rows // units
    early_units = late_from // unit_rows
    sizes = [unit_rows >> i for i in range(len(halvings) + 1)]
    share = sizes[-1]
    line = share % (16 * SLOW) == 0
    piece = share // SLOW if line else share

    early_load = pltpu.make_async_copy(early_hbm.at[core], own.at[pl.ds(0, late_from)], early_sem.at[0])
    early_load.start()
    gh_load = pltpu.make_async_copy(gh_hbm, grays_ref, early_sem.at[1])
    gh_load.start()
    greet(place, [core_pair] + halvings)

    def base(u, stages):
        start = u * unit_rows
        for i in range(stages):
            start = start + place.value(*halvings[i]) * sizes[i + 1]
        return start

    def unit(u):
        return lane_rows(u * unit_rows, unit_rows)

    def core_parts(u):
        if units == 1:
            rows_of = (pl.ds(0, late_from), pl.ds(0, rows - late_from))
            when = (u == 0, u == 0)
            into = (pl.ds(0, late_from), pl.ds(late_from, rows - late_from))
        else:
            rows_of = (unit(u), lane_rows(u * unit_rows - late_from, unit_rows))
            when = (u < early_units, u >= early_units)
            into = (unit(u), unit(u))
        sources = (early_hbm.at[1 - core, rows_of[0]], other.at[rows_of[1]])
        return [
            (
                when[n],
                remote(
                    sources[n], full.at[into[n]], core_sem.at[0, n, u], core_sem.at[1, n, u], place.across(*core_pair)
                ),
            )
            for n in range(2)
        ]

    def halve_copy(i, u):
        size = sizes[i + 1]
        sent = base(u, i) + (1 - place.value(*halvings[i])) * size
        return remote(
            own.at[lane_rows(sent, size)],
            rx[i].at[lane_rows(u * size, size)],
            halve_sem.at[0, i, u],
            halve_sem.at[1, i, u],
            place.across(*halvings[i]),
        )

    def start_core(u):
        for when, copy in core_parts(u):

            @pl.when(when)
            def _(copy=copy):
                copy.start()

    def join_core(u):
        for when, copy in core_parts(u):

            @pl.when(when)
            def _(copy=copy):
                copy.wait()

        own[unit(u), :] = (own[unit(u), :].astype(f32) + full[unit(u), :].astype(f32)).astype(bf16)
        halve_copy(0, u).start()

    def join_half(i):
        def run(u):
            size = sizes[i + 1]
            halve_copy(i, u).wait()
            kept = lane_rows(base(u, i + 1), size)
            own[kept, :] = (own[kept, :].astype(f32) + rx[i][lane_rows(u * size, size), :].astype(f32)).astype(bf16)
            if i + 1 < len(halvings):
                halve_copy(i + 1, u).start()

        return run

    def z_rows(u, chunk):
        return lane_rows(base(u, len(halvings)) + chunk * piece, piece)

    def z_copy(u, step):
        return remote(
            own.at[z_rows(u, (place.slow + step) % SLOW)],
            z_recv.at[u, step - 1],
            z_sem.at[0, u, step - 1],
            z_sem.at[1, u, step - 1],
            place.after(step),
        )

    def z_back_copy(u, step, chunk):
        block = full.at[z_rows(u, chunk)]
        return remote(block, block, zg_sem.at[0, u, step - 1], zg_sem.at[1, u, step - 1], place.after(step))

    def start_z(u):
        for step in range(1, SLOW):
            z_copy(u, step).start()

    def join_z(u):
        total = own[z_rows(u, place.slow), :].astype(f32)
        for step in range(1, SLOW):
            z_copy(u, step).wait()
            total = total + z_recv[u, step - 1].astype(f32)
        full[z_rows(u, place.slow), :] = total.astype(bf16)
        for step in range(1, SLOW):
            z_back_copy(u, step, place.slow).start()

    def join_z_back(u):
        for step in range(1, SLOW):
            z_back_copy(u, step, place.slow).wait_send()
            z_back_copy(u, step, (place.slow + SLOW - step) % SLOW).wait_recv()

    def whole_copy(i, u):
        return remote(
            own.at[lane_rows(base(u, len(halvings)), share)],
            z_recv.at[u, i],
            z_sem.at[0, u, i],
            z_sem.at[1, u, i],
            place.across(*place.slow_bits[i]),
        )

    def whole_step(i):
        def run(u):
            mine = lane_rows(base(u, len(halvings)), share)
            if i > 0:
                whole_copy(i - 1, u).wait()
                own[mine, :] = (own[mine, :].astype(f32) + z_recv[u, i - 1].astype(f32)).astype(bf16)
            if i < len(place.slow_bits):
                whole_copy(i, u).start()
            else:
                full[mine, :] = own[mine, :]

        return run

    def double_copy(i, u):
        block = full.at[lane_rows(base(u, i + 1), sizes[i + 1])]
        return remote(block, block, double_sem.at[0, i, u], double_sem.at[1, i, u], place.across(*halvings[i]))

    def targets(n, c):
        per = width // BLOCK
        part, at = n // per, n % per
        rows_at = pl.ds(pl.multiple_of(at * BLOCK, BLOCK), BLOCK)
        after = pl.ds(pl.multiple_of((n + per - 1) % per * BLOCK, BLOCK), BLOCK)
        half_at = pl.ds(pl.multiple_of(c * width, 128), width)
        lower = pl.ds(pl.multiple_of(c * width + at * BLOCK, BLOCK), BLOCK)
        last = pl.ds(2 * BLOCK, BLOCK)
        return [
            (part == 0, o_u.at[rows_at, half_at]),
            (part == 1, o_d.at[lower]),
            (n == 2 * per, o_o.at[pl.ds(pl.multiple_of(c * BLOCK, BLOCK), BLOCK)]),
            ((n > 2 * per) & (n <= 3 * per) & (c == 0), o_k.at[after]),
            ((n > 2 * per) & (n <= 3 * per) & (c == 1), o_v.at[after]),
            ((n == 3 * per + 1) & (c == 0), o_o.at[last]),
            ((n == 3 * per + 1) & (c == 1), o_q.at[pl.ds(0, BLOCK)]),
            (n == 3 * per + 2, o_q.at[pl.ds(pl.multiple_of((1 + c) * BLOCK, BLOCK), BLOCK)]),
        ]

    def block_rows(n):
        return lane_rows(n * BLOCK, BLOCK)

    def blocks_of(u):
        return [u] if units > 1 else list(range(rows // BLOCK))

    def send_block(n):
        for when, target in targets(n, core):

            @pl.when(when)
            def _(target=target):
                source = full.at[block_rows(n)]
                remote(source, target, back_sem.at[0, n], back_sem.at[1, n], place.across(*core_pair)).start()
                pltpu.make_async_copy(source, target, out_sem.at[n]).start()

    def end_block(n):
        for when, target in targets(n, core):

            @pl.when(when)
            def _(target=target):
                source = full.at[block_rows(n)]
                remote(source, target, back_sem.at[0, n], back_sem.at[1, n], place.across(*core_pair)).wait_send()
                pltpu.make_async_copy(source, target, out_sem.at[n]).wait()

        for when, target in targets(n, 1 - core):

            @pl.when(when)
            def _(target=target):
                source = full.at[block_rows(n)]
                remote(source, target, back_sem.at[0, n], back_sem.at[1, n], place.across(*core_pair)).wait_recv()

    def start_double(u):
        double_copy(len(halvings) - 1, u).start()

    def join_double(i):
        def run(u):
            double_copy(i, u).wait()
            if i > 0:
                double_copy(i - 1, u).start()
            else:
                for n in blocks_of(u):
                    send_block(n)

        return run

    def finish_unit(u):
        for n in blocks_of(u):
            end_block(n)

    stages = [[start_core], [join_core]] + [[join_half(i)] for i in range(len(halvings))]
    if line:
        stages[-1].append(start_z)
        stages += [[join_z], [join_z_back]]
    else:
        stages[-1].append(whole_step(0))
        stages += [[whole_step(i)] for i in range(1, len(place.slow_bits) + 1)]
    stages[-1].append(start_double)
    stages += [[join_double(i)] for i in reversed(range(len(halvings)))]
    stages += [[finish_unit]]

    n_fast, block = lat.shape[1:3]
    group = n_fast * block
    half_rows = block // 2
    fast_sizes = [n_fast >> i for i in range(len(place.fast_bits) + 1)]

    def chunk_of(k):
        near = jnp.minimum(place.slow, SLOW - 1 - place.slow)
        ahead = SLOW - 1 - near
        chunk = jnp.where(k < ahead, SLOW - 1 - k, jnp.where(k - ahead < near, k - ahead, near))
        return jnp.where(place.slow == near, chunk, SLOW - 1 - chunk)

    def lat_base(stages):
        start = 0
        for i in range(stages):
            start = start + place.value(*place.fast_bits[i]) * fast_sizes[i + 1]
        return start

    def lat_half(m):
        return lane_rows((m % 2) * half_rows, half_rows)

    def lat_copy(i, m):
        size = fast_sizes[i + 1]
        sent = lat_base(i) + (1 - place.value(*place.fast_bits[i])) * size
        return remote(
            lat.at[chunk_of(m // 2), pl.ds(sent, size), lat_half(m)],
            lat_recv[i].at[m],
            lat_sem.at[0, i, m],
            lat_sem.at[1, i, m],
            place.across(*place.fast_bits[i]),
        )

    def start_lat(m):
        lat_copy(0, m).start()

    def lat_line(m):
        half = m % 2
        return Line(
            place,
            lambda chunk: lat.at[chunk, place.fast, lat_half(m)],
            lambda way, t: lz_recv.at[half, way, t],
            lambda way, t: lz_sem.at[0, half, way, t],
            lambda way, t: lz_sem.at[1, half, way, t],
        )

    def join_lat(i):
        def run(m):
            lat_copy(i, m).wait()
            kept = lat.at[chunk_of(m // 2), pl.ds(lat_base(i + 1), fast_sizes[i + 1]), lat_half(m)]
            kept[...] = (kept[...].astype(f32) + lat_recv[i][m].astype(f32)).astype(bf16)
            if i + 1 < len(place.fast_bits):
                lat_copy(i + 1, m).start()
            else:
                for t in range(SLOW - 1):

                    @pl.when(m // 2 == t)
                    def _(t=t):
                        lat_line(m).step(t)

        return run

    def finish_lat(m):
        @pl.when(m // 2 == SLOW - 1)
        def _():
            lat_line(m).last(glat_ref.at[lat_half(m)])
            lat_line(m).drain()

    lat_stages = [start_lat] + [join_lat(i) for i in range(len(place.fast_bits))] + [finish_lat]

    def small_copy(i):
        axis, bit = exchanges[i]
        return remote(
            small_now.at[i], small_recv.at[i], small_sem.at[0, i], small_sem.at[1, i], place.across(axis, bit)
        )

    def start_small():
        small_copy(0).start()

    def join_small(i):
        def run():
            small_copy(i).wait()
            small_now[i + 1] = small_now[i] + small_recv[i]
            if i + 1 < len(exchanges):
                small_copy(i + 1).start()

        return run

    tiles, groups = scene_ref.shape[0], width // WIDE
    pairs, parts = tiles // PAIR, group // STEP
    per_chunk = pairs * parts

    def slot_loads(k):
        chunk = chunk_of(k)
        at, columns = lane_rows(chunk * group, group), pl.ds(pl.multiple_of(chunk * group, 128), group)
        return (
            pltpu.make_async_copy(k_hbm.at[at], k_slot, slot_sem.at[0]),
            pltpu.make_async_copy(kt_hbm.at[:, columns], kt_slot, slot_sem.at[1]),
            pltpu.make_async_copy(v_hbm.at[at], v_slot, slot_sem.at[2]),
        )

    def all_load(k):
        columns = pl.ds(pl.multiple_of(chunk_of(k) * group, 128), group)
        return pltpu.make_async_copy(all_hbm.at[:, columns], all_slot, slot_sem.at[3])

    def open_chunk(k):
        for load in slot_loads(k):
            load.wait()

        all_load(k).start()
        seg_ref[...] = segments(lengths, chunk_of(k) * group, group)
        sum_kv[...] = jnp.zeros_like(sum_kv)

    def tile_rows(t):
        return pl.ds(pl.multiple_of(t * TILE, TILE), TILE)

    def back_step(pair, part):
        at = pl.ds(pl.multiple_of(part * STEP, 128), STEP)
        own_tiles = [pair * PAIR + i for i in range(PAIR)]
        seen = jnp.concatenate([seg_ref[at, :]] * PAIR, axis=1) == jnp.concatenate(
            [scene_ref[pl.ds(t, 1), :] for t in own_tiles], axis=1
        )
        for g in range(groups):
            to = group_at(g)
            q_spread = jnp.concatenate([spread_heads(q_ref[tile_rows(t), to]) for t in own_tiles], axis=0)
            g_spread = jnp.concatenate([spread_heads(g_ref[tile_rows(t), to]) for t in own_tiles], axis=0)
            lse = jnp.concatenate([lse_ref[pl.ds(t, 1), to] for t in own_tiles], axis=1)
            dots = jnp.concatenate([dots_ref[pl.ds(t, 1), to] for t in own_tiles], axis=1)
            s = matmul(k_slot[at, to], q_spread, 1, 1)
            p = jnp.where(seen, jnp.exp(s - lse), 0.0)
            sum_kv[1, at, to] += matmul(p.astype(bf16), g_spread, 1, 0)
            gp = matmul(v_slot[at, to], g_spread, 1, 1)
            gs = (p * (gp - dots)).astype(bf16)
            sum_kv[0, at, to] += matmul(gs, q_spread, 1, 0)
            turned_q[g, pair] += matmul(kt_slot[to, at], gs, 1, 0)

    def close_chunk(k):
        @pl.when(k + 1 < SLOW)
        def _():
            for load in slot_loads(k + 1):
                load.start()

        grads_kv[...] = sum_kv[...].astype(bf16)
        total = matmul(grads_kv[0], wk_ref[...], 1, 1) + matmul(grads_kv[1], wv_ref[...], 1, 1)
        lat[chunk_of(k)] = total.astype(bf16).reshape(n_fast, block, width)
        all_load(k).wait()
        for n in range(2):
            weights_kv[n] += matmul(all_slot[...], grads_kv[n], 1, 0)
        small_now[0, 7:8] += jnp.sum(grads_kv[1].astype(f32), axis=0, keepdims=True)

    def attend(step):
        k, part_of = step // per_chunk, step % per_chunk

        @pl.when(part_of == 0)
        def _():
            open_chunk(k)

        back_step(part_of // parts, part_of % parts)

        @pl.when(part_of == per_chunk - 1)
        def _():
            close_chunk(k)

    def key_terms():
        own[late_from : late_from + width, :] = weights_kv[core].astype(bf16)
        other[:width, :] = weights_kv[1 - core].astype(bf16)

    def query_terms():
        for t in range(tiles):
            for g in range(groups):
                turned = turned_q[g, t // PAIR, :, t % PAIR * WIDE : (t % PAIR + 1) * WIDE]
                gq_ref[t * TILE : (t + 1) * TILE, group_at(g)] = (fold_heads(turned) * HEAD ** (-0.5)).astype(bf16)

    def query_weight_terms():
        terms = matmul(shifted_ref[...], gq_ref[...], 0, 0).astype(bf16)
        first, second, third = [terms[b * BLOCK : (b + 1) * BLOCK] for b in range(width // BLOCK)]
        after = late_from + width

        @pl.when(core == 0)
        def _():
            own[after : after + BLOCK, :] = rest_ref[...]
            own[after + BLOCK :, :] = second
            other[width : width + BLOCK, :] = first
            other[width + BLOCK :, :] = third

        @pl.when(core == 1)
        def _():
            own[after : after + BLOCK, :] = first
            own[after + BLOCK :, :] = third
            other[width : width + BLOCK, :] = rest_ref[...]
            other[width + BLOCK :, :] = second

    def ray_terms():
        inputs = rays_ref[...].astype(f32)
        centred = inputs - jnp.mean(inputs, axis=1, keepdims=True)
        inverse = lax.rsqrt(jnp.mean(centred * centred, axis=1, keepdims=True) + 1e-05)
        normed = centred * inverse
        grad_shifted = matmul(gq_ref[...], wq_ref[...], 1, 1)
        grad_normed = grad_shifted * rows_ref[0:1, :]
        gh_load.wait()
        grays_ref[...] += inverse * (
            grad_normed
            - jnp.mean(grad_normed, axis=1, keepdims=True)
            - normed * jnp.mean(grad_normed * normed, axis=1, keepdims=True)
        )
        small_now[0, 4:5] = jnp.sum(grad_shifted * normed, axis=0, keepdims=True)
        small_now[0, 5:6] = jnp.sum(grad_shifted, axis=0, keepdims=True)
        small_now[0, 6:7] = jnp.sum(gq_ref[...].astype(f32), axis=0, keepdims=True)

    for load in slot_loads(0):
        load.start()
    turned_q[...] = jnp.zeros_like(turned_q)
    weights_kv[...] = jnp.zeros_like(weights_kv)
    small_now[0] = small_ref[...]
    early_load.wait()

    steps = SLOW * per_chunk
    late_start = steps if units > 1 else steps + 3
    finish = [key_terms, query_terms, query_weight_terms, ray_terms, start_small]
    work = {steps + n: [run] for n, run in enumerate(finish)}
    for i in range(len(exchanges)):
        work.setdefault(steps + len(finish) + i, []).append(join_small(i))
    lat_wait = LAT_WAIT
    late_waits = [0, LATE_CORE] + [LATE_X] + [LATE_STEP] * (len(stages) - 5) + [LATE_X, 1]
    late_at = [sum(late_waits[: n + 1]) for n in range(len(stages))]
    lat_span = steps + 2 + lat_wait * (len(lat_stages) - 1)
    beats = max(late_start + units - early_units + late_at[-1], lat_span, max(work) + 1)

    def one_beat(now, carry):
        for beat, runs in work.items():

            @pl.when(now == beat)
            def _(runs=runs):
                for run in runs:
                    run()

        for s in range(len(stages)):
            early = now - EARLY_WAIT * s
            late = now - late_start - late_at[s]
            u = jnp.where(late >= 0, late + early_units, early)

            @pl.when(((late >= 0) & (u < units)) | ((early >= 0) & (early < early_units)))
            def _(u=u, s=s):
                for run in stages[s]:
                    run(u)

        for s in range(len(lat_stages)):
            ahead = now - per_chunk - lat_wait * s
            m = ahead // per_chunk * 2 + ahead % per_chunk

            @pl.when((ahead >= 0) & (ahead % per_chunk < 2) & (m < 2 * SLOW))
            def _(m=m, s=s):
                lat_stages[s](m)

        @pl.when(now < steps)
        def _():
            attend(now)

        return carry

    lax.fori_loop(0, beats, one_beat, 0)
    small_out[...] = small_now[len(exchanges)]


def back_and_sum(
    n_seq,
    n_ray,
    block,
    lengths,
    w_query,
    w_key,
    w_value,
    shifted,
    rays,
    gh,
    rows,
    small,
    queries,
    ga,
    lse,
    dots,
    scene_rows,
    rest,
    early,
    keys,
    keys_t,
    values,
    all_t,
):
    n_fast = n_ray // SLOW
    n_x = n_seq // 2
    n_rays, width = rays.shape
    group = n_fast * block
    groups, pairs = width // WIDE, n_rays // TILE // PAIR
    sum_rows = 4 * width
    late_rows = sum_rows - early.shape[1]
    units = units_of(sum_rows, n_x, n_fast)
    halvings = len(bits_of(n_x)) + len(bits_of(n_fast))
    fast_bits = len(bits_of(n_fast))
    exchanges = 1 + halvings + len(bits_of(SLOW))
    share = sum_rows // units >> halvings
    piece = share // SLOW if share % (16 * SLOW) == 0 else share
    half = block // 2
    vmem = pltpu.VMEM
    sem = pltpu.SemaphoreType.DMA
    struct = jax.ShapeDtypeStruct
    in_vmem = pl.BlockSpec(memory_space=vmem)
    anywhere = pl.BlockSpec(memory_space=pl.ANY)
    return pl.pallas_call(
        functools.partial(sum_kernel, n_seq, n_ray, units),
        out_shape=(
            struct((width, width), bf16),
            struct((width, width), bf16),
            struct((width, width), bf16),
            struct((width, width), bf16),
            struct((width, 2 * width), bf16),
            struct((2 * width, width), bf16),
            struct((block, width), f32),
            struct((n_rays, width), f32),
            struct((8, width), f32),
        ),
        in_specs=[pl.BlockSpec(memory_space=pltpu.SMEM)] + [in_vmem] * 13 + [anywhere] * 6,
        out_specs=(anywhere,) * 6 + (in_vmem,) * 3,
        scratch_shapes=[
            vmem((group, width), bf16),
            vmem((width, group), bf16),
            vmem((group, width), bf16),
            vmem((width, group), bf16),
            vmem((group, WIDE), f32),
            vmem((2, group, width), f32),
            vmem((2, group, width), bf16),
            vmem((2, width, width), f32),
            vmem((groups, pairs, WIDE, PAIR * WIDE), f32),
            vmem((n_rays, width), bf16),
            vmem((sum_rows, width), bf16),
            vmem((late_rows, width), bf16),
            vmem((sum_rows, width), bf16),
            [vmem((sum_rows >> (i + 1), width), bf16) for i in range(halvings)],
            vmem((units, SLOW - 1, piece, width), bf16),
            vmem((SLOW, n_fast, block, width), bf16),
            [vmem((2 * SLOW, n_fast >> (i + 1), half, width), bf16) for i in range(fast_bits)],
            vmem((2, 2, SLOW - 1, half, width), bf16),
            vmem((exchanges + 1, 8, width), f32),
            vmem((exchanges, 8, width), f32),
            sem((2,)),
            sem((4,)),
            sem((2, 2, units)),
            sem((2, halvings, units)),
            sem((2, units, SLOW - 1)),
            sem((2, units, SLOW - 1)),
            sem((2, halvings, units)),
            sem((2, sum_rows // BLOCK)),
            sem((sum_rows // BLOCK,)),
            sem((2, fast_bits, 2 * SLOW)),
            sem((2, 2, 2, SLOW - 1)),
            sem((2, exchanges)),
        ],
        compiler_params=pltpu.CompilerParams(collective_id=1, has_side_effects=True, vmem_limit_bytes=63 << 20),
        name="back_and_sum",
    )(
        lengths,
        w_query,
        w_key,
        w_value,
        shifted,
        rays,
        rows,
        small,
        queries,
        ga,
        lse,
        dots,
        scene_rows,
        rest,
        gh,
        early,
        keys,
        keys_t,
        values,
        all_t,
    )


def gather_kernel(
    n_seq,
    n_ray,
    lengths,
    rays_ref,
    lat_ref,
    scene_ref,
    up_bias_ref,
    gain_ref,
    bias_ref,
    q_bias_ref,
    v_bias_ref,
    out_bias_ref,
    down_bias_ref,
    wq_ref,
    wk_ref,
    wv_ref,
    cot_hbm,
    wo_hbm,
    wu_hbm,
    wd_hbm,
    all_ref,
    k_ref,
    kt_ref,
    v_ref,
    q_ref,
    shifted_ref,
    lse_ref,
    rows_ref,
    result_ref,
    gh_ref,
    ga_ref,
    dots_ref,
    small_ref,
    early_hbm,
    rest_ref,
    full,
    all_own,
    k_own,
    kt_own,
    v_own,
    vt_own,
    seg_ref,
    tops,
    totals,
    mixed,
    att_ref,
    cot_ref,
    wo_ref,
    wu_ref,
    wd_ref,
    active_ref,
    gpre_ref,
    gu_slot,
    gd_slot,
    go_slot,
    z_sem,
    y_sem,
    out_sem,
    weight_sem,
    early_sem,
    go_sem,
):
    place = Place(n_seq, n_ray)
    fast_bits = place.fast_bits[::-1]
    greet(place, place.fast_bits)
    block, width = lat_ref.shape
    half_rows = block // 2
    group = place.n_fast * block
    full[place.slow, place.fast] = lat_ref[...]

    def half_at(half):
        return pl.ds(half * half_rows, half_rows)

    def spread(half):
        return Spread(
            place,
            lambda chunk: full.at[chunk, place.fast, half_at(half)],
            lambda way, t: z_sem.at[0, half, way, t],
            lambda way, t: z_sem.at[1, half, way, t],
        )

    def fast_copy(i, chunk, half):
        axis, bit = fast_bits[i]
        mine = full.at[chunk, pl.ds(place.fast // bit * bit, bit), half_at(half)]
        return remote(mine, mine, y_sem.at[0, i, chunk, half], y_sem.at[1, i, chunk, half], place.across(axis, bit))

    def chunk_of(way, t):
        return place.mirrored(way, place.spots[way] - t)

    for half in range(2):
        fast_copy(0, place.slow, half).start()
        spread(half).step(0)

    weight_loads = [
        pltpu.make_async_copy(source, target, weight_sem.at[n])
        for n, (source, target) in enumerate(
            ((wo_hbm, wo_ref), (wu_hbm, wu_ref), (wd_hbm, wd_ref), (cot_hbm, cot_ref))
        )
    ]
    for load in weight_loads:
        load.start()
    for n, vector in enumerate((gain_ref, bias_ref, q_bias_ref, v_bias_ref, out_bias_ref)):
        rows_ref[n : n + 1, :] = vector[...].astype(f32).reshape(1, width)
    rows_ref[5:7, :] = up_bias_ref[...].astype(f32)
    rows_ref[7:8, :] = down_bias_ref[...].astype(f32).reshape(1, width)

    inputs = rays_ref[...].astype(f32)
    centred = inputs - jnp.mean(inputs, axis=1, keepdims=True)
    inverse = lax.rsqrt(jnp.mean(centred * centred, axis=1, keepdims=True) + 1e-05)
    shifted = (centred * inverse * rows_ref[0:1, :] + rows_ref[1:2, :]).astype(bf16)
    shifted_ref[...] = shifted
    queries = (matmul(shifted, wq_ref[...], 1, 0) + rows_ref[2:3, :]).astype(bf16)
    q_ref[...] = (queries.astype(f32) * HEAD ** (-0.5)).astype(bf16)
    tiles, groups = scene_ref.shape[0], width // WIDE
    tops[...] = jnp.full_like(tops, masked_score)
    totals[...] = jnp.zeros_like(totals)
    mixed[...] = jnp.zeros_like(mixed)

    def attend(chunk):
        seg_ref[...] = segments(lengths, chunk * group, group)

        def some_tiles(n, carry):
            own_tiles = [n * FORWARD + i for i in range(FORWARD)]
            scenes = jnp.concatenate([scene_ref[pl.ds(t, 1), :] for t in own_tiles], axis=1)
            seen = jnp.concatenate([seg_ref[...]] * FORWARD, axis=1) == scenes
            scores, old, new = [], [], []
            for g in range(groups):
                spread_q = [
                    spread_heads(q_ref[pl.ds(pl.multiple_of(t * TILE, TILE), TILE), group_at(g)]) for t in own_tiles
                ]
                s = matmul(k_own[:, group_at(g)], jnp.concatenate(spread_q, axis=0), 1, 1)
                scores.append(jnp.where(seen, s, masked_score))
                old.append(jnp.concatenate([tops[g, t] for t in own_tiles], axis=1))
                new.append(jnp.maximum(old[g], jnp.max(fold_rows(scores[g], jnp.max), axis=0, keepdims=True)))
            for g in range(groups):
                fix = jnp.exp(old[g] - new[g])
                e = jnp.exp(scores[g] - new[g][0:1])
                total = fold_rows(e, jnp.sum)
                mix = matmul(vt_own[group_at(g), :], e.astype(bf16), 1, 0)
                for i, t in enumerate(own_tiles):
                    cut = group_at(i)
                    tops[g, t] = new[g][:, cut]
                    totals[g, t] = totals[g, t] * fix[:, cut] + total[:, cut]
                    mixed[g, t] = mixed[g, t] * fix[0:1, cut] + mix[:, cut]
            return carry

        lax.fori_loop(0, tiles // FORWARD, some_tiles, 0)

    def results(chunk):
        rows = pl.ds(pl.multiple_of(chunk * group, 16), group)
        columns = pl.ds(pl.multiple_of(chunk * group, 128), group)
        return [
            (k_own, k_ref.at[rows]),
            (kt_own, kt_ref.at[:, columns]),
            (v_own, v_ref.at[rows]),
            (all_own, all_ref.at[:, columns]),
        ]

    def project(chunk):
        for half in range(2):
            for i in range(len(fast_bits)):
                fast_copy(i, chunk, half).wait()
                if i + 1 < len(fast_bits):
                    fast_copy(i + 1, chunk, half).start()
        latents = full[chunk].reshape(group, width)
        keys = matmul(latents, wk_ref[...], 1, 0).astype(bf16)
        k_own[...] = keys
        all_own[...] = latents.T
        kt_own[...] = keys.T
        values = (matmul(latents, wv_ref[...], 1, 0) + rows_ref[3:4, :]).astype(bf16)
        v_own[...] = values
        vt_own[...] = values.T
        for n, (source, target) in enumerate(results(chunk)):
            pltpu.make_async_copy(source, target, out_sem.at[n]).start()
        attend(chunk)
        for n, (source, target) in enumerate(results(chunk)):
            pltpu.make_async_copy(source, target, out_sem.at[n]).wait()

    def visit(index, carry):
        t, way = index // 2, index % 2
        for later in range(1, SLOW):

            @pl.when(index == 2 * (later - 1))
            def _(later=later):
                for half in range(2):
                    spread(half).step(later)
                    for to in range(2):

                        @pl.when(place.spots[to] >= later)
                        def _(half=half, to=to):
                            fast_copy(0, chunk_of(to, later), half).start()

        spot = jnp.where(way == 0, place.slow, SLOW - 1 - place.slow)
        chunk = jnp.where(way == 0, spot - t, SLOW - 1 - spot + t)

        @pl.when((spot >= t) & (index != 1))
        def _():
            project(chunk)

        return carry

    lax.fori_loop(0, 2 * SLOW, visit, 0)

    for t in range(tiles):
        for g in range(groups):
            total = jnp.sum(totals[g, t], axis=0, keepdims=True)
            att_ref[t * TILE : (t + 1) * TILE, group_at(g)] = fold_heads(mixed[g, t] * (1.0 / total))
            lse_ref[t : t + 1, group_at(g)] = tops[g, t][0:1] + jnp.log(total)

    attended = att_ref[...].astype(bf16)
    weight_loads[0].wait()
    hidden = rays_ref[...].astype(f32) + matmul(attended, wo_ref[...], 1, 0) + rows_ref[4:5, :]
    hidden_low = hidden.astype(bf16)
    hidden_turned = hidden_low.T
    weight_loads[3].wait()
    cot = cot_ref[...]
    inner = wu_ref.shape[1]
    blocks = inner // WIDE
    weight_loads[1].wait()
    weight_loads[2].wait()
    per_half = blocks // 2

    def early_copies(n):
        half, part = n // per_half, n % per_half
        slot = n % 2
        return (
            pltpu.make_async_copy(
                gu_slot.at[slot], early_hbm.at[half, pl.ds(0, width), pl.ds(part * WIDE, WIDE)], early_sem.at[0, slot]
            ),
            pltpu.make_async_copy(
                gd_slot.at[slot], early_hbm.at[half, pl.ds(width + part * WIDE, WIDE)], early_sem.at[1, slot]
            ),
        )

    for n in range(blocks):
        at = slice(n * WIDE, (n + 1) * WIDE)
        bias_row, bias_at = 5 + n * WIDE // width, slice(n * WIDE % width, n * WIDE % width + WIDE)
        pre = matmul(hidden_low, wu_ref[:, at], 1, 0) + rows_ref[bias_row : bias_row + 1, bias_at]
        active, slope = gelu_both(pre)
        active = active.astype(bf16)
        active_ref[:, at] = active
        grad_pre = (matmul(cot, wd_ref[at, :], 1, 1) * slope).astype(bf16)
        gpre_ref[:, at] = grad_pre
        small_ref[bias_row - 4 : bias_row - 3, bias_at] = jnp.sum(grad_pre.astype(f32), axis=0, keepdims=True)
        if n >= 2:
            for copy in early_copies(n - 2):
                copy.wait()
        gu_slot[n % 2] = matmul(hidden_turned, grad_pre, 1, 0).astype(bf16)
        gd_slot[n % 2] = matmul(active, cot, 0, 0).astype(bf16)
        for copy in early_copies(n):
            copy.start()
    result_ref[...] = (hidden + matmul(active_ref[...], wd_ref[...], 1, 0) + rows_ref[7:8, :]).astype(bf16)
    grad_top = cot.astype(f32)
    small_ref[3:4, :] = jnp.sum(grad_top, axis=0, keepdims=True)
    grad_hidden = grad_top + matmul(gpre_ref[...], wu_ref[...], 1, 1)
    gh_ref[...] = grad_hidden
    grad_branch = grad_hidden.astype(bf16)
    small_ref[0:1, :] = jnp.sum(grad_branch.astype(f32), axis=0, keepdims=True)
    small_ref[4:8, :] = jnp.zeros((4, width), f32)
    grad_out = matmul(attended, grad_branch, 0, 0).astype(bf16)
    go_slot[...] = grad_out[: 2 * BLOCK]
    go_copies = [
        pltpu.make_async_copy(
            go_slot.at[pl.ds(c * BLOCK, BLOCK)], early_hbm.at[c, pl.ds(2 * width, BLOCK)], go_sem.at[c]
        )
        for c in range(2)
    ]
    for copy in go_copies:
        copy.start()
    rest_ref[...] = grad_out[2 * BLOCK :]
    grad_attended = matmul(grad_branch, wo_ref[...], 1, 1).astype(bf16)
    ga_ref[...] = grad_attended
    product = grad_attended.astype(f32) * att_ref[...]
    for t in range(dots_ref.shape[0]):
        for g in range(width // WIDE):
            dots_ref[t : t + 1, group_at(g)] = lax.dot_general(
                jnp.ones((8, WIDE), f32),
                spread_heads(product[t * TILE : (t + 1) * TILE, group_at(g)]),
                (((1,), (1,)), ((), ())),
                precision=lax.Precision.HIGHEST,
                preferred_element_type=f32,
            )[0:1, :]
    for copy in early_copies(blocks - 2) + early_copies(blocks - 1) + tuple(go_copies):
        copy.wait()


    for half in range(2):
        spread(half).drain()


def gather_and_attend(
    n_seq, n_ray, rays, latents, lengths, scene_rows, vectors, w_query, w_key, w_value, cotangent, w_out, w_up, w_down
):
    inner = w_up.shape[1]
    block, width = latents.shape
    n_rays = rays.shape[0]
    n_fast = n_ray // SLOW
    group = n_fast * block
    total = n_ray * block
    tiles, groups = n_rays // TILE, width // WIDE
    fast_bits = len(bits_of(n_fast))
    vmem = pltpu.VMEM
    sem = pltpu.SemaphoreType.DMA
    in_vmem = pl.BlockSpec(memory_space=vmem)
    anywhere = pl.BlockSpec(memory_space=pl.ANY)
    struct = jax.ShapeDtypeStruct
    tall, wide = struct((total, width), bf16), struct((width, total), bf16)
    return pl.pallas_call(
        functools.partial(gather_kernel, n_seq, n_ray),
        out_shape=(
            wide,
            tall,
            wide,
            tall,
            struct((n_rays, width), bf16),
            struct((n_rays, width), bf16),
            struct((tiles, width), f32),
            struct((8, width), f32),
            struct((n_rays, width), bf16),
            struct((n_rays, width), f32),
            struct((n_rays, width), bf16),
            struct((tiles, width), f32),
            struct((8, width), f32),
            struct((2, 2 * width + BLOCK, width), bf16),
            struct((width - 2 * BLOCK, width), bf16),
        ),
        in_specs=[pl.BlockSpec(memory_space=pltpu.SMEM)] + [in_vmem] * 13 + [anywhere] * 4,
        out_specs=(anywhere,) * 4 + (in_vmem,) * 9 + (anywhere, in_vmem),
        scratch_shapes=[
            vmem((SLOW, n_fast, block, width), bf16),
            vmem((width, group), bf16),
            vmem((group, width), bf16),
            vmem((width, group), bf16),
            vmem((group, width), bf16),
            vmem((width, group), bf16),
            vmem((group, WIDE), f32),
            vmem((groups, tiles, 8, WIDE), f32),
            vmem((groups, tiles, 8, WIDE), f32),
            vmem((groups, tiles, WIDE, WIDE), f32),
            vmem((n_rays, width), f32),
            vmem((n_rays, width), bf16),
            vmem((width, width), bf16),
            vmem((width, inner), bf16),
            vmem((inner, width), bf16),
            vmem((n_rays, inner), bf16),
            vmem((n_rays, inner), bf16),
            vmem((2, width, WIDE), bf16),
            vmem((2, WIDE, width), bf16),
            vmem((2 * BLOCK, width), bf16),
            sem((2, 2, 2, SLOW - 1)),
            sem((2, fast_bits, SLOW, 2)),
            sem((4,)),
            sem((4,)),
            sem((2, 2)),
            sem((2,)),
        ],
        compiler_params=pltpu.CompilerParams(collective_id=0, has_side_effects=True, vmem_limit_bytes=62 << 20),
        name="gather_and_attend",
    )(lengths, rays, latents, scene_rows, *vectors, w_query, w_key, w_value, cotangent, w_out, w_up, w_down)


def widen_kernel(*refs):
    sums, vectors, wide, lines = refs[:6], refs[6], refs[7:13], refs[13:]
    for source, target in zip(sums, wide):
        target[...] = source[...].astype(f32)
    for n, line in enumerate(lines):
        line[...] = vectors[n, :]


def widen(sums, vectors):
    steps = 6
    width = vectors.shape[1]
    struct = jax.ShapeDtypeStruct
    blocks = [pl.BlockSpec((a.shape[0] // steps, a.shape[1]), lambda i: (i, 0)) for a in sums]
    return pl.pallas_call(
        widen_kernel,
        grid=(steps,),
        out_shape=tuple(struct(a.shape, f32) for a in sums) + (struct((width,), f32),) * vectors.shape[0],
        in_specs=blocks + [pl.BlockSpec(vectors.shape, lambda i: (0, 0))],
        out_specs=tuple(blocks) + (pl.BlockSpec((width,), lambda i: (0,)),) * vectors.shape[0],
        compiler_params=pltpu.CompilerParams(vmem_limit_bytes=62 << 20),
        name="widen",
    )(*sums, vectors)


def local(
    rays,
    latents,
    lengths,
    scenes,
    ln_gain,
    ln_bias,
    w_query,
    b_query,
    w_key,
    w_value,
    b_value,
    w_out,
    b_out,
    w_up,
    b_up,
    w_down,
    b_down,
    cotangent,
):
    width = rays.shape[1]
    n_seq, n_ray = lax.axis_size("seq"), lax.axis_size("ray")
    tiles = rays.shape[0] // TILE
    vectors = (b_up.reshape(-1, width), ln_gain, ln_bias, b_query, b_value, b_out, b_down)
    scene_rows = jnp.broadcast_to(scenes.reshape(tiles, 1, TILE), (tiles, PACK, TILE)).reshape(tiles, WIDE).astype(f32)
    (
        all_t,
        keys,
        keys_t,
        values,
        queries,
        shifted,
        lse,
        rows,
        result,
        grad_hidden,
        grad_attended,
        dots,
        small,
        early,
        rest,
    ) = gather_and_attend(
        n_seq,
        n_ray,
        rays,
        latents,
        lengths,
        scene_rows,
        vectors,
        w_query,
        w_key,
        w_value,
        cotangent,
        w_out,
        w_up,
        w_down,
    )
    sum_q, sum_k, sum_v, sum_o, sum_u, sum_d, grad_latents, grad_rays, small_sums = back_and_sum(
        n_seq,
        n_ray,
        latents.shape[0],
        lengths,
        w_query,
        w_key,
        w_value,
        shifted,
        rays,
        grad_hidden,
        rows,
        small,
        queries,
        grad_attended,
        lse,
        dots,
        scene_rows,
        rest,
        early,
        keys,
        keys_t,
        values,
        all_t,
    )
    wide = widen((sum_q, sum_k, sum_v, sum_o, sum_u, sum_d), small_sums)
    lines = wide[6:]
    return (
        result,
        grad_rays,
        grad_latents,
        lines[4],
        lines[5],
        wide[0],
        lines[6],
        wide[1],
        wide[2],
        lines[7],
        wide[3],
        lines[0],
        wide[4],
        jnp.concatenate(lines[1:3]),
        wide[5],
        lines[3],
    )


def solution(mesh):
    whole = P(("seq", "ray"), None)
    in_specs = (whole, whole, P("seq", None), P(("seq", "ray"))) + (P(),) * 13 + (whole,)
    out_specs = (whole,) * 3 + (P(),) * 13
    return jax.shard_map(local, mesh=mesh, in_specs=in_specs, out_specs=out_specs, check_vma=False)
```

```python
import functools
import math

import jax
import jax.numpy as jnp
from jax import lax
from jax.experimental import pallas as pl
from jax.experimental.pallas import tpu as pltpu
from jax.sharding import PartitionSpec as P

HEADS = 12
HEAD = 64
TILE = 64
WIDE = 256
PACK = WIDE // HEAD
EARLY_WAIT = 2
LATE_CORE, LATE_X, LATE_STEP = 1, 2, 1
LAT_WAIT = 3
FORWARD = 2
PAIR = 3
STEP = 256

masked_score = -1e30
f32 = jnp.float32
bf16 = jnp.bfloat16


def matmul(first_arg, second_arg, first_dim, second_dim):
    return lax.dot_general(
        first_arg,
        second_arg,
        (((first_dim,), (second_dim,)), ((), ())),
        preferred_element_type=jnp.float32,
    )


def own_block():
    row = lax.broadcasted_iota(jnp.int32, (WIDE, WIDE), 0) // TILE
    column = lax.broadcasted_iota(jnp.int32, (WIDE, WIDE), 1) // HEAD
    return row == column


def spread_heads(tile):
    return jnp.where(own_block(), jnp.concatenate([tile] * PACK, axis=0), jnp.zeros((), tile.dtype))


def fold_heads(turned):
    kept = jnp.where(own_block(), turned, 0.0)
    folded = (kept[:, : WIDE // 2] + kept[:, WIDE // 2 :]).T
    return folded[:TILE, :] + folded[TILE:, :]


def fold_rows(block, combine):
    return combine(block.reshape(block.shape[0] // 8, 8, block.shape[1]), axis=0)


def group_at(g):
    return slice(g * WIDE, (g + 1) * WIDE)


def segments(lengths, first, count):
    at = lax.broadcasted_iota(jnp.int32, (count, WIDE), 0) + first
    end, scene = 0, jnp.zeros((count, WIDE), f32)
    for c in range(lengths.shape[1] - 1):
        end = end + lengths[0, c]
        scene = scene + (at >= end).astype(f32)
    return scene


def gelu_both(pre):
    half = 0.5 * (1.0 + lax.erf(pre * math.sqrt(0.5)))
    return pre * half, half + pre * jnp.exp(-0.5 * pre * pre) * (1.0 / math.sqrt(2.0 * math.pi))


MESH = pl.DeviceIdType.MESH
BLOCK = 256
SLOW = 4


def flip(index, bit):
    return index + bit * (1 - 2 * ((index // bit) % 2))


def bits_of(count):
    bits = []
    while count > 1:
        count //= 2
        bits.append(count)
    return bits


def lane_rows(start, size):
    return pl.ds(pl.multiple_of(start, 16), size)


class Place:
    def __init__(self, n_seq, n_ray):
        self.seq = lax.axis_index("seq")
        self.ray = lax.axis_index("ray")
        self.n_fast = n_ray // SLOW
        self.core = self.seq % 2
        self.slow = self.ray // self.n_fast
        self.fast = self.ray % self.n_fast
        self.x_bits = [("seq", 2 * b) for b in bits_of(n_seq // 2)]
        self.fast_bits = [("ray", b) for b in bits_of(self.n_fast)]
        self.slow_bits = [("ray", self.n_fast * b) for b in bits_of(SLOW)]
        self.spots = (self.slow, SLOW - 1 - self.slow)

    def across(self, axis, bit):
        if axis == "seq":
            return (flip(self.seq, bit), self.ray)
        return (self.seq, flip(self.ray, bit))

    def value(self, axis, bit):
        return ((self.seq if axis == "seq" else self.ray) // bit) % 2

    def along(self, way):
        return (self.seq, self.ray + (self.n_fast if way == 0 else -self.n_fast))

    def after(self, step):
        return (self.seq, (self.slow + step) % SLOW * self.n_fast + self.fast)

    def mirrored(self, way, chunk):
        return chunk if way == 0 else SLOW - 1 - chunk


def remote(src, dst, send_sem, recv_sem, device):
    return pltpu.make_async_remote_copy(
        src_ref=src,
        dst_ref=dst,
        send_sem=send_sem,
        recv_sem=recv_sem,
        device_id=device,
        device_id_type=MESH,
    )


def greet(place, exchanges):
    barrier = pltpu.get_barrier_semaphore()
    for axis, bit in exchanges:
        pl.semaphore_signal(barrier, inc=1, device_id=place.across(axis, bit), device_id_type=MESH)
    for step in range(1, SLOW):
        pl.semaphore_signal(barrier, inc=1, device_id=place.after(step), device_id_type=MESH)
    pl.semaphore_wait(barrier, len(exchanges) + SLOW - 1)


class Line:
    def __init__(self, place, block, recv, send_sem, recv_sem):
        self.place, self.block, self.recv, self.send_sem, self.recv_sem = place, block, recv, send_sem, recv_sem

    def copy(self, way, t, to):
        chunk = self.place.mirrored(way, SLOW - 1 - (t - self.place.spots[way]))
        return remote(
            self.block(chunk), self.recv(way, t), self.send_sem(way, t), self.recv_sem(way, t), self.place.along(to)
        )

    def landed(self, way, t):
        remote(
            self.recv(way, t), self.recv(way, t), self.send_sem(way, t), self.recv_sem(way, t), self.place.along(1 - way)
        ).wait_recv()
        return self.recv(way, t)[...].astype(f32)

    def step(self, t):
        for way in range(2):
            spot = self.place.spots[way]

            @pl.when((spot <= t) & (spot < SLOW - 1))
            def _(way=way, spot=spot):
                if t > 0:

                    @pl.when(spot > 0)
                    def _():
                        block = self.block(self.place.mirrored(way, SLOW - 1 - (t - spot)))
                        block[...] = (block[...].astype(f32) + self.landed(way, t - 1)).astype(bf16)

                self.copy(way, t, way).start()

    def last(self, total):
        total[...] = self.block(self.place.slow)[...].astype(f32)
        for way in range(2):

            @pl.when(self.place.spots[way] > 0)
            def _(way=way):
                total[...] += self.landed(way, SLOW - 2)

    def drain(self):
        for way in range(2):
            for t in range(SLOW - 1):
                spot = self.place.spots[way]

                @pl.when((spot <= t) & (spot < SLOW - 1))
                def _(way=way, t=t):
                    self.copy(way, t, way).wait_send()


class Spread:
    def __init__(self, place, block, send_sem, recv_sem):
        self.place, self.block, self.send_sem, self.recv_sem = place, block, send_sem, recv_sem

    def copy(self, way, t, to):
        chunk = self.place.mirrored(way, self.place.spots[way] - t)
        block = self.block(chunk)
        return remote(block, block, self.send_sem(way, t), self.recv_sem(way, t), self.place.along(to))

    def step(self, t):
        for way in range(2):
            spot = self.place.spots[way]

            @pl.when(spot >= t)
            def _(way=way, spot=spot):
                if t > 0:
                    block = self.block(self.place.mirrored(way, spot - t))
                    remote(
                        block, block, self.send_sem(way, t - 1), self.recv_sem(way, t - 1), self.place.along(1 - way)
                    ).wait_recv()
                if t < SLOW - 1:

                    @pl.when(spot < SLOW - 1)
                    def _():
                        self.copy(way, t, way).start()

    def drain(self):
        for way in range(2):
            for t in range(SLOW - 1):
                spot = self.place.spots[way]

                @pl.when((spot >= t) & (spot < SLOW - 1))
                def _(way=way, t=t):
                    self.copy(way, t, way).wait_send()


def units_of(rows, n_x, n_fast):
    share = n_x * n_fast * SLOW * 16
    return rows // BLOCK if BLOCK % share == 0 else 1


def sum_kernel(
    n_seq,
    n_ray,
    units,
    lengths,
    rows_ref,
    small_ref,
    q_ref,
    g_ref,
    lse_ref,
    dots_ref,
    scene_ref,
    rest_ref,
    wq_hbm,
    wk_hbm,
    wv_hbm,
    shifted_hbm,
    rays_hbm,
    gh_hbm,
    early_hbm,
    k_hbm,
    kt_hbm,
    v_hbm,
    all_hbm,
    o_q,
    o_k,
    o_v,
    o_o,
    o_u,
    o_d,
    glat_ref,
    grays_ref,
    small_out,
    wq_ref,
    wk_ref,
    wv_ref,
    shifted_ref,
    rays_ref,
    k_slot,
    kt_slot,
    v_slot,
    all_slot,
    seg_ref,
    sum_kv,
    grads_kv,
    weights_kv,
    turned_q,
    gq_ref,
    own,
    other,
    full,
    rx,
    z_recv,
    lat,
    lat_recv,
    lz_recv,
    small_now,
    small_recv,
    early_sem,
    slot_sem,
    core_sem,
    halve_sem,
    z_sem,
    zg_sem,
    double_sem,
    back_sem,
    out_sem,
    lat_sem,
    lz_sem,
    small_sem,
):
    place = Place(n_seq, n_ray)
    core_pair = ("seq", 1)
    halvings = place.x_bits + place.fast_bits
    exchanges = [core_pair] + halvings + place.slow_bits
    core = place.core
    rows, width = own.shape
    late_from = early_hbm.shape[1]
    unit_rows = rows // units
    early_units = late_from // unit_rows
    sizes = [unit_rows >> i for i in range(len(halvings) + 1)]
    share = sizes[-1]
    line = share % (16 * SLOW) == 0
    piece = share // SLOW if line else share

    early_load = pltpu.make_async_copy(early_hbm.at[core], own.at[pl.ds(0, late_from)], early_sem.at[0])
    early_load.start()
    gh_load = pltpu.make_async_copy(gh_hbm, grays_ref, early_sem.at[1])
    gh_load.start()
    late_loads = [
        pltpu.make_async_copy(source, target, early_sem.at[2 + n])
        for n, (source, target) in enumerate(
            (
                (wq_hbm, wq_ref),
                (wk_hbm, wk_ref),
                (wv_hbm, wv_ref),
                (shifted_hbm, shifted_ref),
                (rays_hbm, rays_ref),
            )
        )
    ]
    greet(place, [core_pair] + halvings)

    def base(u, stages):
        start = u * unit_rows
        for i in range(stages):
            start = start + place.value(*halvings[i]) * sizes[i + 1]
        return start

    def unit(u):
        return lane_rows(u * unit_rows, unit_rows)

    def core_parts(u):
        if units == 1:
            rows_of = (pl.ds(0, late_from), pl.ds(0, rows - late_from))
            when = (u == 0, u == 0)
            into = (pl.ds(0, late_from), pl.ds(late_from, rows - late_from))
        else:
            rows_of = (unit(u), lane_rows(u * unit_rows - late_from, unit_rows))
            when = (u < early_units, u >= early_units)
            into = (unit(u), unit(u))
        sources = (early_hbm.at[1 - core, rows_of[0]], other.at[rows_of[1]])
        return [
            (
                when[n],
                remote(
                    sources[n], full.at[into[n]], core_sem.at[0, n, u], core_sem.at[1, n, u], place.across(*core_pair)
                ),
            )
            for n in range(2)
        ]

    def halve_copy(i, u):
        size = sizes[i + 1]
        sent = base(u, i) + (1 - place.value(*halvings[i])) * size
        return remote(
            own.at[lane_rows(sent, size)],
            rx[i].at[lane_rows(u * size, size)],
            halve_sem.at[0, i, u],
            halve_sem.at[1, i, u],
            place.across(*halvings[i]),
        )

    def start_core(u):
        for when, copy in core_parts(u):

            @pl.when(when)
            def _(copy=copy):
                copy.start()

    def join_core(u):
        for when, copy in core_parts(u):

            @pl.when(when)
            def _(copy=copy):
                copy.wait()

        own[unit(u), :] = (own[unit(u), :].astype(f32) + full[unit(u), :].astype(f32)).astype(bf16)
        halve_copy(0, u).start()

    def join_half(i):
        def run(u):
            size = sizes[i + 1]
            halve_copy(i, u).wait()
            kept = lane_rows(base(u, i + 1), size)
            own[kept, :] = (own[kept, :].astype(f32) + rx[i][lane_rows(u * size, size), :].astype(f32)).astype(bf16)
            if i + 1 < len(halvings):
                halve_copy(i + 1, u).start()

        return run

    def z_rows(u, chunk):
        return lane_rows(base(u, len(halvings)) + chunk * piece, piece)

    def z_copy(u, step):
        return remote(
            own.at[z_rows(u, (place.slow + step) % SLOW)],
            z_recv.at[u, step - 1],
            z_sem.at[0, u, step - 1],
            z_sem.at[1, u, step - 1],
            place.after(step),
        )

    def z_back_copy(u, step, chunk):
        block = full.at[z_rows(u, chunk)]
        return remote(block, block, zg_sem.at[0, u, step - 1], zg_sem.at[1, u, step - 1], place.after(step))

    def start_z(u):
        for step in range(1, SLOW):
            z_copy(u, step).start()

    def join_z(u):
        total = own[z_rows(u, place.slow), :].astype(f32)
        for step in range(1, SLOW):
            z_copy(u, step).wait()
            total = total + z_recv[u, step - 1].astype(f32)
        full[z_rows(u, place.slow), :] = total.astype(bf16)
        for step in range(1, SLOW):
            z_back_copy(u, step, place.slow).start()

    def join_z_back(u):
        for step in range(1, SLOW):
            z_back_copy(u, step, place.slow).wait_send()
            z_back_copy(u, step, (place.slow + SLOW - step) % SLOW).wait_recv()

    def whole_copy(i, u):
        return remote(
            own.at[lane_rows(base(u, len(halvings)), share)],
            z_recv.at[u, i],
            z_sem.at[0, u, i],
            z_sem.at[1, u, i],
            place.across(*place.slow_bits[i]),
        )

    def whole_step(i):
        def run(u):
            mine = lane_rows(base(u, len(halvings)), share)
            if i > 0:
                whole_copy(i - 1, u).wait()
                own[mine, :] = (own[mine, :].astype(f32) + z_recv[u, i - 1].astype(f32)).astype(bf16)
            if i < len(place.slow_bits):
                whole_copy(i, u).start()
            else:
                full[mine, :] = own[mine, :]

        return run

    def double_copy(i, u):
        block = full.at[lane_rows(base(u, i + 1), sizes[i + 1])]
        return remote(block, block, double_sem.at[0, i, u], double_sem.at[1, i, u], place.across(*halvings[i]))

    def targets(n, c):
        per = width // BLOCK
        part, at = n // per, n % per
        rows_at = pl.ds(pl.multiple_of(at * BLOCK, BLOCK), BLOCK)
        after = pl.ds(pl.multiple_of((n + per - 1) % per * BLOCK, BLOCK), BLOCK)
        half_at = pl.ds(pl.multiple_of(c * width, 128), width)
        lower = pl.ds(pl.multiple_of(c * width + at * BLOCK, BLOCK), BLOCK)
        last = pl.ds(2 * BLOCK, BLOCK)
        return [
            (part == 0, o_u.at[rows_at, half_at]),
            (part == 1, o_d.at[lower]),
            (n == 2 * per, o_o.at[pl.ds(pl.multiple_of(c * BLOCK, BLOCK), BLOCK)]),
            ((n > 2 * per) & (n <= 3 * per) & (c == 0), o_k.at[after]),
            ((n > 2 * per) & (n <= 3 * per) & (c == 1), o_v.at[after]),
            ((n == 3 * per + 1) & (c == 0), o_o.at[last]),
            ((n == 3 * per + 1) & (c == 1), o_q.at[pl.ds(0, BLOCK)]),
            (n == 3 * per + 2, o_q.at[pl.ds(pl.multiple_of((1 + c) * BLOCK, BLOCK), BLOCK)]),
        ]

    def block_rows(n):
        return lane_rows(n * BLOCK, BLOCK)

    def blocks_of(u):
        return [u] if units > 1 else list(range(rows // BLOCK))

    def send_block(n):
        for when, target in targets(n, core):

            @pl.when(when)
            def _(target=target):
                source = full.at[block_rows(n)]
                remote(source, target, back_sem.at[0, n], back_sem.at[1, n], place.across(*core_pair)).start()
                pltpu.make_async_copy(source, target, out_sem.at[n]).start()

    def end_block(n):
        for when, target in targets(n, core):

            @pl.when(when)
            def _(target=target):
                source = full.at[block_rows(n)]
                remote(source, target, back_sem.at[0, n], back_sem.at[1, n], place.across(*core_pair)).wait_send()
                pltpu.make_async_copy(source, target, out_sem.at[n]).wait()

        for when, target in targets(n, 1 - core):

            @pl.when(when)
            def _(target=target):
                source = full.at[block_rows(n)]
                remote(source, target, back_sem.at[0, n], back_sem.at[1, n], place.across(*core_pair)).wait_recv()

    def start_double(u):
        double_copy(len(halvings) - 1, u).start()

    def join_double(i):
        def run(u):
            double_copy(i, u).wait()
            if i > 0:
                double_copy(i - 1, u).start()
            else:
                for n in blocks_of(u):
                    send_block(n)

        return run

    def finish_unit(u):
        for n in blocks_of(u):
            end_block(n)

    stages = [[start_core], [join_core]] + [[join_half(i)] for i in range(len(halvings))]
    if line:
        stages[-1].append(start_z)
        stages += [[join_z], [join_z_back]]
    else:
        stages[-1].append(whole_step(0))
        stages += [[whole_step(i)] for i in range(1, len(place.slow_bits) + 1)]
    stages[-1].append(start_double)
    stages += [[join_double(i)] for i in reversed(range(len(halvings)))]
    stages += [[finish_unit]]

    n_fast, block = lat.shape[1:3]
    group = n_fast * block
    half_rows = block // 2
    fast_sizes = [n_fast >> i for i in range(len(place.fast_bits) + 1)]

    def chunk_of(k):
        near = jnp.minimum(place.slow, SLOW - 1 - place.slow)
        ahead = SLOW - 1 - near
        chunk = jnp.where(k < ahead, SLOW - 1 - k, jnp.where(k - ahead < near, k - ahead, near))
        return jnp.where(place.slow == near, chunk, SLOW - 1 - chunk)

    def lat_base(stages):
        start = 0
        for i in range(stages):
            start = start + place.value(*place.fast_bits[i]) * fast_sizes[i + 1]
        return start

    def lat_half(m):
        return lane_rows((m % 2) * half_rows, half_rows)

    def lat_copy(i, m):
        size = fast_sizes[i + 1]
        sent = lat_base(i) + (1 - place.value(*place.fast_bits[i])) * size
        return remote(
            lat.at[chunk_of(m // 2), pl.ds(sent, size), lat_half(m)],
            lat_recv[i].at[m],
            lat_sem.at[0, i, m],
            lat_sem.at[1, i, m],
            place.across(*place.fast_bits[i]),
        )

    def start_lat(m):
        lat_copy(0, m).start()

    def lat_line(m):
        half = m % 2
        return Line(
            place,
            lambda chunk: lat.at[chunk, place.fast, lat_half(m)],
            lambda way, t: lz_recv.at[half, way, t],
            lambda way, t: lz_sem.at[0, half, way, t],
            lambda way, t: lz_sem.at[1, half, way, t],
        )

    def join_lat(i):
        def run(m):
            lat_copy(i, m).wait()
            kept = lat.at[chunk_of(m // 2), pl.ds(lat_base(i + 1), fast_sizes[i + 1]), lat_half(m)]
            kept[...] = (kept[...].astype(f32) + lat_recv[i][m].astype(f32)).astype(bf16)
            if i + 1 < len(place.fast_bits):
                lat_copy(i + 1, m).start()
            else:
                for t in range(SLOW - 1):

                    @pl.when(m // 2 == t)
                    def _(t=t):
                        lat_line(m).step(t)

        return run

    def finish_lat(m):
        @pl.when(m // 2 == SLOW - 1)
        def _():
            lat_line(m).last(glat_ref.at[lat_half(m)])
            lat_line(m).drain()

    lat_stages = [start_lat] + [join_lat(i) for i in range(len(place.fast_bits))] + [finish_lat]

    def small_copy(i):
        axis, bit = exchanges[i]
        return remote(
            small_now.at[i], small_recv.at[i], small_sem.at[0, i], small_sem.at[1, i], place.across(axis, bit)
        )

    def start_small():
        small_copy(0).start()

    def join_small(i):
        def run():
            small_copy(i).wait()
            small_now[i + 1] = small_now[i] + small_recv[i]
            if i + 1 < len(exchanges):
                small_copy(i + 1).start()

        return run

    tiles, groups = scene_ref.shape[0], width // WIDE
    pairs, parts = tiles // PAIR, group // STEP
    per_chunk = pairs * parts

    def slot_loads(k):
        chunk = chunk_of(k)
        at, columns = lane_rows(chunk * group, group), pl.ds(pl.multiple_of(chunk * group, 128), group)
        return (
            pltpu.make_async_copy(k_hbm.at[at], k_slot, slot_sem.at[0]),
            pltpu.make_async_copy(kt_hbm.at[:, columns], kt_slot, slot_sem.at[1]),
            pltpu.make_async_copy(v_hbm.at[at], v_slot, slot_sem.at[2]),
        )

    def all_load(k):
        columns = pl.ds(pl.multiple_of(chunk_of(k) * group, 128), group)
        return pltpu.make_async_copy(all_hbm.at[:, columns], all_slot, slot_sem.at[3])

    def open_chunk(k):
        for load in slot_loads(k):
            load.wait()

        all_load(k).start()
        seg_ref[...] = segments(lengths, chunk_of(k) * group, group)
        sum_kv[...] = jnp.zeros_like(sum_kv)

    def tile_rows(t):
        return pl.ds(pl.multiple_of(t * TILE, TILE), TILE)

    def back_step(pair, part):
        at = pl.ds(pl.multiple_of(part * STEP, 128), STEP)
        own_tiles = [pair * PAIR + i for i in range(PAIR)]
        seen = jnp.concatenate([seg_ref[at, :]] * PAIR, axis=1) == jnp.concatenate(
            [scene_ref[pl.ds(t, 1), :] for t in own_tiles], axis=1
        )
        for g in range(groups):
            to = group_at(g)
            q_spread = jnp.concatenate([spread_heads(q_ref[tile_rows(t), to]) for t in own_tiles], axis=0)
            g_spread = jnp.concatenate([spread_heads(g_ref[tile_rows(t), to]) for t in own_tiles], axis=0)
            lse = jnp.concatenate([lse_ref[pl.ds(t, 1), to] for t in own_tiles], axis=1)
            dots = jnp.concatenate([dots_ref[pl.ds(t, 1), to] for t in own_tiles], axis=1)
            s = matmul(k_slot[at, to], q_spread, 1, 1)
            p = jnp.where(seen, jnp.exp(s - lse), 0.0)
            sum_kv[1, at, to] += matmul(p.astype(bf16), g_spread, 1, 0)
            gp = matmul(v_slot[at, to], g_spread, 1, 1)
            gs = (p * (gp - dots)).astype(bf16)
            sum_kv[0, at, to] += matmul(gs, q_spread, 1, 0)
            turned_q[g, pair] += matmul(kt_slot[to, at], gs, 1, 0)

    def close_chunk(k):
        @pl.when(k + 1 < SLOW)
        def _():
            for load in slot_loads(k + 1):
                load.start()

        @pl.when(k == 0)
        def _():
            for load in late_loads:
                load.wait()

        grads_kv[...] = sum_kv[...].astype(bf16)
        total = matmul(grads_kv[0], wk_ref[...], 1, 1) + matmul(grads_kv[1], wv_ref[...], 1, 1)
        lat[chunk_of(k)] = total.astype(bf16).reshape(n_fast, block, width)
        all_load(k).wait()
        for n in range(2):
            weights_kv[n] += matmul(all_slot[...], grads_kv[n], 1, 0)
        small_now[0, 7:8] += jnp.sum(grads_kv[1].astype(f32), axis=0, keepdims=True)

    def attend(step):
        k, part_of = step // per_chunk, step % per_chunk

        @pl.when(part_of == 0)
        def _():
            open_chunk(k)

        back_step(part_of // parts, part_of % parts)

        @pl.when(part_of == per_chunk - 1)
        def _():
            close_chunk(k)

    def key_terms():
        own[late_from : late_from + width, :] = weights_kv[core].astype(bf16)
        other[:width, :] = weights_kv[1 - core].astype(bf16)

    def query_terms():
        for t in range(tiles):
            for g in range(groups):
                turned = turned_q[g, t // PAIR, :, t % PAIR * WIDE : (t % PAIR + 1) * WIDE]
                gq_ref[t * TILE : (t + 1) * TILE, group_at(g)] = (fold_heads(turned) * HEAD ** (-0.5)).astype(bf16)

    def query_weight_terms():
        terms = matmul(shifted_ref[...], gq_ref[...], 0, 0).astype(bf16)
        first, second, third = [terms[b * BLOCK : (b + 1) * BLOCK] for b in range(width // BLOCK)]
        after = late_from + width

        @pl.when(core == 0)
        def _():
            own[after : after + BLOCK, :] = rest_ref[...]
            own[after + BLOCK :, :] = second
            other[width : width + BLOCK, :] = first
            other[width + BLOCK :, :] = third

        @pl.when(core == 1)
        def _():
            own[after : after + BLOCK, :] = first
            own[after + BLOCK :, :] = third
            other[width : width + BLOCK, :] = rest_ref[...]
            other[width + BLOCK :, :] = second

    def ray_terms():
        inputs = rays_ref[...].astype(f32)
        centred = inputs - jnp.mean(inputs, axis=1, keepdims=True)
        inverse = lax.rsqrt(jnp.mean(centred * centred, axis=1, keepdims=True) + 1e-05)
        normed = centred * inverse
        grad_shifted = matmul(gq_ref[...], wq_ref[...], 1, 1)
        grad_normed = grad_shifted * rows_ref[0:1, :]
        gh_load.wait()
        grays_ref[...] += inverse * (
            grad_normed
            - jnp.mean(grad_normed, axis=1, keepdims=True)
            - normed * jnp.mean(grad_normed * normed, axis=1, keepdims=True)
        )
        small_now[0, 4:5] = jnp.sum(grad_shifted * normed, axis=0, keepdims=True)
        small_now[0, 5:6] = jnp.sum(grad_shifted, axis=0, keepdims=True)
        small_now[0, 6:7] = jnp.sum(gq_ref[...].astype(f32), axis=0, keepdims=True)

    for load in slot_loads(0) + tuple(late_loads):
        load.start()
    turned_q[...] = jnp.zeros_like(turned_q)
    weights_kv[...] = jnp.zeros_like(weights_kv)
    small_now[0] = small_ref[...]
    early_load.wait()

    steps = SLOW * per_chunk
    late_start = steps if units > 1 else steps + 3
    finish = [key_terms, query_terms, query_weight_terms, ray_terms]
    work = {steps - 1 + n: [run] for n, run in enumerate(finish)}
    for i in range(len(exchanges)):
        work.setdefault(steps + len(finish) + i, []).append(join_small(i))
    work[steps + len(finish) - 2].append(start_small)
    lat_wait = LAT_WAIT
    late_waits = [0, LATE_CORE] + [LATE_X] + [LATE_STEP] * (len(stages) - 5) + [LATE_X, 1]
    late_at = [sum(late_waits[: n + 1]) for n in range(len(stages))]
    lat_span = steps + 2 + lat_wait * (len(lat_stages) - 1)
    beats = max(late_start + units - early_units + late_at[-1], lat_span, max(work) + 1)

    def one_beat(now, carry):
        for s in range(len(stages)):
            early = now - EARLY_WAIT * s
            late = now - late_start - late_at[s]
            u = jnp.where(late >= 0, late + early_units, early)

            @pl.when(((late >= 0) & (u < units)) | ((early >= 0) & (early < early_units)))
            def _(u=u, s=s):
                for run in stages[s]:
                    run(u)

        for s in range(len(lat_stages)):
            ahead = now - per_chunk - lat_wait * s
            m = ahead // per_chunk * 2 + ahead % per_chunk

            @pl.when((ahead >= 0) & (ahead % per_chunk < 2) & (m < 2 * SLOW))
            def _(m=m, s=s):
                lat_stages[s](m)

        @pl.when(now < steps)
        def _():
            attend(now)

        for beat, runs in work.items():

            @pl.when(now == beat)
            def _(runs=runs):
                for run in runs:
                    run()

        return carry

    lax.fori_loop(0, beats, one_beat, 0)
    small_out[...] = small_now[len(exchanges)]


def back_and_sum(
    n_seq,
    n_ray,
    block,
    lengths,
    w_query,
    w_key,
    w_value,
    shifted,
    rays,
    gh,
    rows,
    small,
    queries,
    ga,
    lse,
    dots,
    scene_rows,
    rest,
    early,
    keys,
    keys_t,
    values,
    all_t,
):
    n_fast = n_ray // SLOW
    n_x = n_seq // 2
    n_rays, width = rays.shape
    group = n_fast * block
    groups, pairs = width // WIDE, n_rays // TILE // PAIR
    sum_rows = 4 * width
    late_rows = sum_rows - early.shape[1]
    units = units_of(sum_rows, n_x, n_fast)
    halvings = len(bits_of(n_x)) + len(bits_of(n_fast))
    fast_bits = len(bits_of(n_fast))
    exchanges = 1 + halvings + len(bits_of(SLOW))
    share = sum_rows // units >> halvings
    piece = share // SLOW if share % (16 * SLOW) == 0 else share
    half = block // 2
    vmem = pltpu.VMEM
    sem = pltpu.SemaphoreType.DMA
    struct = jax.ShapeDtypeStruct
    in_vmem = pl.BlockSpec(memory_space=vmem)
    anywhere = pl.BlockSpec(memory_space=pl.ANY)
    return pl.pallas_call(
        functools.partial(sum_kernel, n_seq, n_ray, units),
        out_shape=(
            struct((width, width), bf16),
            struct((width, width), bf16),
            struct((width, width), bf16),
            struct((width, width), bf16),
            struct((width, 2 * width), bf16),
            struct((2 * width, width), bf16),
            struct((block, width), f32),
            struct((n_rays, width), f32),
            struct((8, width), f32),
        ),
        in_specs=[pl.BlockSpec(memory_space=pltpu.SMEM)] + [in_vmem] * 8 + [anywhere] * 11,
        out_specs=(anywhere,) * 6 + (in_vmem,) * 3,
        scratch_shapes=[
            vmem((width, width), bf16),
            vmem((width, width), bf16),
            vmem((width, width), bf16),
            vmem((n_rays, width), bf16),
            vmem((n_rays, width), bf16),
            vmem((group, width), bf16),
            vmem((width, group), bf16),
            vmem((group, width), bf16),
            vmem((width, group), bf16),
            vmem((group, WIDE), f32),
            vmem((2, group, width), f32),
            vmem((2, group, width), bf16),
            vmem((2, width, width), f32),
            vmem((groups, pairs, WIDE, PAIR * WIDE), f32),
            vmem((n_rays, width), bf16),
            vmem((sum_rows, width), bf16),
            vmem((late_rows, width), bf16),
            vmem((sum_rows, width), bf16),
            [vmem((sum_rows >> (i + 1), width), bf16) for i in range(halvings)],
            vmem((units, SLOW - 1, piece, width), bf16),
            vmem((SLOW, n_fast, block, width), bf16),
            [vmem((2 * SLOW, n_fast >> (i + 1), half, width), bf16) for i in range(fast_bits)],
            vmem((2, 2, SLOW - 1, half, width), bf16),
            vmem((exchanges + 1, 8, width), f32),
            vmem((exchanges, 8, width), f32),
            sem((7,)),
            sem((4,)),
            sem((2, 2, units)),
            sem((2, halvings, units)),
            sem((2, units, SLOW - 1)),
            sem((2, units, SLOW - 1)),
            sem((2, halvings, units)),
            sem((2, sum_rows // BLOCK)),
            sem((sum_rows // BLOCK,)),
            sem((2, fast_bits, 2 * SLOW)),
            sem((2, 2, 2, SLOW - 1)),
            sem((2, exchanges)),
        ],
        compiler_params=pltpu.CompilerParams(collective_id=1, has_side_effects=True, vmem_limit_bytes=63 << 20),
        name="back_and_sum",
    )(
        lengths,
        rows,
        small,
        queries,
        ga,
        lse,
        dots,
        scene_rows,
        rest,
        w_query,
        w_key,
        w_value,
        shifted,
        rays,
        gh,
        early,
        keys,
        keys_t,
        values,
        all_t,
    )


def gather_kernel(
    n_seq,
    n_ray,
    lengths,
    lat_ref,
    scenes_ref,
    up_bias_ref,
    gain_ref,
    bias_ref,
    q_bias_ref,
    v_bias_ref,
    out_bias_ref,
    down_bias_ref,
    rays_hbm,
    wq_hbm,
    wk_hbm,
    wv_hbm,
    cot_hbm,
    wo_hbm,
    wu_hbm,
    wd_hbm,
    all_ref,
    k_ref,
    kt_ref,
    v_ref,
    q_ref,
    shifted_ref,
    lse_ref,
    scene_ref,
    rows_ref,
    result_ref,
    gh_ref,
    ga_ref,
    dots_ref,
    small_ref,
    early_hbm,
    rest_ref,
    full,
    all_own,
    k_own,
    kt_own,
    v_own,
    vt_own,
    seg_ref,
    tops,
    totals,
    mixed,
    att_ref,
    rays_ref,
    wq_ref,
    wk_ref,
    wv_ref,
    cot_ref,
    wo_ref,
    wu_ref,
    wd_ref,
    active_ref,
    gpre_ref,
    gu_slot,
    gd_slot,
    go_slot,
    z_sem,
    y_sem,
    out_sem,
    weight_sem,
    early_sem,
    go_sem,
):
    place = Place(n_seq, n_ray)
    fast_bits = place.fast_bits[::-1]
    weight_loads = [
        pltpu.make_async_copy(source, target, weight_sem.at[n])
        for n, (source, target) in enumerate(
            (
                (wo_hbm, wo_ref),
                (wu_hbm, wu_ref),
                (wd_hbm, wd_ref),
                (cot_hbm, cot_ref),
                (rays_hbm, rays_ref),
                (wq_hbm, wq_ref),
                (wk_hbm, wk_ref),
                (wv_hbm, wv_ref),
            )
        )
    ]
    for load in weight_loads[4:] + weight_loads[:4]:
        load.start()
    greet(place, place.fast_bits)
    block, width = lat_ref.shape
    half_rows = block // 2
    group = place.n_fast * block
    full[place.slow, place.fast] = lat_ref[...]
    step = k_own.shape[0]
    by_block = step == block

    def half_at(half):
        return pl.ds(half * half_rows, half_rows)

    def spread(half):
        return Spread(
            place,
            lambda chunk: full.at[chunk, place.fast, half_at(half)],
            lambda way, t: z_sem.at[0, half, way, t],
            lambda way, t: z_sem.at[1, half, way, t],
        )

    def fast_copy(i, chunk, half):
        axis, bit = fast_bits[i]
        mine = full.at[chunk, pl.ds(place.fast // bit * bit, bit), half_at(half)]
        return remote(mine, mine, y_sem.at[0, i, chunk, half], y_sem.at[1, i, chunk, half], place.across(axis, bit))

    def chunk_of(way, t):
        return place.mirrored(way, place.spots[way] - t)

    for half in range(2):
        fast_copy(0, place.slow, half).start()
        spread(half).step(0)

    for n, vector in enumerate((gain_ref, bias_ref, q_bias_ref, v_bias_ref, out_bias_ref)):
        rows_ref[n : n + 1, :] = vector[...].astype(f32).reshape(1, width)
    up_bias = up_bias_ref[...].astype(f32).reshape(1, -1)
    for n in range(2):
        rows_ref[5 + n : 6 + n, :] = up_bias[:, n * width : (n + 1) * width]
    rows_ref[7:8, :] = down_bias_ref[...].astype(f32).reshape(1, width)

    scenes = scenes_ref[...].astype(f32).reshape(1, -1)
    for t in range(scene_ref.shape[0]):
        scene_ref[t : t + 1, :] = jnp.concatenate([scenes[:, t * TILE : (t + 1) * TILE]] * PACK, axis=1)

    for load in weight_loads[4:]:
        load.wait()
    inputs = rays_ref[...].astype(f32)
    centred = inputs - jnp.mean(inputs, axis=1, keepdims=True)
    inverse = lax.rsqrt(jnp.mean(centred * centred, axis=1, keepdims=True) + 1e-05)
    shifted = (centred * inverse * rows_ref[0:1, :] + rows_ref[1:2, :]).astype(bf16)
    shifted_ref[...] = shifted
    queries = (matmul(shifted, wq_ref[...], 1, 0) + rows_ref[2:3, :]).astype(bf16)
    q_ref[...] = (queries.astype(f32) * HEAD ** (-0.5)).astype(bf16)
    tiles, groups = scene_ref.shape[0], width // WIDE
    tops[...] = jnp.full_like(tops, masked_score)
    totals[...] = jnp.zeros_like(totals)
    mixed[...] = jnp.zeros_like(mixed)

    def attend(first):
        seg_ref[...] = segments(lengths, first, step)

        def some_tiles(n, carry):
            own_tiles = [n * FORWARD + i for i in range(FORWARD)]
            scenes = jnp.concatenate([scene_ref[pl.ds(t, 1), :] for t in own_tiles], axis=1)
            seen = jnp.concatenate([seg_ref[...]] * FORWARD, axis=1) == scenes
            scores, old, new = [], [], []
            for g in range(groups):
                spread_q = [
                    spread_heads(q_ref[pl.ds(pl.multiple_of(t * TILE, TILE), TILE), group_at(g)]) for t in own_tiles
                ]
                s = matmul(k_own[:, group_at(g)], jnp.concatenate(spread_q, axis=0), 1, 1)
                scores.append(jnp.where(seen, s, masked_score))
                old.append(jnp.concatenate([tops[g, t] for t in own_tiles], axis=1))
                new.append(jnp.maximum(old[g], jnp.max(fold_rows(scores[g], jnp.max), axis=0, keepdims=True)))
            for g in range(groups):
                fix = jnp.exp(old[g] - new[g])
                e = jnp.exp(scores[g] - new[g][0:1])
                total = fold_rows(e, jnp.sum)
                mix = matmul(vt_own[group_at(g), :], e.astype(bf16), 1, 0)
                for i, t in enumerate(own_tiles):
                    cut = group_at(i)
                    tops[g, t] = new[g][:, cut]
                    totals[g, t] = totals[g, t] * fix[:, cut] + total[:, cut]
                    mixed[g, t] = mixed[g, t] * fix[0:1, cut] + mix[:, cut]
            return carry

        lax.fori_loop(0, tiles // FORWARD, some_tiles, 0)

    def results(first):
        rows = pl.ds(pl.multiple_of(first, 16), step)
        columns = pl.ds(pl.multiple_of(first, 128), step)
        return [
            (k_own, k_ref.at[rows]),
            (kt_own, kt_ref.at[:, columns]),
            (v_own, v_ref.at[rows]),
            (all_own, all_ref.at[:, columns]),
        ]

    def await_fast(chunk):
        for half in range(2):
            for i in range(len(fast_bits)):
                fast_copy(i, chunk, half).wait()
                if i + 1 < len(fast_bits):
                    fast_copy(i + 1, chunk, half).start()

    def project(chunk, fast):
        if by_block:
            first, latents = chunk * group + fast * block, full[chunk, fast]
        else:
            first, latents = chunk * group, full[chunk].reshape(group, width)
        keys = matmul(latents, wk_ref[...], 1, 0).astype(bf16)
        k_own[...] = keys
        all_own[...] = latents.T
        kt_own[...] = keys.T
        values = (matmul(latents, wv_ref[...], 1, 0) + rows_ref[3:4, :]).astype(bf16)
        v_own[...] = values
        vt_own[...] = values.T
        for n, (source, target) in enumerate(results(first)):
            pltpu.make_async_copy(source, target, out_sem.at[n]).start()
        attend(first)
        for n, (source, target) in enumerate(results(first)):
            pltpu.make_async_copy(source, target, out_sem.at[n]).wait()

    def visit(index, carry):
        t, across, way = index // 4, index % 4 // 2, index % 2
        for later in range(1, SLOW):

            @pl.when(index == 4 * later)
            def _(later=later):
                for half in range(2):
                    spread(half).step(later)
                    for to in range(2):

                        @pl.when(place.spots[to] >= later)
                        def _(half=half, to=to):
                            fast_copy(0, chunk_of(to, later), half).start()

        far = t - across
        spot = jnp.where(way == 0, place.slow, SLOW - 1 - place.slow)
        chunk = jnp.where(way == 0, spot - far, SLOW - 1 - spot + far)
        due = (far >= 0) & (far < SLOW) & (spot >= far) & ((far > 0) | (way == 0))

        @pl.when(due & (across == 1))
        def _():
            await_fast(chunk)

        @pl.when(due & ((across == 1) | by_block))
        def _():
            project(chunk, jnp.where(across == 1, flip(place.fast, 1), place.fast))

        return carry

    lax.fori_loop(0, 4 * (SLOW + 1), visit, 0)
    for t in range(tiles):
        for g in range(groups):
            total = jnp.sum(totals[g, t], axis=0, keepdims=True)
            att_ref[t * TILE : (t + 1) * TILE, group_at(g)] = fold_heads(mixed[g, t] * (1.0 / total))
            lse_ref[t : t + 1, group_at(g)] = tops[g, t][0:1] + jnp.log(total)

    attended = att_ref[...].astype(bf16)
    weight_loads[0].wait()
    hidden = rays_ref[...].astype(f32) + matmul(attended, wo_ref[...], 1, 0) + rows_ref[4:5, :]
    hidden_low = hidden.astype(bf16)
    hidden_turned = hidden_low.T
    weight_loads[3].wait()
    cot = cot_ref[...]
    inner = wu_ref.shape[1]
    blocks = inner // WIDE
    weight_loads[1].wait()
    weight_loads[2].wait()
    per_half = blocks // 2

    def early_copies(n):
        half, part = n // per_half, n % per_half
        slot = n % 2
        return (
            pltpu.make_async_copy(
                gu_slot.at[slot], early_hbm.at[half, pl.ds(0, width), pl.ds(part * WIDE, WIDE)], early_sem.at[0, slot]
            ),
            pltpu.make_async_copy(
                gd_slot.at[slot], early_hbm.at[half, pl.ds(width + part * WIDE, WIDE)], early_sem.at[1, slot]
            ),
        )

    for n in range(blocks):
        at = slice(n * WIDE, (n + 1) * WIDE)
        bias_row, bias_at = 5 + n * WIDE // width, slice(n * WIDE % width, n * WIDE % width + WIDE)
        pre = matmul(hidden_low, wu_ref[:, at], 1, 0) + rows_ref[bias_row : bias_row + 1, bias_at]
        active, slope = gelu_both(pre)
        active = active.astype(bf16)
        active_ref[:, at] = active
        grad_pre = (matmul(cot, wd_ref[at, :], 1, 1) * slope).astype(bf16)
        gpre_ref[:, at] = grad_pre
        small_ref[bias_row - 4 : bias_row - 3, bias_at] = jnp.sum(grad_pre.astype(f32), axis=0, keepdims=True)
        if n >= 2:
            for copy in early_copies(n - 2):
                copy.wait()
        gu_slot[n % 2] = matmul(hidden_turned, grad_pre, 1, 0).astype(bf16)
        gd_slot[n % 2] = matmul(active, cot, 0, 0).astype(bf16)
        for copy in early_copies(n):
            copy.start()
    result_ref[...] = (hidden + matmul(active_ref[...], wd_ref[...], 1, 0) + rows_ref[7:8, :]).astype(bf16)
    grad_top = cot.astype(f32)
    small_ref[3:4, :] = jnp.sum(grad_top, axis=0, keepdims=True)
    grad_hidden = grad_top + matmul(gpre_ref[...], wu_ref[...], 1, 1)
    gh_ref[...] = grad_hidden
    grad_branch = grad_hidden.astype(bf16)
    small_ref[0:1, :] = jnp.sum(grad_branch.astype(f32), axis=0, keepdims=True)
    small_ref[4:8, :] = jnp.zeros((4, width), f32)
    grad_out = matmul(attended, grad_branch, 0, 0).astype(bf16)
    go_slot[...] = grad_out[: 2 * BLOCK]
    go_copies = [
        pltpu.make_async_copy(
            go_slot.at[pl.ds(c * BLOCK, BLOCK)], early_hbm.at[c, pl.ds(2 * width, BLOCK)], go_sem.at[c]
        )
        for c in range(2)
    ]
    for copy in go_copies:
        copy.start()
    rest_ref[...] = grad_out[2 * BLOCK :]
    grad_attended = matmul(grad_branch, wo_ref[...], 1, 1).astype(bf16)
    ga_ref[...] = grad_attended
    product = grad_attended.astype(f32) * att_ref[...]
    for t in range(dots_ref.shape[0]):
        for g in range(width // WIDE):
            dots_ref[t : t + 1, group_at(g)] = lax.dot_general(
                jnp.ones((8, WIDE), f32),
                spread_heads(product[t * TILE : (t + 1) * TILE, group_at(g)]),
                (((1,), (1,)), ((), ())),
                precision=lax.Precision.HIGHEST,
                preferred_element_type=f32,
            )[0:1, :]
    for copy in early_copies(blocks - 2) + early_copies(blocks - 1) + tuple(go_copies):
        copy.wait()


    for half in range(2):
        spread(half).drain()


def gather_and_attend(
    n_seq, n_ray, rays, latents, lengths, scenes, vectors, w_query, w_key, w_value, cotangent, w_out, w_up, w_down
):
    inner = w_up.shape[1]
    block, width = latents.shape
    n_rays = rays.shape[0]
    n_fast = n_ray // SLOW
    group = n_fast * block
    step = block if block % 128 == 0 and n_fast == 2 else group
    total = n_ray * block
    tiles, groups = n_rays // TILE, width // WIDE
    fast_bits = len(bits_of(n_fast))
    vmem = pltpu.VMEM
    sem = pltpu.SemaphoreType.DMA
    in_vmem = pl.BlockSpec(memory_space=vmem)
    anywhere = pl.BlockSpec(memory_space=pl.ANY)
    struct = jax.ShapeDtypeStruct
    tall, wide = struct((total, width), bf16), struct((width, total), bf16)
    return pl.pallas_call(
        functools.partial(gather_kernel, n_seq, n_ray),
        out_shape=(
            wide,
            tall,
            wide,
            tall,
            struct((n_rays, width), bf16),
            struct((n_rays, width), bf16),
            struct((tiles, width), f32),
            struct((tiles, WIDE), f32),
            struct((8, width), f32),
            struct((n_rays, width), bf16),
            struct((n_rays, width), f32),
            struct((n_rays, width), bf16),
            struct((tiles, width), f32),
            struct((8, width), f32),
            struct((2, 2 * width + BLOCK, width), bf16),
            struct((width - 2 * BLOCK, width), bf16),
        ),
        in_specs=[pl.BlockSpec(memory_space=pltpu.SMEM)] + [in_vmem] * 9 + [anywhere] * 8,
        out_specs=(anywhere,) * 4 + (in_vmem,) * 10 + (anywhere, in_vmem),
        scratch_shapes=[
            vmem((SLOW, n_fast, block, width), bf16),
            vmem((width, step), bf16),
            vmem((step, width), bf16),
            vmem((width, step), bf16),
            vmem((step, width), bf16),
            vmem((width, step), bf16),
            vmem((step, WIDE), f32),
            vmem((groups, tiles, 8, WIDE), f32),
            vmem((groups, tiles, 8, WIDE), f32),
            vmem((groups, tiles, WIDE, WIDE), f32),
            vmem((n_rays, width), f32),
            vmem((n_rays, width), bf16),
            vmem((width, width), bf16),
            vmem((width, width), bf16),
            vmem((width, width), bf16),
            vmem((n_rays, width), bf16),
            vmem((width, width), bf16),
            vmem((width, inner), bf16),
            vmem((inner, width), bf16),
            vmem((n_rays, inner), bf16),
            vmem((n_rays, inner), bf16),
            vmem((2, width, WIDE), bf16),
            vmem((2, WIDE, width), bf16),
            vmem((2 * BLOCK, width), bf16),
            sem((2, 2, 2, SLOW - 1)),
            sem((2, fast_bits, SLOW, 2)),
            sem((4,)),
            sem((8,)),
            sem((2, 2)),
            sem((2,)),
        ],
        compiler_params=pltpu.CompilerParams(collective_id=0, has_side_effects=True, vmem_limit_bytes=62 << 20),
        name="gather_and_attend",
    )(lengths, latents, scenes, *vectors, rays, w_query, w_key, w_value, cotangent, w_out, w_up, w_down)


def widen_kernel(*refs):
    sums, vectors, wide, lines = refs[:6], refs[6], refs[7:13], refs[13:]
    for source, target in zip(sums, wide):
        target[...] = source[...].astype(f32)
    for n, line in enumerate(lines):
        line[...] = vectors[n, :]


def widen(sums, vectors):
    steps = 4
    width = vectors.shape[1]
    struct = jax.ShapeDtypeStruct
    blocks = [pl.BlockSpec((a.shape[0] // steps, a.shape[1]), lambda i: (i, 0)) for a in sums]
    return pl.pallas_call(
        widen_kernel,
        grid=(steps,),
        out_shape=tuple(struct(a.shape, f32) for a in sums) + (struct((width,), f32),) * vectors.shape[0],
        in_specs=blocks + [pl.BlockSpec(vectors.shape, lambda i: (0, 0))],
        out_specs=tuple(blocks) + (pl.BlockSpec((width,), lambda i: (0,)),) * vectors.shape[0],
        compiler_params=pltpu.CompilerParams(vmem_limit_bytes=62 << 20),
        name="widen",
    )(*sums, vectors)


def local(
    rays,
    latents,
    lengths,
    scenes,
    ln_gain,
    ln_bias,
    w_query,
    b_query,
    w_key,
    w_value,
    b_value,
    w_out,
    b_out,
    w_up,
    b_up,
    w_down,
    b_down,
    cotangent,
):
    width = rays.shape[1]
    n_seq, n_ray = lax.axis_size("seq"), lax.axis_size("ray")
    vectors = (b_up, ln_gain, ln_bias, b_query, b_value, b_out, b_down)
    (
        all_t,
        keys,
        keys_t,
        values,
        queries,
        shifted,
        lse,
        scene_rows,
        rows,
        result,
        grad_hidden,
        grad_attended,
        dots,
        small,
        early,
        rest,
    ) = gather_and_attend(
        n_seq,
        n_ray,
        rays,
        latents,
        lengths,
        scenes,
        vectors,
        w_query,
        w_key,
        w_value,
        cotangent,
        w_out,
        w_up,
        w_down,
    )
    sum_q, sum_k, sum_v, sum_o, sum_u, sum_d, grad_latents, grad_rays, small_sums = back_and_sum(
        n_seq,
        n_ray,
        latents.shape[0],
        lengths,
        w_query,
        w_key,
        w_value,
        shifted,
        rays,
        grad_hidden,
        rows,
        small,
        queries,
        grad_attended,
        lse,
        dots,
        scene_rows,
        rest,
        early,
        keys,
        keys_t,
        values,
        all_t,
    )
    wide = widen((sum_q, sum_k, sum_v, sum_o, sum_u, sum_d), small_sums)
    lines = wide[6:]
    return (
        result,
        grad_rays,
        grad_latents,
        lines[4],
        lines[5],
        wide[0],
        lines[6],
        wide[1],
        wide[2],
        lines[7],
        wide[3],
        lines[0],
        wide[4],
        jnp.concatenate(lines[1:3]),
        wide[5],
        lines[3],
    )


def solution(mesh):
    whole = P(("seq", "ray"), None)
    in_specs = (whole, whole, P("seq", None), P(("seq", "ray"))) + (P(),) * 13 + (whole,)
    out_specs = (whole,) * 3 + (P(),) * 13
    return jax.shard_map(local, mesh=mesh, in_specs=in_specs, out_specs=out_specs, check_vma=False)
```

```python
import functools
import math

import jax
import jax.numpy as jnp
from jax import lax
from jax.experimental import pallas as pl
from jax.experimental.pallas import tpu as pltpu
from jax.sharding import PartitionSpec as P

HEADS = 12
HEAD = 64
TILE = 64
WIDE = 256
PACK = WIDE // HEAD
EARLY_WAIT = 2
LATE_CORE, LATE_X, LATE_STEP = 1, 2, 1
LAT_WAIT = 3
FORWARD = 2
PAIR = 3
STEP = 256

masked_score = -1e30
f32 = jnp.float32
bf16 = jnp.bfloat16


def matmul(first_arg, second_arg, first_dim, second_dim):
    return lax.dot_general(
        first_arg,
        second_arg,
        (((first_dim,), (second_dim,)), ((), ())),
        preferred_element_type=jnp.float32,
    )


def own_block():
    row = lax.broadcasted_iota(jnp.int32, (WIDE, WIDE), 0) // TILE
    column = lax.broadcasted_iota(jnp.int32, (WIDE, WIDE), 1) // HEAD
    return row == column


def spread_heads(tile):
    return jnp.where(own_block(), jnp.concatenate([tile] * PACK, axis=0), jnp.zeros((), tile.dtype))


def fold_heads(turned):
    kept = jnp.where(own_block(), turned, 0.0)
    folded = (kept[:, : WIDE // 2] + kept[:, WIDE // 2 :]).T
    return folded[:TILE, :] + folded[TILE:, :]


def fold_rows(block, combine):
    return combine(block.reshape(block.shape[0] // 8, 8, block.shape[1]), axis=0)


def group_at(g):
    return slice(g * WIDE, (g + 1) * WIDE)


def segments(lengths, first, count):
    at = lax.broadcasted_iota(jnp.int32, (count, WIDE), 0) + first
    end, scene = 0, jnp.zeros((count, WIDE), f32)
    for c in range(lengths.shape[1] - 1):
        end = end + lengths[0, c]
        scene = scene + (at >= end).astype(f32)
    return scene


def gelu_both(pre):
    half = 0.5 * (1.0 + lax.erf(pre * math.sqrt(0.5)))
    return pre * half, half + pre * jnp.exp(-0.5 * pre * pre) * (1.0 / math.sqrt(2.0 * math.pi))


MESH = pl.DeviceIdType.MESH
BLOCK = 256
SLOW = 4


def flip(index, bit):
    return index + bit * (1 - 2 * ((index // bit) % 2))


def bits_of(count):
    bits = []
    while count > 1:
        count //= 2
        bits.append(count)
    return bits


def lane_rows(start, size):
    return pl.ds(pl.multiple_of(start, 16), size)


class Place:
    def __init__(self, n_seq, n_ray):
        self.seq = lax.axis_index("seq")
        self.ray = lax.axis_index("ray")
        self.n_fast = n_ray // SLOW
        self.core = self.seq % 2
        self.slow = self.ray // self.n_fast
        self.fast = self.ray % self.n_fast
        self.x_bits = [("seq", 2 * b) for b in bits_of(n_seq // 2)]
        self.fast_bits = [("ray", b) for b in bits_of(self.n_fast)]
        self.slow_bits = [("ray", self.n_fast * b) for b in bits_of(SLOW)]
        self.spots = (self.slow, SLOW - 1 - self.slow)

    def across(self, axis, bit):
        if axis == "seq":
            return (flip(self.seq, bit), self.ray)
        return (self.seq, flip(self.ray, bit))

    def value(self, axis, bit):
        return ((self.seq if axis == "seq" else self.ray) // bit) % 2

    def along(self, way):
        return (self.seq, self.ray + (self.n_fast if way == 0 else -self.n_fast))

    def after(self, step):
        return (self.seq, (self.slow + step) % SLOW * self.n_fast + self.fast)

    def mirrored(self, way, chunk):
        return chunk if way == 0 else SLOW - 1 - chunk


def remote(src, dst, send_sem, recv_sem, device):
    return pltpu.make_async_remote_copy(
        src_ref=src,
        dst_ref=dst,
        send_sem=send_sem,
        recv_sem=recv_sem,
        device_id=device,
        device_id_type=MESH,
    )


def greet(place, exchanges):
    barrier = pltpu.get_barrier_semaphore()
    for axis, bit in exchanges:
        pl.semaphore_signal(barrier, inc=1, device_id=place.across(axis, bit), device_id_type=MESH)
    for step in range(1, SLOW):
        pl.semaphore_signal(barrier, inc=1, device_id=place.after(step), device_id_type=MESH)
    pl.semaphore_wait(barrier, len(exchanges) + SLOW - 1)


class Line:
    def __init__(self, place, block, recv, send_sem, recv_sem):
        self.place, self.block, self.recv, self.send_sem, self.recv_sem = place, block, recv, send_sem, recv_sem

    def copy(self, way, t, to):
        chunk = self.place.mirrored(way, SLOW - 1 - (t - self.place.spots[way]))
        return remote(
            self.block(chunk), self.recv(way, t), self.send_sem(way, t), self.recv_sem(way, t), self.place.along(to)
        )

    def landed(self, way, t):
        remote(
            self.recv(way, t), self.recv(way, t), self.send_sem(way, t), self.recv_sem(way, t), self.place.along(1 - way)
        ).wait_recv()
        return self.recv(way, t)[...].astype(f32)

    def step(self, t):
        for way in range(2):
            spot = self.place.spots[way]

            @pl.when((spot <= t) & (spot < SLOW - 1))
            def _(way=way, spot=spot):
                if t > 0:

                    @pl.when(spot > 0)
                    def _():
                        block = self.block(self.place.mirrored(way, SLOW - 1 - (t - spot)))
                        block[...] = (block[...].astype(f32) + self.landed(way, t - 1)).astype(bf16)

                self.copy(way, t, way).start()

    def last(self, total):
        total[...] = self.block(self.place.slow)[...].astype(f32)
        for way in range(2):

            @pl.when(self.place.spots[way] > 0)
            def _(way=way):
                total[...] += self.landed(way, SLOW - 2)

    def drain(self):
        for way in range(2):
            for t in range(SLOW - 1):
                spot = self.place.spots[way]

                @pl.when((spot <= t) & (spot < SLOW - 1))
                def _(way=way, t=t):
                    self.copy(way, t, way).wait_send()


class Spread:
    def __init__(self, place, block, send_sem, recv_sem):
        self.place, self.block, self.send_sem, self.recv_sem = place, block, send_sem, recv_sem

    def copy(self, way, t, to):
        chunk = self.place.mirrored(way, self.place.spots[way] - t)
        block = self.block(chunk)
        return remote(block, block, self.send_sem(way, t), self.recv_sem(way, t), self.place.along(to))

    def step(self, t):
        for way in range(2):
            spot = self.place.spots[way]

            @pl.when(spot >= t)
            def _(way=way, spot=spot):
                if t > 0:
                    block = self.block(self.place.mirrored(way, spot - t))
                    remote(
                        block, block, self.send_sem(way, t - 1), self.recv_sem(way, t - 1), self.place.along(1 - way)
                    ).wait_recv()
                if t < SLOW - 1:

                    @pl.when(spot < SLOW - 1)
                    def _():
                        self.copy(way, t, way).start()

    def drain(self):
        for way in range(2):
            for t in range(SLOW - 1):
                spot = self.place.spots[way]

                @pl.when((spot >= t) & (spot < SLOW - 1))
                def _(way=way, t=t):
                    self.copy(way, t, way).wait_send()


def units_of(rows, n_x, n_fast):
    share = n_x * n_fast * SLOW * 16
    return rows // BLOCK if BLOCK % share == 0 else 1


def sum_kernel(
    n_seq,
    n_ray,
    units,
    lengths,
    rows_ref,
    small_ref,
    q_ref,
    g_ref,
    lse_ref,
    dots_ref,
    scene_ref,
    rest_ref,
    wq_hbm,
    wk_hbm,
    wv_hbm,
    shifted_hbm,
    rays_hbm,
    gh_hbm,
    early_hbm,
    k_hbm,
    kt_hbm,
    v_hbm,
    all_hbm,
    o_q,
    o_k,
    o_v,
    o_o,
    o_u,
    o_d,
    glat_ref,
    grays_ref,
    small_out,
    wq_ref,
    wk_ref,
    wv_ref,
    shifted_ref,
    rays_ref,
    k_slot,
    kt_slot,
    v_slot,
    all_slot,
    seg_ref,
    sum_kv,
    grads_kv,
    weights_kv,
    turned_q,
    gq_ref,
    own,
    other,
    full,
    rx,
    z_recv,
    lat,
    lat_recv,
    lz_recv,
    small_now,
    small_recv,
    early_sem,
    slot_sem,
    core_sem,
    halve_sem,
    z_sem,
    zg_sem,
    double_sem,
    back_sem,
    out_sem,
    lat_sem,
    lz_sem,
    small_sem,
):
    place = Place(n_seq, n_ray)
    core_pair = ("seq", 1)
    halvings = place.x_bits + place.fast_bits
    exchanges = [core_pair] + halvings + place.slow_bits
    core = place.core
    rows, width = own.shape
    late_from = early_hbm.shape[1]
    unit_rows = rows // units
    early_units = late_from // unit_rows
    sizes = [unit_rows >> i for i in range(len(halvings) + 1)]
    share = sizes[-1]
    line = share % (16 * SLOW) == 0
    piece = share // SLOW if line else share

    early_load = pltpu.make_async_copy(early_hbm.at[core], own.at[pl.ds(0, late_from)], early_sem.at[0])
    early_load.start()
    gh_load = pltpu.make_async_copy(gh_hbm, grays_ref, early_sem.at[1])
    gh_load.start()
    late_loads = [
        pltpu.make_async_copy(source, target, early_sem.at[2 + n])
        for n, (source, target) in enumerate(
            (
                (wq_hbm, wq_ref),
                (wk_hbm, wk_ref),
                (wv_hbm, wv_ref),
                (shifted_hbm, shifted_ref),
                (rays_hbm, rays_ref),
            )
        )
    ]
    greet(place, [core_pair] + halvings)

    def base(u, stages):
        start = u * unit_rows
        for i in range(stages):
            start = start + place.value(*halvings[i]) * sizes[i + 1]
        return start

    def unit(u):
        return lane_rows(u * unit_rows, unit_rows)

    def core_parts(u):
        if units == 1:
            rows_of = (pl.ds(0, late_from), pl.ds(0, rows - late_from))
            when = (u == 0, u == 0)
            into = (pl.ds(0, late_from), pl.ds(late_from, rows - late_from))
        else:
            rows_of = (unit(u), lane_rows(u * unit_rows - late_from, unit_rows))
            when = (u < early_units, u >= early_units)
            into = (unit(u), unit(u))
        sources = (early_hbm.at[1 - core, rows_of[0]], other.at[rows_of[1]])
        return [
            (
                when[n],
                remote(
                    sources[n], full.at[into[n]], core_sem.at[0, n, u], core_sem.at[1, n, u], place.across(*core_pair)
                ),
            )
            for n in range(2)
        ]

    def halve_copy(i, u):
        size = sizes[i + 1]
        sent = base(u, i) + (1 - place.value(*halvings[i])) * size
        return remote(
            own.at[lane_rows(sent, size)],
            rx[i].at[lane_rows(u * size, size)],
            halve_sem.at[0, i, u],
            halve_sem.at[1, i, u],
            place.across(*halvings[i]),
        )

    def start_core(u):
        for when, copy in core_parts(u):

            @pl.when(when)
            def _(copy=copy):
                copy.start()

    def join_core(u):
        for when, copy in core_parts(u):

            @pl.when(when)
            def _(copy=copy):
                copy.wait()

        own[unit(u), :] = (own[unit(u), :].astype(f32) + full[unit(u), :].astype(f32)).astype(bf16)
        halve_copy(0, u).start()

    def join_half(i):
        def run(u):
            size = sizes[i + 1]
            halve_copy(i, u).wait()
            kept = lane_rows(base(u, i + 1), size)
            own[kept, :] = (own[kept, :].astype(f32) + rx[i][lane_rows(u * size, size), :].astype(f32)).astype(bf16)
            if i + 1 < len(halvings):
                halve_copy(i + 1, u).start()

        return run

    def z_rows(u, chunk):
        return lane_rows(base(u, len(halvings)) + chunk * piece, piece)

    def z_copy(u, step):
        return remote(
            own.at[z_rows(u, (place.slow + step) % SLOW)],
            z_recv.at[u, step - 1],
            z_sem.at[0, u, step - 1],
            z_sem.at[1, u, step - 1],
            place.after(step),
        )

    def z_back_copy(u, step, chunk):
        block = full.at[z_rows(u, chunk)]
        return remote(block, block, zg_sem.at[0, u, step - 1], zg_sem.at[1, u, step - 1], place.after(step))

    def start_z(u):
        for step in range(1, SLOW):
            z_copy(u, step).start()

    def join_z(u):
        total = own[z_rows(u, place.slow), :].astype(f32)
        for step in range(1, SLOW):
            z_copy(u, step).wait()
            total = total + z_recv[u, step - 1].astype(f32)
        full[z_rows(u, place.slow), :] = total.astype(bf16)
        for step in range(1, SLOW):
            z_back_copy(u, step, place.slow).start()

    def join_z_back(u):
        for step in range(1, SLOW):
            z_back_copy(u, step, place.slow).wait_send()
            z_back_copy(u, step, (place.slow + SLOW - step) % SLOW).wait_recv()

    def whole_copy(i, u):
        return remote(
            own.at[lane_rows(base(u, len(halvings)), share)],
            z_recv.at[u, i],
            z_sem.at[0, u, i],
            z_sem.at[1, u, i],
            place.across(*place.slow_bits[i]),
        )

    def whole_step(i):
        def run(u):
            mine = lane_rows(base(u, len(halvings)), share)
            if i > 0:
                whole_copy(i - 1, u).wait()
                own[mine, :] = (own[mine, :].astype(f32) + z_recv[u, i - 1].astype(f32)).astype(bf16)
            if i < len(place.slow_bits):
                whole_copy(i, u).start()
            else:
                full[mine, :] = own[mine, :]

        return run

    def double_copy(i, u):
        block = full.at[lane_rows(base(u, i + 1), sizes[i + 1])]
        return remote(block, block, double_sem.at[0, i, u], double_sem.at[1, i, u], place.across(*halvings[i]))

    def targets(n, c):
        per = width // BLOCK
        part, at = n // per, n % per
        rows_at = pl.ds(pl.multiple_of(at * BLOCK, BLOCK), BLOCK)
        after = pl.ds(pl.multiple_of((n + per - 1) % per * BLOCK, BLOCK), BLOCK)
        half_at = pl.ds(pl.multiple_of(c * width, 128), width)
        lower = pl.ds(pl.multiple_of(c * width + at * BLOCK, BLOCK), BLOCK)
        last = pl.ds(2 * BLOCK, BLOCK)
        return [
            (part == 0, o_u.at[rows_at, half_at]),
            (part == 1, o_d.at[lower]),
            (n == 2 * per, o_o.at[pl.ds(pl.multiple_of(c * BLOCK, BLOCK), BLOCK)]),
            ((n > 2 * per) & (n <= 3 * per) & (c == 0), o_k.at[after]),
            ((n > 2 * per) & (n <= 3 * per) & (c == 1), o_v.at[after]),
            ((n == 3 * per + 1) & (c == 0), o_o.at[last]),
            ((n == 3 * per + 1) & (c == 1), o_q.at[pl.ds(0, BLOCK)]),
            (n == 3 * per + 2, o_q.at[pl.ds(pl.multiple_of((1 + c) * BLOCK, BLOCK), BLOCK)]),
        ]

    def block_rows(n):
        return lane_rows(n * BLOCK, BLOCK)

    def blocks_of(u):
        return [u] if units > 1 else list(range(rows // BLOCK))

    def send_block(n):
        for when, target in targets(n, core):

            @pl.when(when)
            def _(target=target):
                source = full.at[block_rows(n)]
                remote(source, target, back_sem.at[0, n], back_sem.at[1, n], place.across(*core_pair)).start()
                pltpu.make_async_copy(source, target, out_sem.at[n]).start()

    def end_block(n):
        for when, target in targets(n, core):

            @pl.when(when)
            def _(target=target):
                source = full.at[block_rows(n)]
                remote(source, target, back_sem.at[0, n], back_sem.at[1, n], place.across(*core_pair)).wait_send()
                pltpu.make_async_copy(source, target, out_sem.at[n]).wait()

        for when, target in targets(n, 1 - core):

            @pl.when(when)
            def _(target=target):
                source = full.at[block_rows(n)]
                remote(source, target, back_sem.at[0, n], back_sem.at[1, n], place.across(*core_pair)).wait_recv()

    def start_double(u):
        double_copy(len(halvings) - 1, u).start()

    def join_double(i):
        def run(u):
            double_copy(i, u).wait()
            if i > 0:
                double_copy(i - 1, u).start()
            else:
                for n in blocks_of(u):
                    send_block(n)

        return run

    def finish_unit(u):
        for n in blocks_of(u):
            end_block(n)

    stages = [[start_core], [join_core]] + [[join_half(i)] for i in range(len(halvings))]
    if line:
        stages[-1].append(start_z)
        stages += [[join_z], [join_z_back]]
    else:
        stages[-1].append(whole_step(0))
        stages += [[whole_step(i)] for i in range(1, len(place.slow_bits) + 1)]
    stages[-1].append(start_double)
    stages += [[join_double(i)] for i in reversed(range(len(halvings)))]
    stages += [[finish_unit]]

    n_fast, block = lat.shape[1:3]
    group = n_fast * block
    half_rows = block // 2
    fast_sizes = [n_fast >> i for i in range(len(place.fast_bits) + 1)]

    def chunk_of(k):
        near = jnp.minimum(place.slow, SLOW - 1 - place.slow)
        ahead = SLOW - 1 - near
        chunk = jnp.where(k < ahead, SLOW - 1 - k, jnp.where(k - ahead < near, k - ahead, near))
        return jnp.where(place.slow == near, chunk, SLOW - 1 - chunk)

    def lat_base(stages):
        start = 0
        for i in range(stages):
            start = start + place.value(*place.fast_bits[i]) * fast_sizes[i + 1]
        return start

    def lat_half(m):
        return lane_rows((m % 2) * half_rows, half_rows)

    def lat_copy(i, m):
        size = fast_sizes[i + 1]
        sent = lat_base(i) + (1 - place.value(*place.fast_bits[i])) * size
        return remote(
            lat.at[chunk_of(m // 2), pl.ds(sent, size), lat_half(m)],
            lat_recv[i].at[m],
            lat_sem.at[0, i, m],
            lat_sem.at[1, i, m],
            place.across(*place.fast_bits[i]),
        )

    def start_lat(m):
        lat_copy(0, m).start()

    def lat_line(m):
        half = m % 2
        return Line(
            place,
            lambda chunk: lat.at[chunk, place.fast, lat_half(m)],
            lambda way, t: lz_recv.at[half, way, t],
            lambda way, t: lz_sem.at[0, half, way, t],
            lambda way, t: lz_sem.at[1, half, way, t],
        )

    def join_lat(i):
        def run(m):
            lat_copy(i, m).wait()
            kept = lat.at[chunk_of(m // 2), pl.ds(lat_base(i + 1), fast_sizes[i + 1]), lat_half(m)]
            kept[...] = (kept[...].astype(f32) + lat_recv[i][m].astype(f32)).astype(bf16)
            if i + 1 < len(place.fast_bits):
                lat_copy(i + 1, m).start()
            else:
                for t in range(SLOW - 1):

                    @pl.when(m // 2 == t)
                    def _(t=t):
                        lat_line(m).step(t)

        return run

    def finish_lat(m):
        @pl.when(m // 2 == SLOW - 1)
        def _():
            lat_line(m).last(glat_ref.at[lat_half(m)])
            lat_line(m).drain()

    lat_stages = [start_lat] + [join_lat(i) for i in range(len(place.fast_bits))] + [finish_lat]

    def small_copy(i):
        axis, bit = exchanges[i]
        return remote(
            small_now.at[i], small_recv.at[i], small_sem.at[0, i], small_sem.at[1, i], place.across(axis, bit)
        )

    def start_small():
        small_copy(0).start()

    def join_small(i):
        def run():
            small_copy(i).wait()
            small_now[i + 1] = small_now[i] + small_recv[i]
            if i + 1 < len(exchanges):
                small_copy(i + 1).start()

        return run

    tiles, groups = scene_ref.shape[0], width // WIDE
    pairs, parts = tiles // PAIR, group // STEP
    per_chunk = pairs * parts

    def slot_loads(k):
        chunk = chunk_of(k)
        at, columns = lane_rows(chunk * group, group), pl.ds(pl.multiple_of(chunk * group, 128), group)
        return (
            pltpu.make_async_copy(k_hbm.at[at], k_slot, slot_sem.at[0]),
            pltpu.make_async_copy(kt_hbm.at[:, columns], kt_slot, slot_sem.at[1]),
            pltpu.make_async_copy(v_hbm.at[at], v_slot, slot_sem.at[2]),
        )

    def all_load(k):
        columns = pl.ds(pl.multiple_of(chunk_of(k) * group, 128), group)
        return pltpu.make_async_copy(all_hbm.at[:, columns], all_slot, slot_sem.at[3])

    def open_chunk(k):
        for load in slot_loads(k):
            load.wait()

        all_load(k).start()
        seg_ref[...] = segments(lengths, chunk_of(k) * group, group)
        sum_kv[...] = jnp.zeros_like(sum_kv)

    def tile_rows(t):
        return pl.ds(pl.multiple_of(t * TILE, TILE), TILE)

    def back_step(pair, part):
        at = pl.ds(pl.multiple_of(part * STEP, 128), STEP)
        own_tiles = [pair * PAIR + i for i in range(PAIR)]
        seen = jnp.concatenate([seg_ref[at, :]] * PAIR, axis=1) == jnp.concatenate(
            [scene_ref[pl.ds(t, 1), :] for t in own_tiles], axis=1
        )
        for g in range(groups):
            to = group_at(g)
            q_spread = jnp.concatenate([spread_heads(q_ref[tile_rows(t), to]) for t in own_tiles], axis=0)
            g_spread = jnp.concatenate([spread_heads(g_ref[tile_rows(t), to]) for t in own_tiles], axis=0)
            lse = jnp.concatenate([lse_ref[pl.ds(t, 1), to] for t in own_tiles], axis=1)
            dots = jnp.concatenate([dots_ref[pl.ds(t, 1), to] for t in own_tiles], axis=1)
            s = matmul(k_slot[at, to], q_spread, 1, 1)
            p = jnp.where(seen, jnp.exp(s - lse), 0.0)
            sum_kv[1, at, to] += matmul(p.astype(bf16), g_spread, 1, 0)
            gp = matmul(v_slot[at, to], g_spread, 1, 1)
            gs = (p * (gp - dots)).astype(bf16)
            sum_kv[0, at, to] += matmul(gs, q_spread, 1, 0)
            turned_q[g, pair] += matmul(kt_slot[to, at], gs, 1, 0)

    def close_chunk(k):
        @pl.when(k + 1 < SLOW)
        def _():
            for load in slot_loads(k + 1):
                load.start()

        @pl.when(k == 0)
        def _():
            for load in late_loads:
                load.wait()

        grads_kv[...] = sum_kv[...].astype(bf16)
        total = matmul(grads_kv[0], wk_ref[...], 1, 1) + matmul(grads_kv[1], wv_ref[...], 1, 1)
        lat[chunk_of(k)] = total.astype(bf16).reshape(n_fast, block, width)
        all_load(k).wait()
        for n in range(2):
            weights_kv[n] += matmul(all_slot[...], grads_kv[n], 1, 0)
        small_now[0, 7:8] += jnp.sum(grads_kv[1].astype(f32), axis=0, keepdims=True)

    def attend(step):
        k, part_of = step // per_chunk, step % per_chunk

        @pl.when(part_of == 0)
        def _():
            open_chunk(k)

        back_step(part_of // parts, part_of % parts)

        @pl.when(part_of == per_chunk - 1)
        def _():
            close_chunk(k)

    def key_terms():
        own[late_from : late_from + width, :] = weights_kv[core].astype(bf16)
        other[:width, :] = weights_kv[1 - core].astype(bf16)

    def query_terms():
        for t in range(tiles):
            for g in range(groups):
                turned = turned_q[g, t // PAIR, :, t % PAIR * WIDE : (t % PAIR + 1) * WIDE]
                gq_ref[t * TILE : (t + 1) * TILE, group_at(g)] = (fold_heads(turned) * HEAD ** (-0.5)).astype(bf16)

    def query_weight_terms():
        terms = matmul(shifted_ref[...], gq_ref[...], 0, 0).astype(bf16)
        first, second, third = [terms[b * BLOCK : (b + 1) * BLOCK] for b in range(width // BLOCK)]
        after = late_from + width

        @pl.when(core == 0)
        def _():
            own[after : after + BLOCK, :] = rest_ref[...]
            own[after + BLOCK :, :] = second
            other[width : width + BLOCK, :] = first
            other[width + BLOCK :, :] = third

        @pl.when(core == 1)
        def _():
            own[after : after + BLOCK, :] = first
            own[after + BLOCK :, :] = third
            other[width : width + BLOCK, :] = rest_ref[...]
            other[width + BLOCK :, :] = second

    def ray_terms():
        inputs = rays_ref[...].astype(f32)
        centred = inputs - jnp.mean(inputs, axis=1, keepdims=True)
        inverse = lax.rsqrt(jnp.mean(centred * centred, axis=1, keepdims=True) + 1e-05)
        normed = centred * inverse
        grad_shifted = matmul(gq_ref[...], wq_ref[...], 1, 1)
        grad_normed = grad_shifted * rows_ref[0:1, :]
        gh_load.wait()
        grays_ref[...] += inverse * (
            grad_normed
            - jnp.mean(grad_normed, axis=1, keepdims=True)
            - normed * jnp.mean(grad_normed * normed, axis=1, keepdims=True)
        )
        small_now[0, 4:5] = jnp.sum(grad_shifted * normed, axis=0, keepdims=True)
        small_now[0, 5:6] = jnp.sum(grad_shifted, axis=0, keepdims=True)
        small_now[0, 6:7] = jnp.sum(gq_ref[...].astype(f32), axis=0, keepdims=True)

    for load in slot_loads(0) + tuple(late_loads):
        load.start()
    turned_q[...] = jnp.zeros_like(turned_q)
    weights_kv[...] = jnp.zeros_like(weights_kv)
    small_now[0] = small_ref[...]
    early_load.wait()

    steps = SLOW * per_chunk
    late_start = steps if units > 1 else steps + 3
    finish = [key_terms, query_terms, query_weight_terms, ray_terms]
    work = {steps - 1 + n + (n > 0): [run] for n, run in enumerate(finish)}
    for i in range(len(exchanges)):
        work.setdefault(steps + len(finish) + 1 + i, []).append(join_small(i))
    work[steps + len(finish) - 1].append(start_small)
    lat_wait = LAT_WAIT
    late_waits = [0, LATE_CORE] + [LATE_X] + [LATE_STEP] * (len(stages) - 5) + [LATE_X, 1]
    late_at = [sum(late_waits[: n + 1]) for n in range(len(stages))]
    lat_span = steps + 2 + lat_wait * (len(lat_stages) - 1)
    beats = max(late_start + units - early_units + late_at[-1], lat_span, max(work) + 1)

    def one_beat(now, carry):
        for s in range(len(stages)):
            early = now - EARLY_WAIT * s
            late = now - late_start - late_at[s]
            u = jnp.where(late >= 0, late + early_units, early)

            @pl.when(((late >= 0) & (u < units)) | ((early >= 0) & (early < early_units)))
            def _(u=u, s=s):
                for run in stages[s]:
                    run(u)

        for s in range(len(lat_stages)):
            ahead = now - per_chunk - lat_wait * s
            m = ahead // per_chunk * 2 + ahead % per_chunk

            @pl.when((ahead >= 0) & (ahead % per_chunk < 2) & (m < 2 * SLOW))
            def _(m=m, s=s):
                lat_stages[s](m)

        @pl.when(now < steps)
        def _():
            attend(now)

        for beat, runs in work.items():

            @pl.when(now == beat)
            def _(runs=runs):
                for run in runs:
                    run()

        return carry

    lax.fori_loop(0, beats, one_beat, 0)
    small_out[...] = small_now[len(exchanges)]


def back_and_sum(
    n_seq,
    n_ray,
    block,
    lengths,
    w_query,
    w_key,
    w_value,
    shifted,
    rays,
    gh,
    rows,
    small,
    queries,
    ga,
    lse,
    dots,
    scene_rows,
    rest,
    early,
    keys,
    keys_t,
    values,
    all_t,
):
    n_fast = n_ray // SLOW
    n_x = n_seq // 2
    n_rays, width = rays.shape
    group = n_fast * block
    groups, pairs = width // WIDE, n_rays // TILE // PAIR
    sum_rows = 4 * width
    late_rows = sum_rows - early.shape[1]
    units = units_of(sum_rows, n_x, n_fast)
    halvings = len(bits_of(n_x)) + len(bits_of(n_fast))
    fast_bits = len(bits_of(n_fast))
    exchanges = 1 + halvings + len(bits_of(SLOW))
    share = sum_rows // units >> halvings
    piece = share // SLOW if share % (16 * SLOW) == 0 else share
    half = block // 2
    vmem = pltpu.VMEM
    sem = pltpu.SemaphoreType.DMA
    struct = jax.ShapeDtypeStruct
    in_vmem = pl.BlockSpec(memory_space=vmem)
    anywhere = pl.BlockSpec(memory_space=pl.ANY)
    return pl.pallas_call(
        functools.partial(sum_kernel, n_seq, n_ray, units),
        out_shape=(
            struct((width, width), bf16),
            struct((width, width), bf16),
            struct((width, width), bf16),
            struct((width, width), bf16),
            struct((width, 2 * width), bf16),
            struct((2 * width, width), bf16),
            struct((block, width), f32),
            struct((n_rays, width), f32),
            struct((8, width), f32),
        ),
        in_specs=[pl.BlockSpec(memory_space=pltpu.SMEM)] + [in_vmem] * 8 + [anywhere] * 11,
        out_specs=(anywhere,) * 6 + (in_vmem,) * 3,
        scratch_shapes=[
            vmem((width, width), bf16),
            vmem((width, width), bf16),
            vmem((width, width), bf16),
            vmem((n_rays, width), bf16),
            vmem((n_rays, width), bf16),
            vmem((group, width), bf16),
            vmem((width, group), bf16),
            vmem((group, width), bf16),
            vmem((width, group), bf16),
            vmem((group, WIDE), f32),
            vmem((2, group, width), f32),
            vmem((2, group, width), bf16),
            vmem((2, width, width), f32),
            vmem((groups, pairs, WIDE, PAIR * WIDE), f32),
            vmem((n_rays, width), bf16),
            vmem((sum_rows, width), bf16),
            vmem((late_rows, width), bf16),
            vmem((sum_rows, width), bf16),
            [vmem((sum_rows >> (i + 1), width), bf16) for i in range(halvings)],
            vmem((units, SLOW - 1, piece, width), bf16),
            vmem((SLOW, n_fast, block, width), bf16),
            [vmem((2 * SLOW, n_fast >> (i + 1), half, width), bf16) for i in range(fast_bits)],
            vmem((2, 2, SLOW - 1, half, width), bf16),
            vmem((exchanges + 1, 8, width), f32),
            vmem((exchanges, 8, width), f32),
            sem((7,)),
            sem((4,)),
            sem((2, 2, units)),
            sem((2, halvings, units)),
            sem((2, units, SLOW - 1)),
            sem((2, units, SLOW - 1)),
            sem((2, halvings, units)),
            sem((2, sum_rows // BLOCK)),
            sem((sum_rows // BLOCK,)),
            sem((2, fast_bits, 2 * SLOW)),
            sem((2, 2, 2, SLOW - 1)),
            sem((2, exchanges)),
        ],
        compiler_params=pltpu.CompilerParams(collective_id=1, has_side_effects=True, vmem_limit_bytes=63 << 20),
        name="back_and_sum",
    )(
        lengths,
        rows,
        small,
        queries,
        ga,
        lse,
        dots,
        scene_rows,
        rest,
        w_query,
        w_key,
        w_value,
        shifted,
        rays,
        gh,
        early,
        keys,
        keys_t,
        values,
        all_t,
    )


def gather_kernel(
    n_seq,
    n_ray,
    lengths,
    lat_ref,
    scenes_ref,
    up_bias_ref,
    gain_ref,
    bias_ref,
    q_bias_ref,
    v_bias_ref,
    out_bias_ref,
    down_bias_ref,
    rays_hbm,
    wq_hbm,
    wk_hbm,
    wv_hbm,
    cot_hbm,
    wo_hbm,
    wu_hbm,
    wd_hbm,
    all_ref,
    k_ref,
    kt_ref,
    v_ref,
    q_ref,
    shifted_ref,
    lse_ref,
    scene_ref,
    rows_ref,
    result_ref,
    gh_ref,
    ga_ref,
    dots_ref,
    small_ref,
    early_hbm,
    rest_ref,
    full,
    all_own,
    k_own,
    kt_own,
    v_own,
    vt_own,
    seg_ref,
    tops,
    totals,
    mixed,
    att_ref,
    rays_ref,
    wq_ref,
    wk_ref,
    wv_ref,
    cot_ref,
    wo_ref,
    wu_ref,
    wd_ref,
    active_ref,
    gpre_ref,
    gu_slot,
    gd_slot,
    go_slot,
    z_sem,
    y_sem,
    out_sem,
    weight_sem,
    early_sem,
    go_sem,
):
    place = Place(n_seq, n_ray)
    fast_bits = place.fast_bits[::-1]
    weight_loads = [
        pltpu.make_async_copy(source, target, weight_sem.at[n])
        for n, (source, target) in enumerate(
            (
                (wo_hbm, wo_ref),
                (wu_hbm, wu_ref),
                (wd_hbm, wd_ref),
                (cot_hbm, cot_ref),
                (rays_hbm, rays_ref),
                (wq_hbm, wq_ref),
                (wk_hbm, wk_ref),
                (wv_hbm, wv_ref),
            )
        )
    ]
    for load in weight_loads[4:] + weight_loads[:4]:
        load.start()
    greet(place, place.fast_bits)
    block, width = lat_ref.shape
    half_rows = block // 2
    group = place.n_fast * block
    full[place.slow, place.fast] = lat_ref[...]
    step = k_own.shape[0]
    by_block = step == block

    def half_at(half):
        return pl.ds(half * half_rows, half_rows)

    def spread(half):
        return Spread(
            place,
            lambda chunk: full.at[chunk, place.fast, half_at(half)],
            lambda way, t: z_sem.at[0, half, way, t],
            lambda way, t: z_sem.at[1, half, way, t],
        )

    def fast_copy(i, chunk, half):
        axis, bit = fast_bits[i]
        mine = full.at[chunk, pl.ds(place.fast // bit * bit, bit), half_at(half)]
        return remote(mine, mine, y_sem.at[0, i, chunk, half], y_sem.at[1, i, chunk, half], place.across(axis, bit))

    def chunk_of(way, t):
        return place.mirrored(way, place.spots[way] - t)

    for half in range(2):
        fast_copy(0, place.slow, half).start()
        spread(half).step(0)

    for n, vector in enumerate((gain_ref, bias_ref, q_bias_ref, v_bias_ref, out_bias_ref)):
        rows_ref[n : n + 1, :] = vector[...].astype(f32).reshape(1, width)
    up_bias = up_bias_ref[...].astype(f32).reshape(1, -1)
    for n in range(2):
        rows_ref[5 + n : 6 + n, :] = up_bias[:, n * width : (n + 1) * width]
    rows_ref[7:8, :] = down_bias_ref[...].astype(f32).reshape(1, width)

    scenes = scenes_ref[...].astype(f32).reshape(1, -1)
    for t in range(scene_ref.shape[0]):
        scene_ref[t : t + 1, :] = jnp.concatenate([scenes[:, t * TILE : (t + 1) * TILE]] * PACK, axis=1)

    for load in weight_loads[4:]:
        load.wait()
    inputs = rays_ref[...].astype(f32)
    centred = inputs - jnp.mean(inputs, axis=1, keepdims=True)
    inverse = lax.rsqrt(jnp.mean(centred * centred, axis=1, keepdims=True) + 1e-05)
    shifted = (centred * inverse * rows_ref[0:1, :] + rows_ref[1:2, :]).astype(bf16)
    shifted_ref[...] = shifted
    queries = (matmul(shifted, wq_ref[...], 1, 0) + rows_ref[2:3, :]).astype(bf16)
    q_ref[...] = (queries.astype(f32) * HEAD ** (-0.5)).astype(bf16)
    tiles, groups = scene_ref.shape[0], width // WIDE
    tops[...] = jnp.full_like(tops, masked_score)
    totals[...] = jnp.zeros_like(totals)
    mixed[...] = jnp.zeros_like(mixed)

    def attend(first):
        seg_ref[...] = segments(lengths, first, step)

        def some_tiles(n, carry):
            own_tiles = [n * FORWARD + i for i in range(FORWARD)]
            scenes = jnp.concatenate([scene_ref[pl.ds(t, 1), :] for t in own_tiles], axis=1)
            seen = jnp.concatenate([seg_ref[...]] * FORWARD, axis=1) == scenes
            scores, old, new = [], [], []
            for g in range(groups):
                spread_q = [
                    spread_heads(q_ref[pl.ds(pl.multiple_of(t * TILE, TILE), TILE), group_at(g)]) for t in own_tiles
                ]
                s = matmul(k_own[:, group_at(g)], jnp.concatenate(spread_q, axis=0), 1, 1)
                scores.append(jnp.where(seen, s, masked_score))
                old.append(jnp.concatenate([tops[g, t] for t in own_tiles], axis=1))
                new.append(jnp.maximum(old[g], jnp.max(fold_rows(scores[g], jnp.max), axis=0, keepdims=True)))
            for g in range(groups):
                fix = jnp.exp(old[g] - new[g])
                e = jnp.exp(scores[g] - new[g][0:1])
                total = fold_rows(e, jnp.sum)
                mix = matmul(vt_own[group_at(g), :], e.astype(bf16), 1, 0)
                for i, t in enumerate(own_tiles):
                    cut = group_at(i)
                    tops[g, t] = new[g][:, cut]
                    totals[g, t] = totals[g, t] * fix[:, cut] + total[:, cut]
                    mixed[g, t] = mixed[g, t] * fix[0:1, cut] + mix[:, cut]
            return carry

        lax.fori_loop(0, tiles // FORWARD, some_tiles, 0)

    def results(first):
        rows = pl.ds(pl.multiple_of(first, 16), step)
        columns = pl.ds(pl.multiple_of(first, 128), step)
        return [
            (k_own, k_ref.at[rows]),
            (kt_own, kt_ref.at[:, columns]),
            (v_own, v_ref.at[rows]),
            (all_own, all_ref.at[:, columns]),
        ]

    def await_fast(chunk):
        for half in range(2):
            for i in range(len(fast_bits)):
                fast_copy(i, chunk, half).wait()
                if i + 1 < len(fast_bits):
                    fast_copy(i + 1, chunk, half).start()

    def project(chunk, fast):
        if by_block:
            first, latents = chunk * group + fast * block, full[chunk, fast]
        else:
            first, latents = chunk * group, full[chunk].reshape(group, width)
        keys = matmul(latents, wk_ref[...], 1, 0).astype(bf16)
        k_own[...] = keys
        all_own[...] = latents.T
        kt_own[...] = keys.T
        values = (matmul(latents, wv_ref[...], 1, 0) + rows_ref[3:4, :]).astype(bf16)
        v_own[...] = values
        vt_own[...] = values.T
        for n, (source, target) in enumerate(results(first)):
            pltpu.make_async_copy(source, target, out_sem.at[n]).start()
        attend(first)
        for n, (source, target) in enumerate(results(first)):
            pltpu.make_async_copy(source, target, out_sem.at[n]).wait()

    def visit(index, carry):
        t, across, way = index // 4, index % 4 // 2, index % 2
        for later in range(1, SLOW):

            @pl.when(index == 4 * later)
            def _(later=later):
                for half in range(2):
                    spread(half).step(later)
                    for to in range(2):

                        @pl.when(place.spots[to] >= later)
                        def _(half=half, to=to):
                            fast_copy(0, chunk_of(to, later), half).start()

        far = t - across
        spot = jnp.where(way == 0, place.slow, SLOW - 1 - place.slow)
        chunk = jnp.where(way == 0, spot - far, SLOW - 1 - spot + far)
        due = (far >= 0) & (far < SLOW) & (spot >= far) & ((far > 0) | (way == 0))

        @pl.when(due & (across == 1))
        def _():
            await_fast(chunk)

        @pl.when(due & ((across == 1) | by_block))
        def _():
            project(chunk, jnp.where(across == 1, flip(place.fast, 1), place.fast))

        return carry

    lax.fori_loop(0, 4 * (SLOW + 1), visit, 0)
    for t in range(tiles):
        for g in range(groups):
            total = jnp.sum(totals[g, t], axis=0, keepdims=True)
            att_ref[t * TILE : (t + 1) * TILE, group_at(g)] = fold_heads(mixed[g, t] * (1.0 / total))
            lse_ref[t : t + 1, group_at(g)] = tops[g, t][0:1] + jnp.log(total)

    attended = att_ref[...].astype(bf16)
    weight_loads[0].wait()
    hidden = rays_ref[...].astype(f32) + matmul(attended, wo_ref[...], 1, 0) + rows_ref[4:5, :]
    hidden_low = hidden.astype(bf16)
    hidden_turned = hidden_low.T
    weight_loads[3].wait()
    cot = cot_ref[...]
    inner = wu_ref.shape[1]
    blocks = inner // WIDE
    weight_loads[1].wait()
    weight_loads[2].wait()
    per_half = blocks // 2

    def early_copies(n):
        half, part = n // per_half, n % per_half
        slot = n % 2
        return (
            pltpu.make_async_copy(
                gu_slot.at[slot], early_hbm.at[half, pl.ds(0, width), pl.ds(part * WIDE, WIDE)], early_sem.at[0, slot]
            ),
            pltpu.make_async_copy(
                gd_slot.at[slot], early_hbm.at[half, pl.ds(width + part * WIDE, WIDE)], early_sem.at[1, slot]
            ),
        )

    for n in range(blocks):
        at = slice(n * WIDE, (n + 1) * WIDE)
        bias_row, bias_at = 5 + n * WIDE // width, slice(n * WIDE % width, n * WIDE % width + WIDE)
        pre = matmul(hidden_low, wu_ref[:, at], 1, 0) + rows_ref[bias_row : bias_row + 1, bias_at]
        active, slope = gelu_both(pre)
        active = active.astype(bf16)
        active_ref[:, at] = active
        grad_pre = (matmul(cot, wd_ref[at, :], 1, 1) * slope).astype(bf16)
        gpre_ref[:, at] = grad_pre
        small_ref[bias_row - 4 : bias_row - 3, bias_at] = jnp.sum(grad_pre.astype(f32), axis=0, keepdims=True)
        if n >= 2:
            for copy in early_copies(n - 2):
                copy.wait()
        gu_slot[n % 2] = matmul(hidden_turned, grad_pre, 1, 0).astype(bf16)
        gd_slot[n % 2] = matmul(active, cot, 0, 0).astype(bf16)
        for copy in early_copies(n):
            copy.start()
    result_ref[...] = (hidden + matmul(active_ref[...], wd_ref[...], 1, 0) + rows_ref[7:8, :]).astype(bf16)
    grad_top = cot.astype(f32)
    small_ref[3:4, :] = jnp.sum(grad_top, axis=0, keepdims=True)
    grad_hidden = grad_top + matmul(gpre_ref[...], wu_ref[...], 1, 1)
    gh_ref[...] = grad_hidden
    grad_branch = grad_hidden.astype(bf16)
    small_ref[0:1, :] = jnp.sum(grad_branch.astype(f32), axis=0, keepdims=True)
    small_ref[4:8, :] = jnp.zeros((4, width), f32)
    grad_out = matmul(attended, grad_branch, 0, 0).astype(bf16)
    go_slot[...] = grad_out[: 2 * BLOCK]
    go_copies = [
        pltpu.make_async_copy(
            go_slot.at[pl.ds(c * BLOCK, BLOCK)], early_hbm.at[c, pl.ds(2 * width, BLOCK)], go_sem.at[c]
        )
        for c in range(2)
    ]
    for copy in go_copies:
        copy.start()
    rest_ref[...] = grad_out[2 * BLOCK :]
    grad_attended = matmul(grad_branch, wo_ref[...], 1, 1).astype(bf16)
    ga_ref[...] = grad_attended
    product = grad_attended.astype(f32) * att_ref[...]
    for t in range(dots_ref.shape[0]):
        for g in range(width // WIDE):
            dots_ref[t : t + 1, group_at(g)] = lax.dot_general(
                jnp.ones((8, WIDE), f32),
                spread_heads(product[t * TILE : (t + 1) * TILE, group_at(g)]),
                (((1,), (1,)), ((), ())),
                precision=lax.Precision.HIGHEST,
                preferred_element_type=f32,
            )[0:1, :]
    for copy in early_copies(blocks - 2) + early_copies(blocks - 1) + tuple(go_copies):
        copy.wait()


    for half in range(2):
        spread(half).drain()


def gather_and_attend(
    n_seq, n_ray, rays, latents, lengths, scenes, vectors, w_query, w_key, w_value, cotangent, w_out, w_up, w_down
):
    inner = w_up.shape[1]
    block, width = latents.shape
    n_rays = rays.shape[0]
    n_fast = n_ray // SLOW
    group = n_fast * block
    step = block if block % 128 == 0 and n_fast == 2 else group
    total = n_ray * block
    tiles, groups = n_rays // TILE, width // WIDE
    fast_bits = len(bits_of(n_fast))
    vmem = pltpu.VMEM
    sem = pltpu.SemaphoreType.DMA
    in_vmem = pl.BlockSpec(memory_space=vmem)
    anywhere = pl.BlockSpec(memory_space=pl.ANY)
    struct = jax.ShapeDtypeStruct
    tall, wide = struct((total, width), bf16), struct((width, total), bf16)
    return pl.pallas_call(
        functools.partial(gather_kernel, n_seq, n_ray),
        out_shape=(
            wide,
            tall,
            wide,
            tall,
            struct((n_rays, width), bf16),
            struct((n_rays, width), bf16),
            struct((tiles, width), f32),
            struct((tiles, WIDE), f32),
            struct((8, width), f32),
            struct((n_rays, width), bf16),
            struct((n_rays, width), f32),
            struct((n_rays, width), bf16),
            struct((tiles, width), f32),
            struct((8, width), f32),
            struct((2, 2 * width + BLOCK, width), bf16),
            struct((width - 2 * BLOCK, width), bf16),
        ),
        in_specs=[pl.BlockSpec(memory_space=pltpu.SMEM)] + [in_vmem] * 9 + [anywhere] * 8,
        out_specs=(anywhere,) * 4 + (in_vmem,) * 10 + (anywhere, in_vmem),
        scratch_shapes=[
            vmem((SLOW, n_fast, block, width), bf16),
            vmem((width, step), bf16),
            vmem((step, width), bf16),
            vmem((width, step), bf16),
            vmem((step, width), bf16),
            vmem((width, step), bf16),
            vmem((step, WIDE), f32),
            vmem((groups, tiles, 8, WIDE), f32),
            vmem((groups, tiles, 8, WIDE), f32),
            vmem((groups, tiles, WIDE, WIDE), f32),
            vmem((n_rays, width), f32),
            vmem((n_rays, width), bf16),
            vmem((width, width), bf16),
            vmem((width, width), bf16),
            vmem((width, width), bf16),
            vmem((n_rays, width), bf16),
            vmem((width, width), bf16),
            vmem((width, inner), bf16),
            vmem((inner, width), bf16),
            vmem((n_rays, inner), bf16),
            vmem((n_rays, inner), bf16),
            vmem((2, width, WIDE), bf16),
            vmem((2, WIDE, width), bf16),
            vmem((2 * BLOCK, width), bf16),
            sem((2, 2, 2, SLOW - 1)),
            sem((2, fast_bits, SLOW, 2)),
            sem((4,)),
            sem((8,)),
            sem((2, 2)),
            sem((2,)),
        ],
        compiler_params=pltpu.CompilerParams(collective_id=0, has_side_effects=True, vmem_limit_bytes=62 << 20),
        name="gather_and_attend",
    )(lengths, latents, scenes, *vectors, rays, w_query, w_key, w_value, cotangent, w_out, w_up, w_down)


def widen_kernel(*refs):
    sums, vectors, wide, lines = refs[:9], refs[9], refs[10:19], refs[19:]
    for source, target in zip(sums, wide):
        target[...] = source[...].astype(target.dtype)
    for n, line in enumerate(lines):
        line[...] = vectors[n, :]


def widen(sums, whole, vectors):
    steps = 4
    width = vectors.shape[1]
    struct = jax.ShapeDtypeStruct
    blocks = [pl.BlockSpec((a.shape[0] // steps, a.shape[1]), lambda i: (i, 0)) for a in sums + whole]
    return pl.pallas_call(
        widen_kernel,
        grid=(steps,),
        out_shape=tuple(struct(a.shape, f32) for a in sums)
        + tuple(struct(a.shape, a.dtype) for a in whole)
        + (struct((width,), f32),) * vectors.shape[0],
        in_specs=blocks + [pl.BlockSpec(vectors.shape, lambda i: (0, 0))],
        out_specs=tuple(blocks) + (pl.BlockSpec((width,), lambda i: (0,)),) * vectors.shape[0],
        compiler_params=pltpu.CompilerParams(vmem_limit_bytes=62 << 20),
        name="widen",
    )(*sums, *whole, vectors)


def local(
    rays,
    latents,
    lengths,
    scenes,
    ln_gain,
    ln_bias,
    w_query,
    b_query,
    w_key,
    w_value,
    b_value,
    w_out,
    b_out,
    w_up,
    b_up,
    w_down,
    b_down,
    cotangent,
):
    width = rays.shape[1]
    n_seq, n_ray = lax.axis_size("seq"), lax.axis_size("ray")
    vectors = (b_up, ln_gain, ln_bias, b_query, b_value, b_out, b_down)
    (
        all_t,
        keys,
        keys_t,
        values,
        queries,
        shifted,
        lse,
        scene_rows,
        rows,
        result,
        grad_hidden,
        grad_attended,
        dots,
        small,
        early,
        rest,
    ) = gather_and_attend(
        n_seq,
        n_ray,
        rays,
        latents,
        lengths,
        scenes,
        vectors,
        w_query,
        w_key,
        w_value,
        cotangent,
        w_out,
        w_up,
        w_down,
    )
    sum_q, sum_k, sum_v, sum_o, sum_u, sum_d, grad_latents, grad_rays, small_sums = back_and_sum(
        n_seq,
        n_ray,
        latents.shape[0],
        lengths,
        w_query,
        w_key,
        w_value,
        shifted,
        rays,
        grad_hidden,
        rows,
        small,
        queries,
        grad_attended,
        lse,
        dots,
        scene_rows,
        rest,
        early,
        keys,
        keys_t,
        values,
        all_t,
    )
    wide = widen(
        (sum_q, sum_k, sum_v, sum_o, sum_u, sum_d), (result, grad_rays, grad_latents), small_sums
    )
    lines = wide[9:]
    return (
        wide[6],
        wide[7],
        wide[8],
        lines[4],
        lines[5],
        wide[0],
        lines[6],
        wide[1],
        wide[2],
        lines[7],
        wide[3],
        lines[0],
        wide[4],
        jnp.concatenate(lines[1:3]),
        wide[5],
        lines[3],
    )


def solution(mesh):
    whole = P(("seq", "ray"), None)
    in_specs = (whole, whole, P("seq", None), P(("seq", "ray"))) + (P(),) * 13 + (whole,)
    out_specs = (whole,) * 3 + (P(),) * 13
    return jax.shard_map(local, mesh=mesh, in_specs=in_specs, out_specs=out_specs, check_vma=False)
```
